512 devices in a mesh: inline: 32 (over y, z_hi, core), freq: 16 (over x, z_lo).
Axes of the slice: x: 4, y: 8, z: 8 (z_hi: 2, z_lo: 4; z = z_hi * 4 + z_lo), core: 2. Of those that a mesh axis runs over, the one named last changes fastest.
Arguments:
- traces_in: float32 [2048, 128, 128], P('freq', 'inline'), may hold values from -6 to 6
- reweights: float32 [2, 1024, 128, 128], P(None, 'freq', 'inline'), may hold values from 0.1 to 10
- live_mask: int32 [128, 128], P('inline'), may hold values 0 or 1
Outputs:
- denoised: float32 [2048, 128, 128], P('freq', 'inline')
The draws below stay inside these ranges and needn't reach their ends.
All inputs are finite; a program needn't handle non-finite values. No bound on the sum of `live_mask` on one device may be relied on, other than what follows from the above.
Results may differ from the reference program's by a relative error of at most 0.0003.
Values sent between devices are 32-bit elements; how exact they have to be, the bound alone decides.
No kernel may reach another device: no remote copies, remote signals or barrier semaphores. Data moves between devices by JAX's collectives and lax.ppermute only.
A program may use at most 64 MiB of HBM per device.

```python
import math
import jax
import jax.numpy as jnp
from jax import lax

NT = 2048
NF = 1024
XL = 128
IL = 128
FILT = 4
WI = 4
WX = 32
ITERS = 2


def set_ends(array, own_key, smallest, high):
    longest = array.shape.index(max(array.shape))
    spots = []
    for shift in (0, 1):
        where = [jax.random.randint(jax.random.fold_in(own_key, axis), (), 0, length) for axis, length in enumerate(array.shape)]
        where[longest] = (where[longest] + shift) % array.shape[longest]
        spots.append(tuple(where))
    return array.at[spots[0]].set(smallest).at[spots[1]].set(high)


def block_scale(own_key, shape, split, smallest, top_value):
    loudness, own = 1.0, jax.random.fold_in(own_key, 6)
    for dim, blocks in split:
        draws = jnp.exp(jax.random.uniform(jax.random.fold_in(own, dim), (blocks,), jnp.float32, smallest / len(split), top_value / len(split)))
        loudness = loudness * jnp.repeat(draws, shape[dim] // blocks).reshape([-1 if axis == dim else 1 for axis in range(len(shape))])
    return loudness


def bell_draw(key, shape, scale, most, pieces=(), held_as=jnp.bfloat16):
    values = jax.random.normal(key, shape, jnp.float32) * scale
    if len(pieces) > 0:
        values = block_scale(key, shape, pieces, -0.22, 0.18) * values
    return jnp.clip(values, min=-most, max=most).astype(held_as)


def setup_inputs(seed: int = 0) -> dict:
    key_list = jax.random.split(jax.random.key(seed), 4)
    traces_in = bell_draw(key_list[0], (NT, IL, XL), 1.0, 6.0, ((0, 16), (1, 32)), jnp.float32)
    reweights = jnp.clip(jnp.exp(math.log(10.0) - 4.6051702 * jax.random.uniform(key_list[1], (ITERS, NF, IL, XL), jnp.float32) ** block_scale(key_list[1], (ITERS, NF, IL, XL), ((1, 16), (2, 32)), -0.2, 0.2)), 0.1, 10.0)
    live_mask = set_ends((jax.random.randint(key_list[2], (IL, XL), 0, 8) < 7).astype(jnp.int32), jax.random.fold_in(key_list[2], 1), 0, 1)
    return dict(traces_in=traces_in, reweights=reweights, live_mask=live_mask)


def cholesky_solve(normal_matrix, target):
    system_size = len(target)
    trace_sum = sum((normal_matrix[column][column] for column in range(system_size)))
    ridge_value = 0.05 * trace_sum / system_size + 1e-05
    factor = {}
    for column in range(system_size):
        diagonal_term = normal_matrix[column][column] + ridge_value
        for inner_index in range(column):
            diagonal_term = diagonal_term - factor[column, inner_index] * factor[column, inner_index]
        pivot_value = jnp.sqrt(diagonal_term)
        factor[column, column] = pivot_value
        for below_row in range(column + 1, system_size):
            entry_value = normal_matrix[below_row][column]
            for inner_index in range(column):
                entry_value = entry_value - factor[below_row, inner_index] * factor[column, inner_index]
            factor[below_row, column] = entry_value / pivot_value
    forward_values = []
    for column in range(system_size):
        entry_value = target[column]
        for inner_index in range(column):
            entry_value = entry_value - factor[column, inner_index] * forward_values[inner_index]
        forward_values.append(entry_value / factor[column, column])
    solution_list = [None] * system_size
    for column in reversed(range(system_size)):
        entry_value = forward_values[column]
        for inner_index in range(column + 1, system_size):
            entry_value = entry_value - factor[inner_index, column] * solution_list[inner_index]
        solution_list[column] = entry_value / factor[column, column]
    return solution_list

def filter_step(padded, weights_now, live_weight):
    freq_count = padded.shape[0]
    inline_rows = padded.shape[2] - 2 * FILT
    crosslines = padded.shape[3]
    real_part = padded[:, 0]
    imag_part = padded[:, 1]

    def shifted(values, offset):
        return values[:, FILT + offset:FILT + offset + inline_rows]

    def tiled(values):
        return values.reshape(freq_count, inline_rows // WI, WI, crosslines // WX, WX)

    def window_sum(values):
        return lax.optimization_barrier(jnp.sum(tiled(values), axis=(2, 4)))
    weighted = weights_now * live_weight[None]
    target_real = shifted(real_part, 0)
    target_imag = shifted(imag_part, 0)
    predicted_real = jnp.zeros(tiled(target_real).shape, jnp.float32)
    predicted_imag = jnp.zeros(tiled(target_real).shape, jnp.float32)
    for direction in (-1, 1):
        lag_real = [shifted(real_part, direction * lag_step) for lag_step in range(1, FILT + 1)]
        lag_imag = [shifted(imag_part, direction * lag_step) for lag_step in range(1, FILT + 1)]
        cross_real = {}
        cross_imag = {}
        for first in range(FILT):
            for second in range(first, FILT):
                cross_real[first, second] = window_sum(weighted * (lag_real[first] * lag_real[second] + lag_imag[first] * lag_imag[second]))
                if second > first:
                    cross_imag[first, second] = window_sum(weighted * (lag_real[first] * lag_imag[second] - lag_imag[first] * lag_real[second]))
        zero_block = jnp.zeros_like(cross_real[0, 0])

        def real_entry(first, second):
            return cross_real[min(first, second), max(first, second)]

        def imag_entry(first, second):
            if first == second:
                return zero_block
            if first < second:
                return cross_imag[first, second]
            return -cross_imag[second, first]
        normal_matrix = [[None] * (2 * FILT) for _ in range(2 * FILT)]
        for first in range(FILT):
            for second in range(FILT):
                normal_matrix[first][second] = real_entry(first, second)
                normal_matrix[FILT + first][FILT + second] = real_entry(first, second)
                normal_matrix[first][FILT + second] = -imag_entry(first, second)
                normal_matrix[FILT + first][second] = imag_entry(first, second)
        target = [None] * (2 * FILT)
        for first in range(FILT):
            target[first] = window_sum(weighted * (lag_real[first] * target_real + lag_imag[first] * target_imag))
            target[FILT + first] = window_sum(weighted * (lag_real[first] * target_imag - lag_imag[first] * target_real))
        solution_list = cholesky_solve(normal_matrix, target)
        for lag_index in range(FILT):
            coef_real = solution_list[lag_index][:, :, None, :, None]
            coef_imag = solution_list[FILT + lag_index][:, :, None, :, None]
            block_real = tiled(lag_real[lag_index])
            block_imag = tiled(lag_imag[lag_index])
            predicted_real = predicted_real + (coef_real * block_real - coef_imag * block_imag)
            predicted_imag = predicted_imag + (coef_real * block_imag + coef_imag * block_real)
    scale_live = 0.5 * live_weight[None]
    new_real = predicted_real.reshape(freq_count, inline_rows, crosslines) * scale_live
    new_imag = predicted_imag.reshape(freq_count, inline_rows, crosslines) * scale_live
    return jnp.stack([new_real, new_imag], axis=1)

def reference(traces_in, reweights, live_mask):
    live_weight = live_mask.astype(jnp.float32)
    signal = traces_in * live_weight[None]
    spectrum = jnp.fft.rfft(signal, axis=0)[:NF]
    current = jnp.stack([jnp.real(spectrum), jnp.imag(spectrum)], axis=1).astype(jnp.float32)
    block_size = math.gcd(NF, 64)
    block_count = NF // block_size
    for iteration in range(ITERS):
        padded = jnp.pad(current, ((0, 0), (0, 0), (FILT, FILT), (0, 0)))
        padded_blocks = padded.reshape((block_count, block_size) + padded.shape[1:])
        weight_blocks = reweights[iteration].reshape((block_count, block_size) + reweights.shape[2:])
        current = lax.map(lambda block_pair: filter_step(block_pair[0], block_pair[1], live_weight), (padded_blocks, weight_blocks)).reshape(current.shape)
    complex_state = current[:, 0] + 1j * current[:, 1]
    extended = jnp.concatenate([complex_state, jnp.zeros((1,) + complex_state.shape[1:], complex_state.dtype)], axis=0)
    return jnp.fft.irfft(extended, n=NT, axis=0).astype(jnp.float32)
```

```python
import math

import jax
import jax.numpy as jnp
import numpy as np
from jax import lax
from jax.experimental import pallas as pl
from jax.experimental.pallas import tpu as pltpu
from jax.sharding import PartitionSpec as P

NT = 2048
FILT = 4
ITERS = 2
RADIX = 16
SPAN = 128
BINS = 64
WINDOWS = 4
WX = 32
LANES = 128
f32, bf16 = jnp.float32, jnp.bfloat16


def local_bin(m, e):
    side, step = divmod(e, 4)
    residue = m if side == 0 else (8 if m == 0 else RADIX - m)
    return 16 * step + residue


def bin_order():
    return [local_bin(m, e) for m in range(8) for e in range(8)]


def split_table(table):
    high = table.astype(np.float32).astype(bf16)
    low = (table - high.astype(np.float64)).astype(np.float32).astype(bf16)
    return high, low


def transform_tables():
    forward = np.zeros((8, 2 * SPAN, 2 * SPAN))
    inverse = np.zeros((8, 2 * SPAN, 2 * SPAN))
    r = np.arange(SPAN)
    for m in range(8):
        for g in range(RADIX):
            for e in range(8):
                f = BINS * g + local_bin(m, e)
                angle = 2.0 * np.pi * ((f * r) % NT) / NT
                c, s = np.cos(angle), np.sin(angle)
                col = g * 8 + e
                if m == 0:
                    part = slice(0, SPAN) if e < 4 else slice(SPAN, 2 * SPAN)
                    forward[m, part, col] = c
                    forward[m, part, SPAN + col] = -s
                else:
                    sign = 1.0 if e < 4 else -1.0
                    forward[m, :SPAN, col] = c
                    forward[m, SPAN:, col] = sign * s
                    forward[m, :SPAN, SPAN + col] = -s
                    forward[m, SPAN:, SPAN + col] = sign * c
                scale = (1.0 if f == 0 else 2.0) / NT * (1.0 if m == 0 else 0.5)
                inverse[m, col] = forward[m, :, col] * scale
                inverse[m, SPAN + col] = forward[m, :, SPAN + col] * scale
    return split_table(forward), split_table(inverse)


def spread_table():
    table = np.zeros((BINS, LANES), np.float32)
    for place, b in enumerate(bin_order()):
        table[b, place] = 1.0
        table[b, BINS + place] = 1.0
    return table.astype(bf16)


def cadd(a, b):
    im = a[1] if b[1] is None else (b[1] if a[1] is None else a[1] + b[1])
    return a[0] + b[0], im


def csub(a, b):
    im = a[1] if b[1] is None else (-b[1] if a[1] is None else a[1] - b[1])
    return a[0] - b[0], im


def conj(a):
    return a[0], None if a[1] is None else -a[1]


def turn(a, step, size):
    step = step % size
    if step == 0:
        return a
    if 4 * step == size:
        return (jnp.zeros_like(a[0]) if a[1] is None else -a[1]), a[0]
    if 4 * step == 3 * size:
        return (jnp.zeros_like(a[0]) if a[1] is None else a[1]), -a[0]
    c, s = math.cos(2 * math.pi * step / size), math.sin(2 * math.pi * step / size)
    if a[1] is None:
        return a[0] * c, a[0] * s
    return a[0] * c - a[1] * s, a[0] * s + a[1] * c


def real_transform(values):
    n = len(values)
    if n == 1:
        return [(values[0], None)]
    if n == 2:
        return [(values[0] + values[1], None), (values[0] - values[1], None)]
    even, odd = real_transform(values[::2]), real_transform(values[1::2])
    out = [None] * (n // 2 + 1)
    for p in range(n // 4 + 1):
        turned = turn(odd[p], -p, n)
        out[p] = cadd(even[p], turned)
        out[n // 2 - p] = conj(csub(even[p], turned))
    out[0] = (out[0][0], None)
    out[n // 2] = (out[n // 2][0], None)
    return out


def real_inverse(bins):
    n = 2 * (len(bins) - 1)
    if n == 2:
        return [bins[0][0] + bins[1][0], bins[0][0] - bins[1][0]]
    quarter = n // 4
    first, second = [], []
    for p in range(quarter + 1):
        other = conj(bins[n // 2 - p])
        total, rest = cadd(bins[p], other), turn(csub(bins[p], other), p, n)
        if p in (0, quarter):
            total, rest = (total[0], None), (rest[0], None)
        first.append(total)
        second.append(rest)
    out = [None] * n
    out[::2], out[1::2] = real_inverse(first), real_inverse(second)
    return out


def split_dot(lhs, high, low):
    rows = lhs.shape[0]
    top = lhs.astype(bf16)
    rest = (lhs - top.astype(f32)).astype(bf16)
    both = jnp.dot(jnp.concatenate([top, rest], axis=0), high, preferred_element_type=f32)
    return both[:rows] + both[rows:] + jnp.dot(top, low, preferred_element_type=f32)


def swap_blocks(arrays, lane):
    arrays = list(arrays)
    for d in (1, 2, 4):
        upper = (lane & (8 * d)) != 0
        for i in range(8):
            if i & d:
                continue
            a, b = arrays[i], arrays[i + d]
            arrays[i] = jnp.where(upper, pltpu.roll(b, 8 * d, 1), a)
            arrays[i + d] = jnp.where(upper, b, pltpu.roll(a, LANES - 8 * d, 1))
    return arrays


def send_kernel(traces, live, out):
    alive = live[...].astype(f32)
    for i in range(FILT):
        rows = traces[pl.ds(i, SPAN, stride=FILT), :] * alive[i : i + 1]
        out[i] = rows.T


def forward_kernel(blocks, high, low, out):
    lane = lax.broadcasted_iota(jnp.int32, (WX, LANES), 1)
    left = lane < BINS
    bins = real_transform([blocks[j] for j in range(RADIX)])
    real, imag = [], []
    for m in range(8):
        pair = [bins[0][0], bins[8][0]] if m == 0 else list(bins[m])
        product = split_dot(jnp.concatenate(pair, axis=1), high[m], low[m])
        real.append(product[:, :LANES])
        imag.append(product[:, LANES:])
    real, imag = swap_blocks(real, lane), swap_blocks(imag, lane)
    for g in range(8):
        out[g] = jnp.where(left, real[g], pltpu.roll(imag[g], BINS, 1))
        out[8 + g] = jnp.where(left, pltpu.roll(real[g], BINS, 1), imag[g])


def inverse_kernel(blocks, high, low, out):
    lane = lax.broadcasted_iota(jnp.int32, (WX, LANES), 1)
    left = lane < BINS
    real, imag = [], []
    for g in range(8):
        first, second = blocks[g], blocks[8 + g]
        real.append(jnp.where(left, first, pltpu.roll(second, BINS, 1)))
        imag.append(jnp.where(left, pltpu.roll(first, BINS, 1), second))
    real, imag = swap_blocks(real, lane), swap_blocks(imag, lane)
    bins = [None] * 9
    for m in range(8):
        product = split_dot(jnp.concatenate([real[m], imag[m]], axis=1), high[m], low[m])
        first, second = product[:, :LANES], product[:, LANES:]
        if m == 0:
            bins[0], bins[8] = (first, None), (second, None)
        else:
            bins[m] = (first, second)
    for j, values in enumerate(real_inverse(bins)):
        out[j] = values


def receive_kernel(blocks, out):
    for i in range(FILT):
        out[pl.ds(i, SPAN, stride=FILT), :] = blocks[i].T


def solve(matrix, target):
    n = FILT
    trace = matrix[0][0][0]
    for k in range(1, n):
        trace = trace + matrix[k][k][0]
    ridge = (0.05 * 2.0 / (2 * n)) * trace + 1e-05

    def cmul(a, b):
        return a[0] * b[0] - a[1] * b[1], a[0] * b[1] + a[1] * b[0]

    diag = [matrix[k][k][0] + ridge for k in range(n)]
    upper = {(k, l): matrix[k][l] for k in range(n) for l in range(k + 1, n)}
    rhs = list(target)
    inv = [None] * n
    for k in range(n):
        inv[k] = 1.0 / diag[k]
        for i in range(k + 1, n):
            re, im = upper[k, i]
            factor = (re * inv[k], -im * inv[k])
            diag[i] = diag[i] - (re * factor[0] - im * factor[1])
            for l in range(i + 1, n):
                t = cmul(factor, upper[k, l])
                upper[i, l] = (upper[i, l][0] - t[0], upper[i, l][1] - t[1])
            t = cmul(factor, rhs[k])
            rhs[i] = (rhs[i][0] - t[0], rhs[i][1] - t[1])
    found = [None] * n
    for k in reversed(range(n)):
        re, im = rhs[k]
        for l in range(k + 1, n):
            t = cmul(upper[k, l], found[l])
            re, im = re - t[0], im - t[1]
        found[k] = (re * inv[k], im * inv[k])
    return found


PAIRS = [(k, l) for k in range(FILT) for l in range(k, FILT)]
OFF = [(k, l) for k, l in PAIRS if k < l]
SUMS = len(PAIRS) + len(OFF) + 2 * FILT


def filter_kernel(before, block, after, weights, live, spread, out, omega, turned, sums, coefs):
    alive = live[...].astype(f32)
    table = spread[...]
    for i in range(FILT):
        rows = weights[pl.ds(i, BINS, stride=FILT), :] * alive[i : i + 1]
        top = rows.astype(bf16)
        rest = (rows - top.astype(f32)).astype(bf16)
        over = (((0,), (0,)), ((), ()))
        omega[i] = lax.dot_general(top, table, over, preferred_element_type=f32) + lax.dot_general(
            rest, table, over, preferred_element_type=f32
        )
    parts = (before, block, after)
    for part in range(3):
        for c in range(4 * FILT):
            turned[part, c] = pltpu.roll(parts[part][c], BINS, 1)

    def row_of(row):
        return divmod(row + FILT, FILT)

    def load(row, w, lines):
        part, i = row_of(row)
        return parts[part][i * WINDOWS + w, lines, :]

    def load_turned(row, w, lines):
        part, i = row_of(row)
        return turned[part, i * WINDOWS + w, lines, :]

    def gather(w, carry):
        for way, d in enumerate((-1, 1)):
            acc = [None] * SUMS

            def add(place, value):
                acc[place] = value if acc[place] is None else acc[place] + value

            for sub in range(WX // 8):
                lines = pl.ds(sub * 8, 8)
                wide = pl.ds(pl.multiple_of(w * WX + sub * 8, 8), 8)
                rows, turns = {}, {}
                for i in range(FILT):
                    for k in range(FILT + 1):
                        row = i + d * k
                        if row not in rows:
                            rows[row] = load(row, w, lines)
                            turns[row] = load_turned(row, w, lines)
                for i in range(FILT):
                    om = omega[i, wide, :]
                    place = 0
                    weighted = [om * rows[i + d * (k + 1)] for k in range(FILT)]
                    for k, l in PAIRS:
                        add(place, weighted[k] * rows[i + d * (l + 1)])
                        place += 1
                    for k, l in OFF:
                        add(place, weighted[k] * turns[i + d * (l + 1)])
                        place += 1
                    for k in range(FILT):
                        add(place, weighted[k] * rows[i])
                        add(place + 1, weighted[k] * turns[i])
                        place += 2
            for place in range(SUMS):
                start = pl.multiple_of((w * 2 + way) * 8, 8)
                sums[place, pl.ds(start, 8), :] = acc[place]
        return carry

    lax.fori_loop(0, WINDOWS, gather, 0)

    lane = lax.broadcasted_iota(jnp.int32, (8, LANES), 1)
    sign = jnp.where(lane < BINS, 1.0, -1.0).astype(f32)

    def total(place):
        value = sums[place, pl.ds(0, 8, stride=8), :]
        for s in range(1, 8):
            value = value + sums[place, pl.ds(s, 8, stride=8), :]
        return value

    def real_sum(place):
        value = total(place)
        return value + pltpu.roll(value, BINS, 1)

    def imag_sum(place):
        value = total(place)
        return (value - pltpu.roll(value, BINS, 1)) * sign

    matrix = [[None] * FILT for _ in range(FILT)]
    for place, (k, l) in enumerate(PAIRS):
        matrix[k][l] = (real_sum(place), None)
    for place, (k, l) in enumerate(OFF):
        matrix[k][l] = (matrix[k][l][0], imag_sum(len(PAIRS) + place))
    base = len(PAIRS) + len(OFF)
    target = [(real_sum(base + 2 * k), imag_sum(base + 2 * k + 1)) for k in range(FILT)]
    for k, (re, im) in enumerate(solve(matrix, target)):
        coefs[2 * k] = re
        coefs[2 * k + 1] = -im * sign

    def predict(w, carry):
        for sub in range(WX // 8):
            lines = pl.ds(sub * 8, 8)
            wide = pl.ds(pl.multiple_of(w * WX + sub * 8, 8), 8)
            acc = [None] * FILT
            for way, d in enumerate((-1, 1)):
                for k in range(FILT):
                    one = coefs[2 * k, pl.ds(w * 2 + way, 1), :]
                    two = coefs[2 * k + 1, pl.ds(w * 2 + way, 1), :]
                    for i in range(FILT):
                        row = i + d * (k + 1)
                        value = one * load(row, w, lines) + two * load_turned(row, w, lines)
                        acc[i] = value if acc[i] is None else acc[i] + value
            for i in range(FILT):
                half = jnp.where(omega[i, wide, :] > 0.0, 0.5, 0.0)
                out[i * WINDOWS + w, lines, :] = acc[i] * half
        return carry

    lax.fori_loop(0, WINDOWS, predict, 0)


def kernel_call(body, shape, scratch=(), name=None):
    return pl.pallas_call(
        body,
        out_shape=jax.ShapeDtypeStruct(shape, f32),
        scratch_shapes=list(scratch),
        compiler_params=pltpu.CompilerParams(vmem_limit_bytes=40 * 1024 * 1024),
        name=name,
    )


CHUNKS = (RADIX, WX, LANES)


def send_call(traces, live):
    rows = traces.reshape(SPAN * FILT, LANES)
    return kernel_call(send_kernel, (FILT, LANES, SPAN), name="send")(rows, live).reshape(CHUNKS)


def forward_call(blocks, high, low):
    return kernel_call(forward_kernel, CHUNKS, name="forward")(blocks, high, low)


def inverse_call(blocks, high, low):
    return kernel_call(inverse_kernel, CHUNKS, name="inverse")(blocks, high, low)


def filter_call(before, block, after, weights, live, spread):
    scratch = [
        pltpu.VMEM((FILT, LANES, LANES), f32),
        pltpu.VMEM((3,) + CHUNKS, f32),
        pltpu.VMEM((SUMS, 64, LANES), f32),
        pltpu.VMEM((2 * FILT, 8, LANES), f32),
    ]
    rows = weights.reshape(BINS * FILT, LANES)
    return kernel_call(filter_kernel, CHUNKS, scratch, name="filter")(
        before, block, after, rows, live, spread
    )


def receive_call(blocks):
    rows = blocks.reshape(FILT, LANES, SPAN)
    return kernel_call(receive_kernel, (SPAN * FILT, LANES), name="receive")(rows).reshape(
        SPAN, FILT, LANES
    )


def local(tables, traces_in, reweights, live_mask):
    (fh, fl), (ih, il), spread = tables
    fh, fl, ih, il, spread = (jnp.asarray(t) for t in (fh, fl, ih, il, spread))

    def exchange(blocks):
        return lax.all_to_all(blocks, "freq", 0, 0, tiled=True)

    count = lax.axis_size("inline")
    up = [(i, i + 1) for i in range(count - 1)]
    down = [(i + 1, i) for i in range(count - 1)]
    sent = send_call(traces_in, live_mask)
    current = exchange(forward_call(exchange(sent), fh, fl))
    for n in range(ITERS):
        before = lax.ppermute(current, "inline", up)
        after = lax.ppermute(current, "inline", down)
        current = filter_call(before, current, after, reweights[n], live_mask, spread)
    return receive_call(exchange(inverse_call(exchange(current), ih, il)))


def solution(mesh):
    tables = (*transform_tables(), spread_table())

    def run(traces_in, reweights, live_mask):
        return local(tables, traces_in, reweights, live_mask)

    in_specs = (P("freq", "inline", None), P(None, "freq", "inline", None), P("inline", None))
    out_specs = P("freq", "inline", None)
    return jax.shard_map(run, mesh=mesh, in_specs=in_specs, out_specs=out_specs, check_vma=False)
```

```python
import functools
import math

import jax
import jax.numpy as jnp
import numpy as np
from jax import lax
from jax.experimental import pallas as pl
from jax.experimental.pallas import tpu as pltpu
from jax.sharding import PartitionSpec as P

NT = 2048
FILT = 4
ITERS = 2
RADIX = 16
SPAN = 128
BINS = 64
WINDOWS = 4
WX = 32
ROWS = 16
UNITS = 8
LANES = 128
f32, bf16 = jnp.float32, jnp.bfloat16


def low_bin(m, s, b):
    residue = m if s == 0 else (8 if m == 0 else RADIX - m)
    return 16 * b + residue


INNER = [(s, b) for s in range(2) for b in range(2)]
HALF = BINS // 2


def split_table(table):
    high = table.astype(np.float32).astype(bf16)
    low = (table - high.astype(np.float64)).astype(np.float32).astype(bf16)
    return high, low


def transform_tables():
    forward = np.zeros((8, 2 * SPAN, 2 * SPAN))
    inverse = np.zeros((8, 2 * SPAN, 2 * SPAN))
    r = np.arange(SPAN)
    for m in range(8):
        for part in range(2 * RADIX):
            zh, g = divmod(part, RADIX)
            for place, (s, b) in enumerate(INNER):
                f = BINS * g + HALF * zh + low_bin(m, s, b)
                angle = 2.0 * np.pi * ((f * r) % NT) / NT
                c, sn = np.cos(angle), np.sin(angle)
                col = part * 4 + place
                if m == 0:
                    span = slice(s * SPAN, (s + 1) * SPAN)
                    forward[m, span, col] = c
                    forward[m, span, SPAN + col] = -sn
                else:
                    sign = 1.0 if s == 0 else -1.0
                    forward[m, :SPAN, col] = c
                    forward[m, SPAN:, col] = sign * sn
                    forward[m, :SPAN, SPAN + col] = -sn
                    forward[m, SPAN:, SPAN + col] = sign * c
                scale = (1.0 if f == 0 else 2.0) / NT * (1.0 if m == 0 else 0.5)
                inverse[m, col] = forward[m, :, col] * scale
                inverse[m, SPAN + col] = forward[m, :, SPAN + col] * scale
    return split_table(forward), split_table(inverse)


def spread_table():
    table = np.zeros((HALF, LANES), np.float32)
    for m in range(8):
        for place, (s, b) in enumerate(INNER):
            for quarter in range(4):
                table[low_bin(m, s, b), quarter * HALF + m * 4 + place] = 1.0
    return table.astype(bf16)


def cadd(a, b):
    im = a[1] if b[1] is None else (b[1] if a[1] is None else a[1] + b[1])
    return a[0] + b[0], im


def csub(a, b):
    im = a[1] if b[1] is None else (-b[1] if a[1] is None else a[1] - b[1])
    return a[0] - b[0], im


def conj(a):
    return a[0], None if a[1] is None else -a[1]


def turn(a, step, size):
    step = step % size
    if step == 0:
        return a
    if 4 * step == size:
        return (jnp.zeros_like(a[0]) if a[1] is None else -a[1]), a[0]
    if 4 * step == 3 * size:
        return (jnp.zeros_like(a[0]) if a[1] is None else a[1]), -a[0]
    c, s = math.cos(2 * math.pi * step / size), math.sin(2 * math.pi * step / size)
    if a[1] is None:
        return a[0] * c, a[0] * s
    return a[0] * c - a[1] * s, a[0] * s + a[1] * c


def real_transform(values):
    n = len(values)
    if n == 1:
        return [(values[0], None)]
    if n == 2:
        return [(values[0] + values[1], None), (values[0] - values[1], None)]
    even, odd = real_transform(values[::2]), real_transform(values[1::2])
    out = [None] * (n // 2 + 1)
    for p in range(n // 4 + 1):
        turned = turn(odd[p], -p, n)
        out[p] = cadd(even[p], turned)
        out[n // 2 - p] = conj(csub(even[p], turned))
    out[0] = (out[0][0], None)
    out[n // 2] = (out[n // 2][0], None)
    return out


def real_inverse(bins):
    n = 2 * (len(bins) - 1)
    if n == 2:
        return [bins[0][0] + bins[1][0], bins[0][0] - bins[1][0]]
    quarter = n // 4
    first, second = [], []
    for p in range(quarter + 1):
        other = conj(bins[n // 2 - p])
        total, rest = cadd(bins[p], other), turn(csub(bins[p], other), p, n)
        if p in (0, quarter):
            total, rest = (total[0], None), (rest[0], None)
        first.append(total)
        second.append(rest)
    out = [None] * n
    out[::2], out[1::2] = real_inverse(first), real_inverse(second)
    return out


def split_dot(lhs, high, low):
    rows = lhs.shape[0]
    top = lhs.astype(bf16)
    rest = (lhs - top.astype(f32)).astype(bf16)
    both = jnp.dot(jnp.concatenate([top, rest], axis=0), high, preferred_element_type=f32)
    return both[:rows] + both[rows:] + jnp.dot(top, low, preferred_element_type=f32)


def swap_blocks(arrays, lane, width):
    arrays = list(arrays)
    n = len(arrays)
    d = 1
    while d < n:
        upper = (lane & (width * d)) != 0
        for i in range(n):
            if i & d:
                continue
            a, b = arrays[i], arrays[i + d]
            arrays[i] = jnp.where(upper, pltpu.roll(b, width * d, 1), a)
            arrays[i + d] = jnp.where(upper, b, pltpu.roll(a, LANES - width * d, 1))
        d *= 2
    return arrays


def lanes_of(rows):
    return lax.broadcasted_iota(jnp.int32, (rows, LANES), 1)


def send_kernel(traces, live, weights, out, give):
    alive = live[...].astype(f32)
    for i in range(FILT):
        rows = traces[pl.ds(i, SPAN, stride=FILT), :] * alive[i : i + 1]
        turned = rows.T
        for w in range(WINDOWS):
            out[w * FILT + i] = turned[w * WX : (w + 1) * WX]
    other = (1 - lax.axis_index("zh")) * (HALF * FILT)
    pair = jnp.concatenate([alive, alive], axis=0)
    for n in range(ITERS):
        for k in range(HALF * FILT // 8):
            start = pl.multiple_of(n * BINS * FILT + other + 8 * k, 8)
            give[n, pl.ds(8 * k, 8), :] = weights[pl.ds(start, 8), :] * pair


def forward_kernel(blocks, high, low, out):
    lane = lanes_of(WX)
    bins = real_transform([blocks[j] for j in range(RADIX)])
    real, imag = [], []
    for m in range(8):
        pair = [bins[0][0], bins[8][0]] if m == 0 else list(bins[m])
        product = split_dot(jnp.concatenate(pair, axis=1), high[m], low[m])
        real.append(product[:, :LANES])
        imag.append(product[:, LANES:])
    real, imag = swap_blocks(real, lane, 4), swap_blocks(imag, lane, 4)
    for k in range(8):
        pieces = [real[k][:16], real[k][16:], imag[k][:16], imag[k][16:]]
        for top, tile in enumerate(swap_blocks(pieces, lanes_of(16), HALF)):
            out[top * 8 + k] = tile


def inverse_kernel(blocks, high, low, out):
    lane = lanes_of(WX)
    real, imag = [], []
    for k in range(8):
        pieces = swap_blocks([blocks[top * 8 + k] for top in range(4)], lanes_of(16), HALF)
        real.append(jnp.concatenate(pieces[:2], axis=0))
        imag.append(jnp.concatenate(pieces[2:], axis=0))
    real, imag = swap_blocks(real, lane, 4), swap_blocks(imag, lane, 4)
    bins = [None] * 9
    for m in range(8):
        product = split_dot(jnp.concatenate([real[m], imag[m]], axis=1), high[m], low[m])
        first, second = product[:, :LANES], product[:, LANES:]
        if m == 0:
            bins[0], bins[8] = (first, None), (second, None)
        else:
            bins[m] = (first, second)
    for j, values in enumerate(real_inverse(bins)):
        out[j] = values


def receive_kernel(blocks, out):
    for i in range(FILT):
        rows = jnp.concatenate([blocks[w * FILT + i] for w in range(WINDOWS)], axis=0)
        out[pl.ds(i, SPAN, stride=FILT), :] = rows.T


def solve(matrix, target):
    n = FILT
    trace = matrix[0][0][0]
    for k in range(1, n):
        trace = trace + matrix[k][k][0]
    ridge = (0.05 * 2.0 / (2 * n)) * trace + 1e-05

    def cmul(a, b):
        return a[0] * b[0] - a[1] * b[1], a[0] * b[1] + a[1] * b[0]

    diag = [matrix[k][k][0] + ridge for k in range(n)]
    upper = {(k, l): matrix[k][l] for k in range(n) for l in range(k + 1, n)}
    rhs = list(target)
    inv = [None] * n
    for k in range(n):
        inv[k] = 1.0 / diag[k]
        for i in range(k + 1, n):
            re, im = upper[k, i]
            factor = (re * inv[k], -im * inv[k])
            diag[i] = diag[i] - (re * factor[0] - im * factor[1])
            for l in range(i + 1, n):
                t = cmul(factor, upper[k, l])
                upper[i, l] = (upper[i, l][0] - t[0], upper[i, l][1] - t[1])
            t = cmul(factor, rhs[k])
            rhs[i] = (rhs[i][0] - t[0], rhs[i][1] - t[1])
    found = [None] * n
    for k in reversed(range(n)):
        re, im = rhs[k]
        for l in range(k + 1, n):
            t = cmul(upper[k, l], found[l])
            re, im = re - t[0], im - t[1]
        found[k] = (re * inv[k], im * inv[k])
    return found


PAIRS = [(k, l) for k in range(FILT) for l in range(k, FILT)]
OFF = [(k, l) for k, l in PAIRS if k < l]
SUMS = len(PAIRS) + len(OFF) + 2 * FILT


def filter_kernel(n, block, partner, edge, weights, live, got, spread, *refs):
    out, edge_out = refs[:2] if len(refs) == 8 else (refs[0], None)
    sides, turned_sides, turned, omega, sums, coefs = refs[-6:]
    core, own = lax.axis_index("c"), lax.axis_index("zh")
    alive = live[...].astype(f32)
    table = spread[...]
    over = (((0,), (0,)), ((), ()))
    upper = (lanes_of(ROWS) & HALF) != 0
    for mine in (True, False):
        beta = own if mine else 1 - own
        for i in range(FILT):
            if mine:
                rows = weights[pl.ds(n * BINS * FILT + own * HALF * FILT + i, HALF, stride=FILT), :] * alive[i : i + 1]
            else:
                rows = got[n, pl.ds(i, HALF, stride=FILT), :]
            top = rows.astype(bf16)
            rest = (rows - top.astype(f32)).astype(bf16)
            wide = lax.dot_general(top, table, over, preferred_element_type=f32) + lax.dot_general(
                rest, table, over, preferred_element_type=f32
            )
            for w in range(WINDOWS):
                first, second = wide[w * WX : w * WX + ROWS], wide[w * WX + ROWS : (w + 1) * WX]
                omega[beta * WINDOWS + w, i * ROWS : (i + 1) * ROWS] = jnp.where(upper, second, first)
    for k in range(4 * FILT):
        values = edge[k]
        sides[2 * core, k] = values
        turned_sides[2 * core, k] = pltpu.roll(values, BINS, 1)
        for p in range(2):
            values = partner[p * 4 * FILT + k]
            sides[1 - core + p, k] = values
            turned_sides[1 - core + p, k] = pltpu.roll(values, BINS, 1)
            turned[p * 4 * FILT + k] = pltpu.roll(block[p * 4 * FILT + k], BINS, 1)

    def load(row, unit, lines, plain=True):
        beta, w = unit // WINDOWS, unit % WINDOWS
        part, i = divmod(row + FILT, FILT)
        if part == 1:
            return (block if plain else turned)[unit * FILT + i, lines, :]
        return (sides if plain else turned_sides)[beta + part // 2, w * FILT + i, lines, :]

    def gather(unit, carry):
        for way, d in enumerate((-1, 1)):
            acc = [None] * SUMS

            def add(place, value):
                acc[place] = value if acc[place] is None else acc[place] + value

            for sub in range(ROWS // 8):
                lines = pl.ds(sub * 8, 8)
                rows, turns = {}, {}
                for i in range(FILT):
                    for k in range(FILT + 1):
                        row = i + d * k
                        if row not in rows:
                            rows[row] = load(row, unit, lines)
                            turns[row] = load(row, unit, lines, False)
                for i in range(FILT):
                    om = omega[unit, pl.ds(i * ROWS + sub * 8, 8), :]
                    place = 0
                    weighted = [om * rows[i + d * (k + 1)] for k in range(FILT)]
                    for k, l in PAIRS:
                        add(place, weighted[k] * rows[i + d * (l + 1)])
                        place += 1
                    for k, l in OFF:
                        add(place, weighted[k] * turns[i + d * (l + 1)])
                        place += 1
                    for k in range(FILT):
                        add(place, weighted[k] * rows[i])
                        add(place + 1, weighted[k] * turns[i])
                        place += 2
            for place in range(SUMS):
                start = pl.multiple_of((unit * 2 + way) * 8, 8)
                sums[place, pl.ds(start, 8), :] = acc[place]
        return carry

    lax.fori_loop(0, UNITS, gather, 0)

    sign = jnp.where(lanes_of(2 * UNITS) < BINS, 1.0, -1.0).astype(f32)

    def total(place):
        value = sums[place, pl.ds(0, 2 * UNITS, stride=8), :]
        for s in range(1, 8):
            value = value + sums[place, pl.ds(s, 2 * UNITS, stride=8), :]
        return value

    def both_halves(value):
        return value + pltpu.roll(value, HALF, 1)

    def real_sum(place):
        value = total(place)
        return both_halves(value + pltpu.roll(value, BINS, 1))

    def imag_sum(place):
        value = total(place)
        return both_halves((value - pltpu.roll(value, BINS, 1)) * sign)

    matrix = [[None] * FILT for _ in range(FILT)]
    for place, (k, l) in enumerate(PAIRS):
        matrix[k][l] = (real_sum(place), None)
    for place, (k, l) in enumerate(OFF):
        matrix[k][l] = (matrix[k][l][0], imag_sum(len(PAIRS) + place))
    base = len(PAIRS) + len(OFF)
    target = [(real_sum(base + 2 * k), imag_sum(base + 2 * k + 1)) for k in range(FILT)]
    for k, (re, im) in enumerate(solve(matrix, target)):
        coefs[2 * k] = re
        coefs[2 * k + 1] = -im * sign

    def predict(unit, carry):
        for sub in range(ROWS // 8):
            lines = pl.ds(sub * 8, 8)
            acc = [None] * FILT
            for way, d in enumerate((-1, 1)):
                for k in range(FILT):
                    one = coefs[2 * k, pl.ds(unit * 2 + way, 1), :]
                    two = coefs[2 * k + 1, pl.ds(unit * 2 + way, 1), :]
                    for i in range(FILT):
                        row = i + d * (k + 1)
                        value = one * load(row, unit, lines) + two * load(row, unit, lines, False)
                        acc[i] = value if acc[i] is None else acc[i] + value
            for i in range(FILT):
                half = jnp.where(omega[unit, pl.ds(i * ROWS + sub * 8, 8), :] > 0.0, 0.5, 0.0)
                out[unit * FILT + i, lines, :] = acc[i] * half
        return carry

    lax.fori_loop(0, UNITS, predict, 0)
    if edge_out is not None:
        for k in range(4 * FILT):
            edge_out[k] = out[core * 4 * FILT + k]


def kernel_call(body, shapes, scratch=(), name=None):
    out = [jax.ShapeDtypeStruct(shape, f32) for shape in shapes]
    return pl.pallas_call(
        body,
        out_shape=out if len(out) > 1 else out[0],
        scratch_shapes=list(scratch),
        compiler_params=pltpu.CompilerParams(vmem_limit_bytes=16 * 1024 * 1024),
        name=name,
    )


TRACES = (RADIX, WX, LANES)
TILES = (8 * FILT, ROWS, LANES)
EDGE = (4 * FILT, ROWS, LANES)
GIVE = (ITERS, HALF * FILT, LANES)


def send_call(traces, live, weights):
    rows = traces.reshape(SPAN * FILT, LANES)
    return kernel_call(send_kernel, [TRACES, GIVE], name="send")(rows, live, weights)


def forward_call(blocks, high, low):
    return kernel_call(forward_kernel, [TILES], name="forward")(blocks, high, low)


def inverse_call(blocks, high, low):
    return kernel_call(inverse_kernel, [TRACES], name="inverse")(blocks, high, low)


def filter_call(n, block, partner, edge, weights, live, got, spread):
    scratch = [
        pltpu.VMEM((3,) + EDGE, f32),
        pltpu.VMEM((3,) + EDGE, f32),
        pltpu.VMEM(TILES, f32),
        pltpu.VMEM((UNITS, FILT * ROWS, LANES), f32),
        pltpu.VMEM((SUMS, 16 * UNITS, LANES), f32),
        pltpu.VMEM((2 * FILT, 2 * UNITS, LANES), f32),
    ]
    shapes = [TILES, EDGE] if n + 1 < ITERS else [TILES]
    body = functools.partial(filter_kernel, n)
    return kernel_call(body, shapes, scratch, name="filter")(
        block, partner, edge, weights, live, got, spread
    )


def receive_call(blocks):
    return kernel_call(receive_kernel, [(SPAN * FILT, LANES)], name="receive")(blocks).reshape(
        SPAN, FILT, LANES
    )


def local(tables, traces_in, reweights, live_mask):
    (fh, fl), (ih, il), spread = tables
    fh, fl, ih, il, spread = (jnp.asarray(t) for t in (fh, fl, ih, il, spread))

    def exchange(blocks, axes):
        return lax.all_to_all(blocks, axes, 0, 0, tiled=True)

    swap = [(0, 1), (1, 0)]
    ys = lax.axis_size("y")
    shift = [(2 * y + 1, 2 * y + 2) for y in range(ys - 1)] + [(2 * y + 2, 2 * y + 1) for y in range(ys - 1)]
    weights = reweights.reshape(ITERS * BINS * FILT, LANES)
    sent, give = send_call(traces_in, live_mask, weights)
    got = lax.ppermute(give, "zh", swap)
    spectra = forward_call(exchange(sent, ("x", "zl")), fh, fl)
    spectra, got = lax.optimization_barrier((spectra, got))
    block = exchange(spectra, ("zh", "x", "zl"))
    edge = lax.dynamic_index_in_dim(block.reshape((2,) + EDGE), lax.axis_index("c"), 0, False)
    for n in range(ITERS):
        partner = lax.ppermute(block, "c", swap)
        beyond = lax.ppermute(edge, ("y", "c"), shift)
        found = filter_call(n, block, partner, beyond, weights, live_mask, got, spread)
        block, edge = found if n + 1 < ITERS else (found, None)
    back = exchange(block, ("zh", "x", "zl"))
    return receive_call(exchange(inverse_call(back, ih, il), ("x", "zl")))


def solution(mesh):
    tables = (*transform_tables(), spread_table())

    def run(traces_in, reweights, live_mask):
        return local(tables, traces_in, reweights, live_mask)

    inner = jax.sharding.Mesh(mesh.devices.reshape(-1, 2, 2, 4, 4), ("y", "zh", "c", "x", "zl"))
    inline, freq = ("y", "zh", "c"), ("x", "zl")
    in_specs = (P(freq, inline, None), P(None, freq, inline, None), P(inline, None))
    out_specs = P(freq, inline, None)
    return jax.shard_map(run, mesh=inner, in_specs=in_specs, out_specs=out_specs, check_vma=False)
```

```python
import functools
import math

import jax
import jax.numpy as jnp
import numpy as np
from jax import lax
from jax.experimental import pallas as pl
from jax.experimental.pallas import tpu as pltpu
from jax.sharding import PartitionSpec as P

NT = 2048
FILT = 4
ITERS = 2
RADIX = 16
SPAN = 128
BINS = 64
WINDOWS = 4
WX = 32
ROWS = 16
UNITS = 8
LANES = 128
f32, bf16 = jnp.float32, jnp.bfloat16


def low_bin(m, s, b):
    residue = m if s == 0 else (8 if m == 0 else RADIX - m)
    return 16 * b + residue


INNER = [(s, b) for s in range(2) for b in range(2)]
HALF = BINS // 2


def held_bins(part):
    zh, x, zl = part // 16, part // 4 % 4, part % 4
    z = 4 * zh + zl
    half, source = (0, z - 2) if 2 <= z <= 5 else (1, (z + 2) % 8)
    return half, 4 * x + source


def split_table(table):
    high = table.astype(np.float32).astype(bf16)
    low = (table - high.astype(np.float64)).astype(np.float32).astype(bf16)
    return high, low


def transform_tables():
    forward = np.zeros((2, 2 * SPAN, 2 * SPAN))
    inverse = np.zeros((2, 2 * SPAN, 2 * SPAN))
    r = np.arange(SPAN)
    for part in range(2 * RADIX):
        half, g = held_bins(part)
        for place, (s, b) in enumerate(INNER):
            base = BINS * g + HALF * half + 16 * b
            col = part * 4 + place
            f = base + 8 * s
            angle = 2.0 * np.pi * ((f * r) % NT) / NT
            span = slice(s * SPAN, (s + 1) * SPAN)
            forward[0, span, col] = np.cos(angle)
            forward[0, span, SPAN + col] = -np.sin(angle)
            angle = 2.0 * np.pi * (((base // RADIX + s) * r) % SPAN) / SPAN
            sign = 1.0 if s == 0 else -1.0
            forward[1, :SPAN, col] = np.cos(angle)
            forward[1, SPAN:, col] = sign * np.sin(angle)
            forward[1, :SPAN, SPAN + col] = -np.sin(angle)
            forward[1, SPAN:, SPAN + col] = sign * np.cos(angle)
            scale = (1.0 if f == 0 else 2.0) / NT
            for which, factor in ((0, scale), (1, 1.0 / NT)):
                inverse[which, col] = forward[which, :, col] * factor
                inverse[which, SPAN + col] = forward[which, :, SPAN + col] * factor
    return split_table(forward), split_table(inverse)


def turn_table():
    angle = 2.0 * np.pi * np.arange(8)[:, None] * np.arange(SPAN)[None] / NT
    return np.stack([np.cos(angle), np.sin(angle)]).astype(np.float32)


def spread_table():
    table = np.zeros((HALF, LANES), np.float32)
    for m in range(8):
        for place, (s, b) in enumerate(INNER):
            for quarter in range(4):
                table[low_bin(m, s, b), quarter * HALF + m * 4 + place] = 1.0
    return table.astype(bf16)


def cadd(a, b):
    im = a[1] if b[1] is None else (b[1] if a[1] is None else a[1] + b[1])
    return a[0] + b[0], im


def csub(a, b):
    im = a[1] if b[1] is None else (-b[1] if a[1] is None else a[1] - b[1])
    return a[0] - b[0], im


def conj(a):
    return a[0], None if a[1] is None else -a[1]


def turn(a, step, size):
    step = step % size
    if step == 0:
        return a
    if 4 * step == size:
        return (jnp.zeros_like(a[0]) if a[1] is None else -a[1]), a[0]
    if 4 * step == 3 * size:
        return (jnp.zeros_like(a[0]) if a[1] is None else a[1]), -a[0]
    c, s = math.cos(2 * math.pi * step / size), math.sin(2 * math.pi * step / size)
    if a[1] is None:
        return a[0] * c, a[0] * s
    return a[0] * c - a[1] * s, a[0] * s + a[1] * c


def real_transform(values):
    n = len(values)
    if n == 1:
        return [(values[0], None)]
    if n == 2:
        return [(values[0] + values[1], None), (values[0] - values[1], None)]
    even, odd = real_transform(values[::2]), real_transform(values[1::2])
    out = [None] * (n // 2 + 1)
    for p in range(n // 4 + 1):
        turned = turn(odd[p], -p, n)
        out[p] = cadd(even[p], turned)
        out[n // 2 - p] = conj(csub(even[p], turned))
    out[0] = (out[0][0], None)
    out[n // 2] = (out[n // 2][0], None)
    return out


def real_inverse(bins):
    n = 2 * (len(bins) - 1)
    if n == 2:
        return [bins[0][0] + bins[1][0], bins[0][0] - bins[1][0]]
    quarter = n // 4
    first, second = [], []
    for p in range(quarter + 1):
        other = conj(bins[n // 2 - p])
        total, rest = cadd(bins[p], other), turn(csub(bins[p], other), p, n)
        if p in (0, quarter):
            total, rest = (total[0], None), (rest[0], None)
        first.append(total)
        second.append(rest)
    out = [None] * n
    out[::2], out[1::2] = real_inverse(first), real_inverse(second)
    return out


def split_dot(lhs, high, low):
    rows = lhs.shape[0]
    top = lhs.astype(bf16)
    rest = (lhs - top.astype(f32)).astype(bf16)
    both = jnp.dot(jnp.concatenate([top, rest], axis=0), high, preferred_element_type=f32)
    return both[:rows] + both[rows:] + jnp.dot(top, low, preferred_element_type=f32)


def swap_blocks(arrays, lane, width):
    arrays = list(arrays)
    n = len(arrays)
    d = 1
    while d < n:
        upper = (lane & (width * d)) != 0
        for i in range(n):
            if i & d:
                continue
            a, b = arrays[i], arrays[i + d]
            arrays[i] = jnp.where(upper, pltpu.roll(b, width * d, 1), a)
            arrays[i + d] = jnp.where(upper, b, pltpu.roll(a, LANES - width * d, 1))
        d *= 2
    return arrays


def lanes_of(rows):
    return lax.broadcasted_iota(jnp.int32, (rows, LANES), 1)


def send_kernel(traces, out):
    for i in range(FILT):
        turned = traces[pl.ds(i, SPAN, stride=FILT), :].T
        for w in range(WINDOWS):
            out[w * FILT + i] = turned[w * WX : (w + 1) * WX]


def share_kernel(weights, live, plus, minus):
    alive = live[...].astype(f32)
    pair = jnp.concatenate([alive, alive], axis=0)
    count = HALF * FILT
    own = lax.axis_index("zh") * count
    for n in range(ITERS):
        for target, first in ((plus, own), (minus, count - own)):
            for k in range(0, count, 8):
                start = pl.multiple_of(n * BINS * FILT + first + k, 8)
                target[n, k : k + 8, :] = weights[pl.ds(start, 8), :] * pair


def forward_kernel(blocks, live, high, low, turns, out, alive):
    row = live[pl.ds(lax.axis_index("zl"), 1), :].astype(f32)
    alive[...] = jnp.broadcast_to(row, (LANES, LANES)).T
    mask = alive[pl.ds(pl.multiple_of(lax.axis_index("x") * WX, WX), WX), :]
    lane = lanes_of(WX)
    bins = real_transform([blocks[j] * mask for j in range(RADIX)])
    first = split_dot(jnp.concatenate([bins[0][0], bins[8][0]], axis=1), high[0], low[0])
    rows = []
    for m in range(1, 8):
        (re, im), c, s = bins[m], turns[0, m : m + 1, :], turns[1, m : m + 1, :]
        rows.append(jnp.concatenate([re * c + im * s, im * c - re * s], axis=1))
    others = split_dot(jnp.concatenate(rows, axis=0), high[1], low[1])
    real = [first[:, :LANES]] + [others[WX * m : WX * m + WX, :LANES] for m in range(7)]
    imag = [first[:, LANES:]] + [others[WX * m : WX * m + WX, LANES:] for m in range(7)]
    real, imag = swap_blocks(real, lane, 4), swap_blocks(imag, lane, 4)
    for k in range(8):
        pieces = [real[k][:16], real[k][16:], imag[k][:16], imag[k][16:]]
        for top, tile in enumerate(swap_blocks(pieces, lanes_of(16), HALF)):
            out[top * 8 + k] = tile


def inverse_kernel(blocks, high, low, turns, out):
    lane = lanes_of(WX)
    real, imag = [], []
    for k in range(8):
        pieces = swap_blocks([blocks[top * 8 + k] for top in range(4)], lanes_of(16), HALF)
        real.append(jnp.concatenate(pieces[:2], axis=0))
        imag.append(jnp.concatenate(pieces[2:], axis=0))
    real, imag = swap_blocks(real, lane, 4), swap_blocks(imag, lane, 4)
    first = split_dot(jnp.concatenate([real[0], imag[0]], axis=1), high[0], low[0])
    rows = [jnp.concatenate([real[m], imag[m]], axis=1) for m in range(1, 8)]
    others = split_dot(jnp.concatenate(rows, axis=0), high[1], low[1])
    bins = [(first[:, :LANES], None)] + [None] * 7 + [(first[:, LANES:], None)]
    for m in range(1, 8):
        value = others[WX * (m - 1) : WX * m]
        re, im, c, s = value[:, :LANES], value[:, LANES:], turns[0, m : m + 1, :], turns[1, m : m + 1, :]
        bins[m] = (re * c - im * s, re * s + im * c)
    for j, values in enumerate(real_inverse(bins)):
        out[j] = values


def receive_kernel(blocks, out):
    for i in range(FILT):
        rows = jnp.concatenate([blocks[w * FILT + i] for w in range(WINDOWS)], axis=0)
        out[pl.ds(i, SPAN, stride=FILT), :] = rows.T


def solve(matrix, target):
    n = FILT
    trace = matrix[0][0][0]
    for k in range(1, n):
        trace = trace + matrix[k][k][0]
    ridge = (0.05 * 2.0 / (2 * n)) * trace + 1e-05

    def cmul(a, b):
        return a[0] * b[0] - a[1] * b[1], a[0] * b[1] + a[1] * b[0]

    diag = [matrix[k][k][0] + ridge for k in range(n)]
    upper = {(k, l): matrix[k][l] for k in range(n) for l in range(k + 1, n)}
    rhs = list(target)
    inv = [None] * n
    for k in range(n):
        inv[k] = 1.0 / diag[k]
        for i in range(k + 1, n):
            re, im = upper[k, i]
            factor = (re * inv[k], -im * inv[k])
            diag[i] = diag[i] - (re * factor[0] - im * factor[1])
            for l in range(i + 1, n):
                t = cmul(factor, upper[k, l])
                upper[i, l] = (upper[i, l][0] - t[0], upper[i, l][1] - t[1])
            t = cmul(factor, rhs[k])
            rhs[i] = (rhs[i][0] - t[0], rhs[i][1] - t[1])
    found = [None] * n
    for k in reversed(range(n)):
        re, im = rhs[k]
        for l in range(k + 1, n):
            t = cmul(upper[k, l], found[l])
            re, im = re - t[0], im - t[1]
        found[k] = (re * inv[k], im * inv[k])
    return found


PAIRS = [(k, l) for k in range(FILT) for l in range(k, FILT)]
OFF = [(k, l) for k, l in PAIRS if k < l]
SUMS = len(PAIRS) + len(OFF) + 2 * FILT


def prepare_kernel(plus, minus, spread, omega):
    z = 4 * lax.axis_index("zh") + lax.axis_index("zl")
    inner = jnp.where((z >= 2) & (z <= 5), 0, 1)
    table = spread[...]
    over = (((0,), (0,)), ((), ()))
    upper = (lanes_of(ROWS) & HALF) != 0
    for n in range(ITERS):
        for i in range(FILT):
            for source, beta in ((plus, inner), (minus, 1 - inner)):
                rows = source[n, pl.ds(i, HALF, stride=FILT), :]
                top = rows.astype(bf16)
                rest = (rows - top.astype(f32)).astype(bf16)
                wide = lax.dot_general(top, table, over, preferred_element_type=f32) + lax.dot_general(
                    rest, table, over, preferred_element_type=f32
                )
                for w in range(WINDOWS):
                    first, second = wide[w * WX : w * WX + ROWS], wide[w * WX + ROWS : (w + 1) * WX]
                    omega[n, beta * WINDOWS + w, i * ROWS : (i + 1) * ROWS] = jnp.where(upper, second, first)


def predictions(jobs, omega, turned, sums, coefs, store):
    slots = WINDOWS * len(jobs)
    blocks = []
    for own, side, _, _ in jobs:
        blocks += [ref for ref in (own, side) if all(ref is not other for other in blocks)]
    for place, ref in enumerate(blocks):
        for k in range(4 * FILT):
            turned[place, k] = pltpu.roll(ref[k], BINS, 1)
    places = [[next(p for p, other in enumerate(blocks) if other is ref) for ref in job[:2]] for job in jobs]

    def tile_of(row, w, flip):
        row = row % FILT
        return w * FILT + row + flip * (FILT - 1 - 2 * row)

    def rows_of(job, w, lines):
        own, side, _, flip = jobs[job]
        plain, quarter = [], []
        for row in range(2 * FILT):
            which, tile = row // FILT, tile_of(row, w, flip)
            plain.append((own, side)[which][tile, lines, :])
            quarter.append(turned[places[job][which], tile, lines, :])
        return plain, quarter

    def weight_of(job, i, w, sub):
        _, _, beta, flip = jobs[job]
        start = tile_of(i, 0, flip) * ROWS + sub * 8
        return omega[beta * WINDOWS + w, pl.ds(pl.multiple_of(start, 8), 8), :]

    def gather(w, carry):
        for job in range(len(jobs)):
            acc = [None] * SUMS

            def add(place, value):
                acc[place] = value if acc[place] is None else acc[place] + value

            for sub in range(ROWS // 8):
                rows, turns = rows_of(job, w, pl.ds(sub * 8, 8))
                for i in range(FILT):
                    om = weight_of(job, i, w, sub)
                    weighted = [om * rows[i + k + 1] for k in range(FILT)]
                    place = 0
                    for k, l in PAIRS:
                        add(place, weighted[k] * rows[i + l + 1])
                        place += 1
                    for k, l in OFF:
                        add(place, weighted[k] * turns[i + l + 1])
                        place += 1
                    for k in range(FILT):
                        add(place, weighted[k] * rows[i])
                        add(place + 1, weighted[k] * turns[i])
                        place += 2
            start = pl.multiple_of((job * WINDOWS + w) * 8, 8)
            for place in range(SUMS):
                sums[place, pl.ds(start, 8), :] = acc[place]
        return carry

    lax.fori_loop(0, WINDOWS, gather, 0)

    sign = jnp.where(lanes_of(slots) < BINS, 1.0, -1.0).astype(f32)

    def total(place):
        value = sums[place, pl.ds(0, slots, stride=8), :]
        for s in range(1, 8):
            value = value + sums[place, pl.ds(s, slots, stride=8), :]
        return value

    def both_halves(value):
        return value + pltpu.roll(value, HALF, 1)

    def real_sum(place):
        value = total(place)
        return both_halves(value + pltpu.roll(value, BINS, 1))

    def imag_sum(place):
        value = total(place)
        return both_halves((value - pltpu.roll(value, BINS, 1)) * sign)

    matrix = [[None] * FILT for _ in range(FILT)]
    for place, (k, l) in enumerate(PAIRS):
        matrix[k][l] = (real_sum(place), None)
    for place, (k, l) in enumerate(OFF):
        matrix[k][l] = (matrix[k][l][0], imag_sum(len(PAIRS) + place))
    base = len(PAIRS) + len(OFF)
    target = [(real_sum(base + 2 * k), imag_sum(base + 2 * k + 1)) for k in range(FILT)]
    for k, (re, im) in enumerate(solve(matrix, target)):
        coefs[2 * k] = re
        coefs[2 * k + 1] = -im * sign

    def predict(w, carry):
        for sub in range(ROWS // 8):
            lines = pl.ds(sub * 8, 8)
            for job in range(len(jobs)):
                rows, turns = rows_of(job, w, lines)
                acc = [None] * FILT
                for k in range(FILT):
                    one = coefs[2 * k, pl.ds(job * WINDOWS + w, 1), :]
                    two = coefs[2 * k + 1, pl.ds(job * WINDOWS + w, 1), :]
                    for i in range(FILT):
                        value = one * rows[i + k + 1] + two * turns[i + k + 1]
                        acc[i] = value if acc[i] is None else acc[i] + value
                for i in range(FILT):
                    store(job, tile_of(i, w, jobs[job][3]), lines, acc[i], weight_of(job, i, w, sub))
        return carry

    lax.fori_loop(0, WINDOWS, predict, 0)


def beyond_kernel(n, beyond, edge, omegas, held, *refs):
    core = lax.axis_index("c")

    *outs, turned, sums, coefs = refs
    rest_at, edge_at = (0, 1) if n + 1 < ITERS else (1 - core, core)

    def store(job, tile, lines, value, weight):
        half = jnp.where(weight > 0.0, 0.5, 0.0)
        value = (value + held[1, tile, lines, :]) * half
        outs[0][edge_at, tile, lines, :] = value
        if n + 1 < ITERS:
            outs[1][tile, lines, :] = value

    predictions([(edge, beyond, core, 1 - core)], omegas.at[n], turned, sums, coefs, store)
    for k in range(4 * FILT):
        outs[0][rest_at, k] = held[0, k]


def filter_kernel(n, own, partner, omegas, out, turned, sums, coefs):
    core = lax.axis_index("c")
    rest_at, edge_at = (1 - core, core) if n == 0 else (0, 1)
    rest, edge = own.at[rest_at], own.at[edge_at]
    near, far = (partner.at[core], partner.at[1 - core]) if n == 0 else (partner.at[0], partner.at[1])

    def store(job, tile, lines, value, weight):
        if job == 0:
            out[1, tile, lines, :] = value
        elif job == 1:
            out[0, tile, lines, :] = value
        else:
            out[0, tile, lines, :] = (out[0, tile, lines, :] + value) * jnp.where(weight > 0.0, 0.5, 0.0)

    jobs = [(edge, near, core, core), (rest, near, 1 - core, 1 - core), (rest, far, 1 - core, core)]
    predictions(jobs, omegas.at[n], turned, sums, coefs, store)


def kernel_call(body, shapes, scratch=(), name=None):
    out = [jax.ShapeDtypeStruct(shape, f32) for shape in shapes]
    return pl.pallas_call(
        body,
        out_shape=out if len(out) > 1 else out[0],
        scratch_shapes=list(scratch),
        compiler_params=pltpu.CompilerParams(vmem_limit_bytes=16 * 1024 * 1024),
        name=name,
    )


TRACES = (RADIX, WX, LANES)
TILES = (8 * FILT, ROWS, LANES)
EDGE = (4 * FILT, ROWS, LANES)
GIVE = (ITERS, HALF * FILT, LANES)


def send_call(traces):
    return kernel_call(send_kernel, [TRACES], name="send")(traces.reshape(SPAN * FILT, LANES))


def share_call(weights, live):
    return kernel_call(share_kernel, [GIVE, GIVE], name="share")(weights, live)


def forward_call(blocks, live, *tables):
    scratch = [pltpu.VMEM((LANES, LANES), f32)]
    return kernel_call(forward_kernel, [TILES], scratch, "forward")(blocks, live, *tables)


def inverse_call(blocks, *tables):
    return kernel_call(inverse_kernel, [TRACES], name="inverse")(blocks, *tables)


def prepare_call(plus, minus, spread):
    shape = (ITERS, UNITS, FILT * ROWS, LANES)
    return kernel_call(prepare_kernel, [shape], name="prepare")(plus, minus, spread)


def filter_scratch(blocks, jobs):
    return [
        pltpu.VMEM((blocks,) + EDGE, f32),
        pltpu.VMEM((SUMS, 8 * WINDOWS * jobs, LANES), f32),
        pltpu.VMEM((2 * FILT, WINDOWS * jobs, LANES), f32),
    ]


def beyond_call(n, beyond, edge, omegas, held):
    both = (2,) + EDGE
    body = functools.partial(beyond_kernel, n)
    shapes = [both, EDGE] if n + 1 < ITERS else [both]
    return kernel_call(body, shapes, filter_scratch(2, 1), name="beyond")(beyond, edge, omegas, held)


def filter_call(n, own, partner, omegas):
    body = functools.partial(filter_kernel, n)
    return kernel_call(body, [(2,) + EDGE], filter_scratch(4, 3), name="filter")(own, partner, omegas)


def receive_call(blocks):
    return kernel_call(receive_kernel, [(SPAN * FILT, LANES)], name="receive")(blocks).reshape(
        SPAN, FILT, LANES
    )


def local(tables, traces_in, reweights, live_mask):
    (fh, fl), (ih, il), spread, turns = tables
    fh, fl, ih, il, spread, turns = (jnp.asarray(t) for t in (fh, fl, ih, il, spread, turns))

    def exchange(blocks, axes):
        return lax.all_to_all(blocks, axes, 0, 0, tiled=True)

    swap = [(0, 1), (1, 0)]
    ys = lax.axis_size("y")
    shift = [(2 * y + 1, 2 * y + 2) for y in range(ys - 1)] + [(2 * y + 2, 2 * y + 1) for y in range(ys - 1)]
    weights = reweights.reshape(ITERS * BINS * FILT, LANES)
    sent = send_call(traces_in)
    plus, minus = share_call(weights, live_mask)
    plus = lax.ppermute(plus, ("zh", "zl"), [(z, (z + 2) % 8) for z in range(8)])
    minus = lax.ppermute(minus, ("zh", "zl"), [(z, (z - 2) % 8) for z in range(8)])
    spectra = forward_call(exchange(sent, ("x", "zl")), live_mask, fh, fl, turns)
    spectra, plus, minus = lax.optimization_barrier((spectra, plus, minus))
    block = exchange(spectra, ("zh", "x", "zl"))
    omegas = prepare_call(plus, minus, spread)
    block = block.reshape((2,) + EDGE)
    edge = lax.dynamic_index_in_dim(block, lax.axis_index("c"), 0, False)
    for n in range(ITERS):
        beyond = lax.ppermute(edge, ("y", "c"), shift)
        partner = lax.ppermute(block, "c", swap)
        held = filter_call(n, block, partner, omegas)
        found = beyond_call(n, beyond, edge, omegas, held)
        block, edge = found if n + 1 < ITERS else (found, None)
    back = exchange(block.reshape(TILES), ("zh", "x", "zl"))
    return receive_call(exchange(inverse_call(back, ih, il, turns), ("x", "zl")))


def solution(mesh):
    tables = (*transform_tables(), spread_table(), turn_table())

    def run(traces_in, reweights, live_mask):
        return local(tables, traces_in, reweights, live_mask)

    inner = jax.sharding.Mesh(mesh.devices.reshape(-1, 2, 2, 4, 4), ("y", "zh", "c", "x", "zl"))
    inline, freq = ("y", "zh", "c"), ("x", "zl")
    in_specs = (P(freq, inline, None), P(None, freq, inline, None), P(inline, None))
    out_specs = P(freq, inline, None)
    return jax.shard_map(run, mesh=inner, in_specs=in_specs, out_specs=out_specs, check_vma=False)
```

```python
import functools
import math

import jax
import jax.numpy as jnp
import numpy as np
from jax import lax
from jax.experimental import pallas as pl
from jax.experimental.pallas import tpu as pltpu
from jax.sharding import PartitionSpec as P

NT = 2048
FILT = 4
ITERS = 2
RADIX = 16
SPAN = 128
BINS = 64
WINDOWS = 4
WX = 32
ROWS = 16
UNITS = 8
LANES = 128
f32, bf16 = jnp.float32, jnp.bfloat16


def low_bin(m, s, b):
    residue = m if s == 0 else (8 if m == 0 else RADIX - m)
    return 16 * b + residue


INNER = [(s, b) for s in range(2) for b in range(2)]
HALF = BINS // 2


def held_bins(part):
    return divmod(part, RADIX)


def split_table(table):
    high = table.astype(np.float32).astype(bf16)
    low = (table - high.astype(np.float64)).astype(np.float32).astype(bf16)
    return high, low


def transform_tables():
    forward = np.zeros((2, 2 * SPAN, 2 * SPAN))
    inverse = np.zeros((2, 2 * SPAN, 2 * SPAN))
    r = np.arange(SPAN)
    for part in range(2 * RADIX):
        half, g = held_bins(part)
        for place, (s, b) in enumerate(INNER):
            base = BINS * g + HALF * half + 16 * b
            col = part * 4 + place
            f = base + 8 * s
            angle = 2.0 * np.pi * ((f * r) % NT) / NT
            span = slice(s * SPAN, (s + 1) * SPAN)
            forward[0, span, col] = np.cos(angle)
            forward[0, span, SPAN + col] = -np.sin(angle)
            angle = 2.0 * np.pi * (((base // RADIX + s) * r) % SPAN) / SPAN
            sign = 1.0 if s == 0 else -1.0
            forward[1, :SPAN, col] = np.cos(angle)
            forward[1, SPAN:, col] = sign * np.sin(angle)
            forward[1, :SPAN, SPAN + col] = -np.sin(angle)
            forward[1, SPAN:, SPAN + col] = sign * np.cos(angle)
            scale = (1.0 if f == 0 else 2.0) / NT
            for which, factor in ((0, scale), (1, 1.0 / NT)):
                inverse[which, col] = forward[which, :, col] * factor
                inverse[which, SPAN + col] = forward[which, :, SPAN + col] * factor
    return split_table(forward), split_table(inverse)


def turn_table():
    angle = 2.0 * np.pi * np.arange(8)[:, None] * np.arange(SPAN)[None] / NT
    return np.stack([np.cos(angle), np.sin(angle)]).astype(np.float32)


def spread_table():
    table = np.zeros((HALF, LANES), np.float32)
    for m in range(8):
        for place, (s, b) in enumerate(INNER):
            for quarter in range(4):
                table[low_bin(m, s, b), quarter * HALF + m * 4 + place] = 1.0
    return table.astype(bf16)


def cadd(a, b):
    im = a[1] if b[1] is None else (b[1] if a[1] is None else a[1] + b[1])
    return a[0] + b[0], im


def csub(a, b):
    im = a[1] if b[1] is None else (-b[1] if a[1] is None else a[1] - b[1])
    return a[0] - b[0], im


def conj(a):
    return a[0], None if a[1] is None else -a[1]


def turn(a, step, size):
    step = step % size
    if step == 0:
        return a
    if 4 * step == size:
        return (jnp.zeros_like(a[0]) if a[1] is None else -a[1]), a[0]
    if 4 * step == 3 * size:
        return (jnp.zeros_like(a[0]) if a[1] is None else a[1]), -a[0]
    c, s = math.cos(2 * math.pi * step / size), math.sin(2 * math.pi * step / size)
    if a[1] is None:
        return a[0] * c, a[0] * s
    return a[0] * c - a[1] * s, a[0] * s + a[1] * c


def real_transform(values):
    n = len(values)
    if n == 1:
        return [(values[0], None)]
    if n == 2:
        return [(values[0] + values[1], None), (values[0] - values[1], None)]
    even, odd = real_transform(values[::2]), real_transform(values[1::2])
    out = [None] * (n // 2 + 1)
    for p in range(n // 4 + 1):
        turned = turn(odd[p], -p, n)
        out[p] = cadd(even[p], turned)
        out[n // 2 - p] = conj(csub(even[p], turned))
    out[0] = (out[0][0], None)
    out[n // 2] = (out[n // 2][0], None)
    return out


def real_inverse(bins):
    n = 2 * (len(bins) - 1)
    if n == 2:
        return [bins[0][0] + bins[1][0], bins[0][0] - bins[1][0]]
    quarter = n // 4
    first, second = [], []
    for p in range(quarter + 1):
        other = conj(bins[n // 2 - p])
        total, rest = cadd(bins[p], other), turn(csub(bins[p], other), p, n)
        if p in (0, quarter):
            total, rest = (total[0], None), (rest[0], None)
        first.append(total)
        second.append(rest)
    out = [None] * n
    out[::2], out[1::2] = real_inverse(first), real_inverse(second)
    return out


def split_dot(lhs, high, low):
    rows = lhs.shape[0]
    top = lhs.astype(bf16)
    rest = (lhs - top.astype(f32)).astype(bf16)
    both = jnp.dot(jnp.concatenate([top, rest], axis=0), high, preferred_element_type=f32)
    return both[:rows] + both[rows:] + jnp.dot(top, low, preferred_element_type=f32)


def swap_blocks(arrays, lane, width):
    arrays = list(arrays)
    n = len(arrays)
    d = 1
    while d < n:
        upper = (lane & (width * d)) != 0
        for i in range(n):
            if i & d:
                continue
            a, b = arrays[i], arrays[i + d]
            arrays[i] = jnp.where(upper, pltpu.roll(b, width * d, 1), a)
            arrays[i + d] = jnp.where(upper, b, pltpu.roll(a, LANES - width * d, 1))
        d *= 2
    return arrays


def lanes_of(rows):
    return lax.broadcasted_iota(jnp.int32, (rows, LANES), 1)


def send_kernel(traces, out):
    for i in range(FILT):
        turned = traces[pl.ds(i, SPAN, stride=FILT), :].T
        for w in range(WINDOWS):
            out[w * FILT + i] = turned[w * WX : (w + 1) * WX]


def forward_kernel(blocks, live, high, low, turns, out, alive):
    row = live[pl.ds(lax.axis_index("zl"), 1), :].astype(f32)
    alive[...] = jnp.broadcast_to(row, (LANES, LANES)).T
    mask = alive[pl.ds(pl.multiple_of(lax.axis_index("x") * WX, WX), WX), :]
    lane = lanes_of(WX)
    bins = real_transform([blocks[j] * mask for j in range(RADIX)])
    first = split_dot(jnp.concatenate([bins[0][0], bins[8][0]], axis=1), high[0], low[0])
    rows = []
    for m in range(1, 8):
        (re, im), c, s = bins[m], turns[0, m : m + 1, :], turns[1, m : m + 1, :]
        rows.append(jnp.concatenate([re * c + im * s, im * c - re * s], axis=1))
    others = split_dot(jnp.concatenate(rows, axis=0), high[1], low[1])
    real = [first[:, :LANES]] + [others[WX * m : WX * m + WX, :LANES] for m in range(7)]
    imag = [first[:, LANES:]] + [others[WX * m : WX * m + WX, LANES:] for m in range(7)]
    real, imag = swap_blocks(real, lane, 4), swap_blocks(imag, lane, 4)
    for k in range(8):
        pieces = [real[k][:16], real[k][16:], imag[k][:16], imag[k][16:]]
        for top, tile in enumerate(swap_blocks(pieces, lanes_of(16), HALF)):
            out[top * 8 + k] = tile


def inverse_kernel(blocks, high, low, turns, out):
    lane = lanes_of(WX)
    real, imag = [], []
    for k in range(8):
        pieces = swap_blocks([blocks[top * 8 + k] for top in range(4)], lanes_of(16), HALF)
        real.append(jnp.concatenate(pieces[:2], axis=0))
        imag.append(jnp.concatenate(pieces[2:], axis=0))
    real, imag = swap_blocks(real, lane, 4), swap_blocks(imag, lane, 4)
    first = split_dot(jnp.concatenate([real[0], imag[0]], axis=1), high[0], low[0])
    rows = [jnp.concatenate([real[m], imag[m]], axis=1) for m in range(1, 8)]
    others = split_dot(jnp.concatenate(rows, axis=0), high[1], low[1])
    bins = [(first[:, :LANES], None)] + [None] * 7 + [(first[:, LANES:], None)]
    for m in range(1, 8):
        value = others[WX * (m - 1) : WX * m]
        re, im, c, s = value[:, :LANES], value[:, LANES:], turns[0, m : m + 1, :], turns[1, m : m + 1, :]
        bins[m] = (re * c - im * s, re * s + im * c)
    for j, values in enumerate(real_inverse(bins)):
        out[j] = values


def receive_kernel(blocks, out):
    for i in range(FILT):
        rows = jnp.concatenate([blocks[w * FILT + i] for w in range(WINDOWS)], axis=0)
        out[pl.ds(i, SPAN, stride=FILT), :] = rows.T


def solve(matrix, target):
    n = FILT
    trace = matrix[0][0][0]
    for k in range(1, n):
        trace = trace + matrix[k][k][0]
    ridge = (0.05 * 2.0 / (2 * n)) * trace + 1e-05

    def cmul(a, b):
        return a[0] * b[0] - a[1] * b[1], a[0] * b[1] + a[1] * b[0]

    diag = [matrix[k][k][0] + ridge for k in range(n)]
    upper = {(k, l): matrix[k][l] for k in range(n) for l in range(k + 1, n)}
    rhs = list(target)
    inv = [None] * n
    for k in range(n):
        inv[k] = 1.0 / diag[k]
        for i in range(k + 1, n):
            re, im = upper[k, i]
            factor = (re * inv[k], -im * inv[k])
            diag[i] = diag[i] - (re * factor[0] - im * factor[1])
            for l in range(i + 1, n):
                t = cmul(factor, upper[k, l])
                upper[i, l] = (upper[i, l][0] - t[0], upper[i, l][1] - t[1])
            t = cmul(factor, rhs[k])
            rhs[i] = (rhs[i][0] - t[0], rhs[i][1] - t[1])
    found = [None] * n
    for k in reversed(range(n)):
        re, im = rhs[k]
        for l in range(k + 1, n):
            t = cmul(upper[k, l], found[l])
            re, im = re - t[0], im - t[1]
        found[k] = (re * inv[k], im * inv[k])
    return found


PAIRS = [(k, l) for k in range(FILT) for l in range(k, FILT)]
OFF = [(k, l) for k, l in PAIRS if k < l]
SUMS = len(PAIRS) + len(OFF) + 2 * FILT


def prepare_kernel(weights, live, got, spread, omega):
    own = lax.axis_index("zh")
    alive = live[...].astype(f32)
    table = spread[...]
    over = (((0,), (0,)), ((), ()))
    upper = (lanes_of(ROWS) & HALF) != 0
    for n in range(ITERS):
        for i in range(FILT):
            start = n * BINS * FILT + own * HALF * FILT + i
            mine = weights[pl.ds(start, HALF, stride=FILT), :] * alive[i : i + 1]
            for rows, beta in ((mine, own), (got[n, pl.ds(i, HALF, stride=FILT), :], 1 - own)):
                top = rows.astype(bf16)
                rest = (rows - top.astype(f32)).astype(bf16)
                wide = lax.dot_general(top, table, over, preferred_element_type=f32) + lax.dot_general(
                    rest, table, over, preferred_element_type=f32
                )
                for w in range(WINDOWS):
                    first, second = wide[w * WX : w * WX + ROWS], wide[w * WX + ROWS : (w + 1) * WX]
                    omega[n, beta * WINDOWS + w, i * ROWS : (i + 1) * ROWS] = jnp.where(upper, second, first)


def predictions(jobs, omega, turned, sums, coefs, store):
    slots = WINDOWS * len(jobs)
    blocks = []
    for own, side, _, _ in jobs:
        blocks += [ref for ref in (own, side) if all(ref is not other for other in blocks)]
    for place, ref in enumerate(blocks):
        for k in range(4 * FILT):
            turned[place, k] = pltpu.roll(ref[k], BINS, 1)
    places = [[next(p for p, other in enumerate(blocks) if other is ref) for ref in job[:2]] for job in jobs]

    def tile_of(row, w, flip):
        row = row % FILT
        return w * FILT + row + flip * (FILT - 1 - 2 * row)

    def rows_of(job, w, lines):
        own, side, _, flip = jobs[job]
        plain, quarter = [], []
        for row in range(2 * FILT):
            which, tile = row // FILT, tile_of(row, w, flip)
            plain.append((own, side)[which][tile, lines, :])
            quarter.append(turned[places[job][which], tile, lines, :])
        return plain, quarter

    def weight_of(job, i, w, sub):
        _, _, beta, flip = jobs[job]
        start = tile_of(i, 0, flip) * ROWS + sub * 8
        return omega[beta * WINDOWS + w, pl.ds(pl.multiple_of(start, 8), 8), :]

    def gather(w, carry):
        for job in range(len(jobs)):
            acc = [None] * SUMS

            def add(place, value):
                acc[place] = value if acc[place] is None else acc[place] + value

            for sub in range(ROWS // 8):
                rows, turns = rows_of(job, w, pl.ds(sub * 8, 8))
                for i in range(FILT):
                    om = weight_of(job, i, w, sub)
                    weighted = [om * rows[i + k + 1] for k in range(FILT)]
                    place = 0
                    for k, l in PAIRS:
                        add(place, weighted[k] * rows[i + l + 1])
                        place += 1
                    for k, l in OFF:
                        add(place, weighted[k] * turns[i + l + 1])
                        place += 1
                    for k in range(FILT):
                        add(place, weighted[k] * rows[i])
                        add(place + 1, weighted[k] * turns[i])
                        place += 2
            start = pl.multiple_of((job * WINDOWS + w) * 8, 8)
            for place in range(SUMS):
                sums[place, pl.ds(start, 8), :] = acc[place]
        return carry

    lax.fori_loop(0, WINDOWS, gather, 0)

    sign = jnp.where(lanes_of(slots) < BINS, 1.0, -1.0).astype(f32)

    def total(place):
        value = sums[place, pl.ds(0, slots, stride=8), :]
        for s in range(1, 8):
            value = value + sums[place, pl.ds(s, slots, stride=8), :]
        return value

    def both_halves(value):
        return value + pltpu.roll(value, HALF, 1)

    def real_sum(place):
        value = total(place)
        return both_halves(value + pltpu.roll(value, BINS, 1))

    def imag_sum(place):
        value = total(place)
        return both_halves((value - pltpu.roll(value, BINS, 1)) * sign)

    matrix = [[None] * FILT for _ in range(FILT)]
    for place, (k, l) in enumerate(PAIRS):
        matrix[k][l] = (real_sum(place), None)
    for place, (k, l) in enumerate(OFF):
        matrix[k][l] = (matrix[k][l][0], imag_sum(len(PAIRS) + place))
    base = len(PAIRS) + len(OFF)
    target = [(real_sum(base + 2 * k), imag_sum(base + 2 * k + 1)) for k in range(FILT)]
    for k, (re, im) in enumerate(solve(matrix, target)):
        coefs[2 * k] = re
        coefs[2 * k + 1] = -im * sign

    def predict(w, carry):
        for sub in range(ROWS // 8):
            lines = pl.ds(sub * 8, 8)
            for job in range(len(jobs)):
                rows, turns = rows_of(job, w, lines)
                acc = [None] * FILT
                for k in range(FILT):
                    one = coefs[2 * k, pl.ds(job * WINDOWS + w, 1), :]
                    two = coefs[2 * k + 1, pl.ds(job * WINDOWS + w, 1), :]
                    for i in range(FILT):
                        value = one * rows[i + k + 1] + two * turns[i + k + 1]
                        acc[i] = value if acc[i] is None else acc[i] + value
                for i in range(FILT):
                    store(job, tile_of(i, w, jobs[job][3]), lines, acc[i], weight_of(job, i, w, sub))
        return carry

    lax.fori_loop(0, WINDOWS, predict, 0)


def beyond_kernel(n, beyond, edge, omegas, out, turned, sums, coefs):
    core = lax.axis_index("c")

    def store(job, tile, lines, value, weight):
        out[tile, lines, :] = value

    predictions([(edge, beyond, core, 1 - core)], omegas.at[n], turned, sums, coefs, store)


def filter_kernel(n, part, own, partner, omegas, *refs):
    *outs, turned, sums, coefs = refs
    core = lax.axis_index("c")
    rest_at, edge_at = (1 - core, core) if n == 0 else (0, 1)
    rest, edge = own.at[rest_at], own.at[edge_at]
    near, far = (partner.at[core], partner.at[1 - core]) if n == 0 else (partner.at[0], partner.at[1])
    new_rest, new_edge = (outs[0].at[0], outs[0].at[1]) if n + 1 < ITERS else (outs[0].at[1 - core], outs[0].at[core])

    def store(job, tile, lines, value, weight):
        half = jnp.where(weight > 0.0, 0.5, 0.0)
        if job == 0:
            value = (value + part[tile, lines, :]) * half
            new_edge[tile, lines, :] = value
            if n + 1 < ITERS:
                outs[1][tile, lines, :] = value
        elif job == 1:
            new_rest[tile, lines, :] = value
        else:
            new_rest[tile, lines, :] = (new_rest[tile, lines, :] + value) * half

    jobs = [(edge, near, core, core), (rest, near, 1 - core, 1 - core), (rest, far, 1 - core, core)]
    predictions(jobs, omegas.at[n], turned, sums, coefs, store)


def kernel_call(body, shapes, scratch=(), name=None, cost=None):
    out = [jax.ShapeDtypeStruct(shape, f32) for shape in shapes]
    return pl.pallas_call(
        body,
        out_shape=out if len(out) > 1 else out[0],
        scratch_shapes=list(scratch),
        compiler_params=pltpu.CompilerParams(vmem_limit_bytes=16 * 1024 * 1024),
        name=name,
        cost_estimate=cost,
    )


TRACES = (RADIX, WX, LANES)
TILES = (8 * FILT, ROWS, LANES)
EDGE = (4 * FILT, ROWS, LANES)
GIVE = (ITERS, HALF * FILT, LANES)


def send_call(traces):
    return kernel_call(send_kernel, [TRACES], name="send")(traces.reshape(SPAN * FILT, LANES))


def share(weights, live):
    start = (1 - lax.axis_index("zh")) * HALF
    zero = jnp.zeros_like(start)
    mine = lax.dynamic_slice(
        weights, (zero, start, zero, zero), (ITERS, HALF, FILT, LANES), allow_negative_indices=False
    )
    return jnp.where(live > 0, mine, 0.0).reshape(GIVE)


def forward_call(blocks, live, *tables):
    scratch = [pltpu.VMEM((LANES, LANES), f32)]
    return kernel_call(forward_kernel, [TILES], scratch, "forward")(blocks, live, *tables)


def inverse_call(blocks, *tables):
    return kernel_call(inverse_kernel, [TRACES], name="inverse")(blocks, *tables)


def prepare_call(weights, live, got, spread):
    shape = (ITERS, UNITS, FILT * ROWS, LANES)
    cost = pl.CostEstimate(flops=16_000_000_000, bytes_accessed=64_000_000, transcendentals=0)
    return kernel_call(prepare_kernel, [shape], (), "prepare", cost)(weights, live, got, spread)


def filter_scratch(blocks, jobs):
    return [
        pltpu.VMEM((blocks,) + EDGE, f32),
        pltpu.VMEM((SUMS, 8 * WINDOWS * jobs, LANES), f32),
        pltpu.VMEM((2 * FILT, WINDOWS * jobs, LANES), f32),
    ]


def beyond_call(n, edge, beyond, omegas):
    body = functools.partial(beyond_kernel, n)
    cost = pl.CostEstimate(flops=4_000_000_000, bytes_accessed=16_000_000, transcendentals=0)
    return kernel_call(body, [EDGE], filter_scratch(2, 1), "beyond", cost)(beyond, edge, omegas)


def filter_call(n, part, own, partner, omegas):
    both = (2,) + EDGE
    shapes = [both, EDGE] if n + 1 < ITERS else [both]
    body = functools.partial(filter_kernel, n)
    return kernel_call(body, shapes, filter_scratch(4, 3), name="filter")(part, own, partner, omegas)


def receive_call(blocks):
    return kernel_call(receive_kernel, [(SPAN * FILT, LANES)], name="receive")(blocks).reshape(
        SPAN, FILT, LANES
    )


def local(tables, traces_in, reweights, live_mask):
    (fh, fl), (ih, il), spread, turns = tables
    fh, fl, ih, il, spread, turns = (jnp.asarray(t) for t in (fh, fl, ih, il, spread, turns))

    def exchange(blocks, axes):
        return lax.all_to_all(blocks, axes, 0, 0, tiled=True)

    swap = [(0, 1), (1, 0)]
    ys = lax.axis_size("y")
    shift = [(2 * y + 1, 2 * y + 2) for y in range(ys - 1)] + [(2 * y + 2, 2 * y + 1) for y in range(ys - 1)]
    weights = reweights.reshape(ITERS * BINS * FILT, LANES)
    sent = send_call(traces_in)
    got = lax.ppermute(share(reweights, live_mask), "zh", swap)
    omegas = prepare_call(weights, live_mask, got, spread)
    core = lax.axis_index("c")
    sent, omegas, core = lax.optimization_barrier((exchange(sent, ("x", "zl")), omegas, core))
    block = exchange(forward_call(sent, live_mask, fh, fl, turns), ("zh", "x", "zl"))
    block = block.reshape((2,) + EDGE)
    edge = lax.dynamic_slice(block, (core, 0, 0, 0), (1,) + EDGE, allow_negative_indices=False).reshape(EDGE)
    for n in range(ITERS):
        beyond = lax.ppermute(edge, ("y", "c"), shift)
        partner = lax.ppermute(block, "c", swap)
        part = beyond_call(n, edge, beyond, omegas)
        found = filter_call(n, part, block, partner, omegas)
        block, edge = found if n + 1 < ITERS else (found, None)
    back = exchange(block.reshape(TILES), ("zh", "x", "zl"))
    return receive_call(exchange(inverse_call(back, ih, il, turns), ("x", "zl")))


def solution(mesh):
    tables = (*transform_tables(), spread_table(), turn_table())

    def run(traces_in, reweights, live_mask):
        return local(tables, traces_in, reweights, live_mask)

    inner = jax.sharding.Mesh(mesh.devices.reshape(-1, 2, 2, 4, 4), ("y", "zh", "c", "x", "zl"))
    inline, freq = ("y", "zh", "c"), ("x", "zl")
    in_specs = (P(freq, inline, None), P(None, freq, inline, None), P(inline, None))
    out_specs = P(freq, inline, None)
    return jax.shard_map(run, mesh=inner, in_specs=in_specs, out_specs=out_specs, check_vma=False)
```

```python
import functools
import math

import jax
import jax.numpy as jnp
import numpy as np
from jax import lax
from jax.experimental import pallas as pl
from jax.experimental.pallas import tpu as pltpu
from jax.sharding import PartitionSpec as P

NT = 2048
FILT = 4
ITERS = 2
RADIX = 16
SPAN = 128
BINS = 64
WINDOWS = 4
WX = 32
LANES = 128
f32, bf16 = jnp.float32, jnp.bfloat16


def low_bin(m, s, b):
    residue = m if s == 0 else (8 if m == 0 else RADIX - m)
    return 16 * b + residue


INNER = [(a, s, b) for a in range(2) for s in range(2) for b in range(2)]
HALF = BINS // 2


def split_table(table):
    high = table.astype(np.float32).astype(bf16)
    low = (table - high.astype(np.float64)).astype(np.float32).astype(bf16)
    return high, low


def transform_tables():
    forward = np.zeros((2, 2 * SPAN, 2 * SPAN))
    inverse = np.zeros((2, 2 * SPAN, 2 * SPAN))
    r = np.arange(SPAN)
    for spot in range(2 * 8):
        kappa, part = divmod(spot, 8)
        zh, zl = divmod(part, 4)
        for place, (a, s, b) in enumerate(INNER):
            base = BINS * (4 * (2 * kappa + a) + zl) + HALF * zh + 16 * b
            col = spot * 8 + place
            f = base + 8 * s
            angle = 2.0 * np.pi * ((f * r) % NT) / NT
            span = slice(s * SPAN, (s + 1) * SPAN)
            forward[0, span, col] = np.cos(angle)
            forward[0, span, SPAN + col] = -np.sin(angle)
            angle = 2.0 * np.pi * (((base // RADIX + s) * r) % SPAN) / SPAN
            sign = 1.0 if s == 0 else -1.0
            forward[1, :SPAN, col] = np.cos(angle)
            forward[1, SPAN:, col] = sign * np.sin(angle)
            forward[1, :SPAN, SPAN + col] = -np.sin(angle)
            forward[1, SPAN:, SPAN + col] = sign * np.cos(angle)
            scale = (1.0 if f == 0 else 2.0) / NT
            for which, factor in ((0, scale), (1, 1.0 / NT)):
                inverse[which, col] = forward[which, :, col] * factor
                inverse[which, SPAN + col] = forward[which, :, SPAN + col] * factor
    return split_table(forward), split_table(inverse)


def turn_table():
    angle = 2.0 * np.pi * np.arange(8)[:, None] * np.arange(SPAN)[None] / NT
    return np.stack([np.cos(angle), np.sin(angle)]).astype(np.float32)


def spread_table():
    table = np.zeros((BINS, LANES), np.float32)
    for m in range(8):
        for place, (a, s, b) in enumerate(INNER):
            row = HALF * a + low_bin(m, s, b)
            table[row, m * 8 + place] = 1.0
            table[row, BINS + m * 8 + place] = 1.0
    return table.astype(bf16)


def cadd(a, b):
    im = a[1] if b[1] is None else (b[1] if a[1] is None else a[1] + b[1])
    return a[0] + b[0], im


def csub(a, b):
    im = a[1] if b[1] is None else (-b[1] if a[1] is None else a[1] - b[1])
    return a[0] - b[0], im


def conj(a):
    return a[0], None if a[1] is None else -a[1]


def turn(a, step, size):
    step = step % size
    if step == 0:
        return a
    if 4 * step == size:
        return (jnp.zeros_like(a[0]) if a[1] is None else -a[1]), a[0]
    if 4 * step == 3 * size:
        return (jnp.zeros_like(a[0]) if a[1] is None else a[1]), -a[0]
    c, s = math.cos(2 * math.pi * step / size), math.sin(2 * math.pi * step / size)
    if a[1] is None:
        return a[0] * c, a[0] * s
    return a[0] * c - a[1] * s, a[0] * s + a[1] * c


def real_transform(values):
    n = len(values)
    if n == 1:
        return [(values[0], None)]
    if n == 2:
        return [(values[0] + values[1], None), (values[0] - values[1], None)]
    even, odd = real_transform(values[::2]), real_transform(values[1::2])
    out = [None] * (n // 2 + 1)
    for p in range(n // 4 + 1):
        turned = turn(odd[p], -p, n)
        out[p] = cadd(even[p], turned)
        out[n // 2 - p] = conj(csub(even[p], turned))
    out[0] = (out[0][0], None)
    out[n // 2] = (out[n // 2][0], None)
    return out


def real_inverse(bins):
    n = 2 * (len(bins) - 1)
    if n == 2:
        return [bins[0][0] + bins[1][0], bins[0][0] - bins[1][0]]
    quarter = n // 4
    first, second = [], []
    for p in range(quarter + 1):
        other = conj(bins[n // 2 - p])
        total, rest = cadd(bins[p], other), turn(csub(bins[p], other), p, n)
        if p in (0, quarter):
            total, rest = (total[0], None), (rest[0], None)
        first.append(total)
        second.append(rest)
    out = [None] * n
    out[::2], out[1::2] = real_inverse(first), real_inverse(second)
    return out


def split_dot(lhs, high, low):
    rows = lhs.shape[0]
    top = lhs.astype(bf16)
    rest = (lhs - top.astype(f32)).astype(bf16)
    both = jnp.dot(jnp.concatenate([top, rest], axis=0), high, preferred_element_type=f32)
    return both[:rows] + both[rows:] + jnp.dot(top, low, preferred_element_type=f32)


def swap_blocks(arrays, lane, width):
    arrays = list(arrays)
    n = len(arrays)
    d = 1
    while d < n:
        upper = (lane & (width * d)) != 0
        for i in range(n):
            if i & d:
                continue
            a, b = arrays[i], arrays[i + d]
            arrays[i] = jnp.where(upper, pltpu.roll(b, width * d, 1), a)
            arrays[i + d] = jnp.where(upper, b, pltpu.roll(a, LANES - width * d, 1))
        d *= 2
    return arrays


def lanes_of(rows):
    return lax.broadcasted_iota(jnp.int32, (rows, LANES), 1)


def send_kernel(traces, out):
    for i in range(FILT):
        turned = traces[pl.ds(i, SPAN, stride=FILT), :].T
        for w in range(WINDOWS):
            out[w * FILT + i] = turned[w * WX : (w + 1) * WX]


def forward_kernel(blocks, live, high, low, turns, out, alive):
    row = live[pl.ds(lax.axis_index("zl"), 1), :].astype(f32)
    alive[...] = jnp.broadcast_to(row, (LANES, LANES)).T
    mask = alive[pl.ds(pl.multiple_of(lax.axis_index("x") * WX, WX), WX), :]
    lane = lanes_of(WX)
    bins = real_transform([blocks[j] * mask for j in range(RADIX)])
    first = split_dot(jnp.concatenate([bins[0][0], bins[8][0]], axis=1), high[0], low[0])
    rows = []
    for m in range(1, 8):
        (re, im), c, s = bins[m], turns[0, m : m + 1, :], turns[1, m : m + 1, :]
        rows.append(jnp.concatenate([re * c + im * s, im * c - re * s], axis=1))
    others = split_dot(jnp.concatenate(rows, axis=0), high[1], low[1])
    real = [first[:, :LANES]] + [others[WX * m : WX * m + WX, :LANES] for m in range(7)]
    imag = [first[:, LANES:]] + [others[WX * m : WX * m + WX, LANES:] for m in range(7)]
    real, imag = swap_blocks(real, lane, 8), swap_blocks(imag, lane, 8)
    left = lane < BINS
    for part in range(8):
        out[part, 0] = jnp.where(left, real[part], pltpu.roll(imag[part], BINS, 1))
        out[part, 1] = jnp.where(left, pltpu.roll(real[part], BINS, 1), imag[part])


def inverse_kernel(blocks, high, low, turns, out):
    lane = lanes_of(WX)
    left = lane < BINS
    real, imag = [], []
    for part in range(8):
        first, second = blocks[part, 0], blocks[part, 1]
        real.append(jnp.where(left, first, pltpu.roll(second, BINS, 1)))
        imag.append(jnp.where(left, pltpu.roll(first, BINS, 1), second))
    real, imag = swap_blocks(real, lane, 8), swap_blocks(imag, lane, 8)
    first = split_dot(jnp.concatenate([real[0], imag[0]], axis=1), high[0], low[0])
    rows = [jnp.concatenate([real[m], imag[m]], axis=1) for m in range(1, 8)]
    others = split_dot(jnp.concatenate(rows, axis=0), high[1], low[1])
    bins = [(first[:, :LANES], None)] + [None] * 7 + [(first[:, LANES:], None)]
    for m in range(1, 8):
        value = others[WX * (m - 1) : WX * m]
        re, im, c, s = value[:, :LANES], value[:, LANES:], turns[0, m : m + 1, :], turns[1, m : m + 1, :]
        bins[m] = (re * c - im * s, re * s + im * c)
    for j, values in enumerate(real_inverse(bins)):
        out[j] = values


def receive_kernel(blocks, out):
    for i in range(FILT):
        rows = jnp.concatenate([blocks[w * FILT + i] for w in range(WINDOWS)], axis=0)
        out[pl.ds(i, SPAN, stride=FILT), :] = rows.T


def solve(matrix, target):
    n = FILT
    trace = matrix[0][0][0]
    for k in range(1, n):
        trace = trace + matrix[k][k][0]
    ridge = (0.05 * 2.0 / (2 * n)) * trace + 1e-05

    def cmul(a, b):
        return a[0] * b[0] - a[1] * b[1], a[0] * b[1] + a[1] * b[0]

    diag = [matrix[k][k][0] + ridge for k in range(n)]
    upper = {(k, l): matrix[k][l] for k in range(n) for l in range(k + 1, n)}
    rhs = list(target)
    inv = [None] * n
    for k in range(n):
        inv[k] = 1.0 / diag[k]
        for i in range(k + 1, n):
            re, im = upper[k, i]
            factor = (re * inv[k], -im * inv[k])
            diag[i] = diag[i] - (re * factor[0] - im * factor[1])
            for l in range(i + 1, n):
                t = cmul(factor, upper[k, l])
                upper[i, l] = (upper[i, l][0] - t[0], upper[i, l][1] - t[1])
            t = cmul(factor, rhs[k])
            rhs[i] = (rhs[i][0] - t[0], rhs[i][1] - t[1])
    found = [None] * n
    for k in reversed(range(n)):
        re, im = rhs[k]
        for l in range(k + 1, n):
            t = cmul(upper[k, l], found[l])
            re, im = re - t[0], im - t[1]
        found[k] = (re * inv[k], im * inv[k])
    return found


PAIRS = [(k, l) for k in range(FILT) for l in range(k, FILT)]
OFF = [(k, l) for k, l in PAIRS if k < l]
SUMS = len(PAIRS) + len(OFF) + 2 * FILT


def windows_kernel(weights, live, got, here, across, beside, held):
    own, x = lax.axis_index("zh"), lax.axis_index("x")
    alive = live[...].astype(f32)
    for n in range(ITERS):
        mine, other = [], []
        for i in range(FILT):
            start = n * BINS * FILT + own * HALF * FILT + i
            mine.append(weights[pl.ds(start, HALF, stride=FILT), :] * alive[i : i + 1])
            other.append(got[n, pl.ds(i, HALF, stride=FILT), :])
        for rows, beta in ((mine, own), (other, 1 - own)):
            for w, block in enumerate(swap_blocks(rows, lanes_of(HALF), WX)):
                held[w, beta, n] = block
    pair = x + 1 - 2 * lax.rem(x, 2)
    here[...] = held[x]
    across[...] = held[WINDOWS - 1 - x]
    beside[0] = held[pair]
    beside[1] = held[WINDOWS - 1 - pair]


def prepare_kernel(here, beside, across, spread, omega, held):
    x = lax.axis_index("x")
    pair = x + 1 - 2 * lax.rem(x, 2)
    held[x] = here[...]
    held[pair] = beside[0]
    held[WINDOWS - 1 - x] = across[0]
    held[WINDOWS - 1 - pair] = across[1]
    table = spread[...]
    over = (((0,), (0,)), ((), ()))
    for n in range(ITERS):
        for beta in range(2):
            for kappa in range(2):
                rows = jnp.concatenate([held[2 * kappa + a, beta, n] for a in range(2)], axis=0)
                top = rows.astype(bf16)
                rest = (rows - top.astype(f32)).astype(bf16)
                omega[n, beta * 2 + kappa] = lax.dot_general(
                    top, table, over, preferred_element_type=f32
                ) + lax.dot_general(rest, table, over, preferred_element_type=f32)


def predictions(jobs, omega, turned, sums, coefs, store):
    slots = TWO * len(jobs)
    blocks = []
    for own, side, _, _ in jobs:
        blocks += [ref for ref in (own, side) if all(ref is not other for other in blocks)]
    for place, ref in enumerate(blocks):
        for k in range(TWO * FILT):
            turned[place, k] = pltpu.roll(ref[k], BINS, 1)
    places = [[next(p for p, other in enumerate(blocks) if other is ref) for ref in job[:2]] for job in jobs]

    def tile_of(row, w, flip):
        row = row % FILT
        return (row + flip * (FILT - 1 - 2 * row)) * TWO + w

    def rows_of(job, w, lines):
        own, side, _, flip = jobs[job]
        plain, quarter = [], []
        for row in range(2 * FILT):
            which, tile = row // FILT, tile_of(row, w, flip)
            plain.append((own, side)[which][tile, lines, :])
            quarter.append(turned[places[job][which], tile, lines, :])
        return plain, quarter

    def weight_of(job, i, w, sub):
        _, _, beta, flip = jobs[job]
        start = tile_of(i, 0, flip) // TWO * ROWS + sub * 8
        return omega[beta * TWO + w, pl.ds(pl.multiple_of(start, 8), 8), :]

    def gather(w, carry):
        for job in range(len(jobs)):
            acc = [None] * SUMS

            def add(place, value):
                acc[place] = value if acc[place] is None else acc[place] + value

            for sub in range(ROWS // 8):
                rows, turns = rows_of(job, w, pl.ds(sub * 8, 8))
                for i in range(FILT):
                    om = weight_of(job, i, w, sub)
                    weighted = [om * rows[i + k + 1] for k in range(FILT)]
                    place = 0
                    for k, l in PAIRS:
                        add(place, weighted[k] * rows[i + l + 1])
                        place += 1
                    for k, l in OFF:
                        add(place, weighted[k] * turns[i + l + 1])
                        place += 1
                    for k in range(FILT):
                        add(place, weighted[k] * rows[i])
                        add(place + 1, weighted[k] * turns[i])
                        place += 2
            start = pl.multiple_of((job * TWO + w) * 8, 8)
            for place in range(SUMS):
                sums[place, pl.ds(start, 8), :] = acc[place]
        return carry

    lax.fori_loop(0, TWO, gather, 0)

    sign = jnp.where(lanes_of(slots) < BINS, 1.0, -1.0).astype(f32)

    def total(place):
        value = sums[place, pl.ds(0, slots, stride=8), :]
        for s in range(1, 8):
            value = value + sums[place, pl.ds(s, slots, stride=8), :]
        return value

    def real_sum(place):
        value = total(place)
        return value + pltpu.roll(value, BINS, 1)

    def imag_sum(place):
        value = total(place)
        return (value - pltpu.roll(value, BINS, 1)) * sign

    matrix = [[None] * FILT for _ in range(FILT)]
    for place, (k, l) in enumerate(PAIRS):
        matrix[k][l] = (real_sum(place), None)
    for place, (k, l) in enumerate(OFF):
        matrix[k][l] = (matrix[k][l][0], imag_sum(len(PAIRS) + place))
    base = len(PAIRS) + len(OFF)
    target = [(real_sum(base + 2 * k), imag_sum(base + 2 * k + 1)) for k in range(FILT)]
    for k, (re, im) in enumerate(solve(matrix, target)):
        coefs[2 * k] = re
        coefs[2 * k + 1] = -im * sign

    def predict(w, carry):
        for sub in range(ROWS // 8):
            lines = pl.ds(sub * 8, 8)
            for job in range(len(jobs)):
                rows, turns = rows_of(job, w, lines)
                acc = [None] * FILT
                for k in range(FILT):
                    one = coefs[2 * k, pl.ds(job * TWO + w, 1), :]
                    two = coefs[2 * k + 1, pl.ds(job * TWO + w, 1), :]
                    for i in range(FILT):
                        value = one * rows[i + k + 1] + two * turns[i + k + 1]
                        acc[i] = value if acc[i] is None else acc[i] + value
                for i in range(FILT):
                    store(job, tile_of(i, w, jobs[job][3]), lines, acc[i], weight_of(job, i, w, sub))
        return carry

    lax.fori_loop(0, TWO, predict, 0)


def pick_kernel(block, out):
    out[...] = block[lax.axis_index("c")]


def beyond_kernel(n, beyond, edge, omegas, out, turned, sums, coefs):
    core = lax.axis_index("c")

    def store(job, tile, lines, value, weight):
        out[tile, lines, :] = value

    predictions([(edge, beyond, core, 1 - core)], omegas.at[n], turned, sums, coefs, store)


def filter_kernel(n, part, own, partner, omegas, *refs):
    *outs, turned, sums, coefs = refs
    core = lax.axis_index("c")
    rest_at, edge_at = (1 - core, core) if n == 0 else (0, 1)
    rest, edge = own.at[rest_at], own.at[edge_at]
    near, far = (partner.at[core], partner.at[1 - core]) if n == 0 else (partner.at[0], partner.at[1])
    new_rest, new_edge = (outs[0].at[0], outs[0].at[1]) if n + 1 < ITERS else (outs[0].at[1 - core], outs[0].at[core])

    def store(job, tile, lines, value, weight):
        half = jnp.where(weight > 0.0, 0.5, 0.0)
        if job == 0:
            value = (value + part[tile, lines, :]) * half
            new_edge[tile, lines, :] = value
            if n + 1 < ITERS:
                outs[1][tile, lines, :] = value
        elif job == 1:
            new_rest[tile, lines, :] = value
        else:
            new_rest[tile, lines, :] = (new_rest[tile, lines, :] + value) * half

    jobs = [(edge, near, core, core), (rest, near, 1 - core, 1 - core), (rest, far, 1 - core, core)]
    predictions(jobs, omegas.at[n], turned, sums, coefs, store)


def kernel_call(body, shapes, scratch=(), name=None, cost=None):
    out = [jax.ShapeDtypeStruct(shape, f32) for shape in shapes]
    return pl.pallas_call(
        body,
        out_shape=out if len(out) > 1 else out[0],
        scratch_shapes=list(scratch),
        compiler_params=pltpu.CompilerParams(vmem_limit_bytes=16 * 1024 * 1024),
        name=name,
        cost_estimate=cost,
    )


TRACES = (RADIX, WX, LANES)
TWO = 2
ROWS = WX
TILES = (2 * FILT, TWO, ROWS, LANES)
EDGE = (TWO * FILT, ROWS, LANES)
PART = (2, ITERS, HALF, LANES)
GIVE = (ITERS, HALF * FILT, LANES)


def send_call(traces):
    return kernel_call(send_kernel, [TRACES], name="send")(traces.reshape(SPAN * FILT, LANES))


def share(weights, live):
    start = (1 - lax.axis_index("zh")) * HALF
    zero = jnp.zeros_like(start)
    mine = lax.dynamic_slice(
        weights, (zero, start, zero, zero), (ITERS, HALF, FILT, LANES), allow_negative_indices=False
    )
    return jnp.where(live > 0, mine, 0.0).reshape(GIVE)


def forward_call(blocks, live, *tables):
    scratch = [pltpu.VMEM((LANES, LANES), f32)]
    return kernel_call(forward_kernel, [TILES], scratch, "forward")(blocks, live, *tables)


def inverse_call(blocks, *tables):
    return kernel_call(inverse_kernel, [TRACES], name="inverse")(blocks, *tables)


def windows_call(weights, live, got):
    cost = pl.CostEstimate(flops=16_000_000_000, bytes_accessed=64_000_000, transcendentals=0)
    scratch = [pltpu.VMEM((WINDOWS,) + PART, f32)]
    return kernel_call(windows_kernel, [PART, PART, (2,) + PART], scratch, "windows", cost)(weights, live, got)


def prepare_call(*arrays):
    shape = (ITERS, 2 * TWO, FILT * ROWS, LANES)
    scratch = [pltpu.VMEM((WINDOWS,) + PART, f32)]
    return kernel_call(prepare_kernel, [shape], scratch, "prepare")(*arrays)


def filter_scratch(blocks, jobs):
    return [
        pltpu.VMEM((blocks,) + EDGE, f32),
        pltpu.VMEM((SUMS, 8 * TWO * jobs, LANES), f32),
        pltpu.VMEM((2 * FILT, TWO * jobs, LANES), f32),
    ]


def pick_call(block):
    cost = pl.CostEstimate(flops=16_000_000_000, bytes_accessed=64_000_000, transcendentals=0)
    return kernel_call(pick_kernel, [EDGE], (), "pick", cost)(block)


def beyond_call(n, edge, beyond, omegas):
    body = functools.partial(beyond_kernel, n)
    cost = pl.CostEstimate(flops=4_000_000_000, bytes_accessed=16_000_000, transcendentals=0)
    return kernel_call(body, [EDGE], filter_scratch(2, 1), "beyond", cost)(beyond, edge, omegas)


def filter_call(n, part, own, partner, omegas):
    both = (2,) + EDGE
    shapes = [both, EDGE] if n + 1 < ITERS else [both]
    body = functools.partial(filter_kernel, n)
    return kernel_call(body, shapes, filter_scratch(4, 3), name="filter")(part, own, partner, omegas)


def receive_call(blocks):
    return kernel_call(receive_kernel, [(SPAN * FILT, LANES)], name="receive")(blocks).reshape(
        SPAN, FILT, LANES
    )


def local(tables, traces_in, reweights, live_mask):
    (fh, fl), (ih, il), spread, turns = tables
    fh, fl, ih, il, spread, turns = (jnp.asarray(t) for t in (fh, fl, ih, il, spread, turns))

    def exchange(blocks, axes):
        return lax.all_to_all(blocks, axes, 0, 0, tiled=True)

    swap = [(0, 1), (1, 0)]
    ys = lax.axis_size("y")
    shift = [(2 * y + 1, 2 * y + 2) for y in range(ys - 1)] + [(2 * y + 2, 2 * y + 1) for y in range(ys - 1)]
    weights = reweights.reshape(ITERS * BINS * FILT, LANES)
    sent = send_call(traces_in)
    got = lax.ppermute(share(reweights, live_mask), "zh", swap)
    here, across, beside = windows_call(weights, live_mask, got)
    beside = lax.ppermute(beside, "x", [(i, i ^ 1) for i in range(WINDOWS)])
    sent, here, across, beside = lax.optimization_barrier((exchange(sent, ("x", "zl")), here, across, beside))
    across = lax.ppermute(jnp.stack([across, beside[1]]), "x", [(i, WINDOWS - 1 - i) for i in range(WINDOWS)])
    block = exchange(forward_call(sent, live_mask, fh, fl, turns), ("zh", "zl")).reshape((2,) + EDGE)
    edge = pick_call(block)
    omegas = None
    for n in range(ITERS):
        beyond = lax.ppermute(edge, ("y", "c"), shift)
        partner = lax.ppermute(block, "c", swap)
        if omegas is None:
            edge, across = lax.optimization_barrier((edge, across))
            omegas = prepare_call(here, beside, across, spread)
        part = beyond_call(n, edge, beyond, omegas)
        found = filter_call(n, part, block, partner, omegas)
        block, edge = found if n + 1 < ITERS else (found, None)
    back = exchange(block.reshape(TILES), ("zh", "zl"))
    return receive_call(exchange(inverse_call(back, ih, il, turns), ("x", "zl")))


def solution(mesh):
    tables = (*transform_tables(), spread_table(), turn_table())

    def run(traces_in, reweights, live_mask):
        return local(tables, traces_in, reweights, live_mask)

    inner = jax.sharding.Mesh(mesh.devices.reshape(-1, 2, 2, 4, 4), ("y", "zh", "c", "x", "zl"))
    inline, freq = ("y", "zh", "c"), ("x", "zl")
    in_specs = (P(freq, inline, None), P(None, freq, inline, None), P(inline, None))
    out_specs = P(freq, inline, None)
    return jax.shard_map(run, mesh=inner, in_specs=in_specs, out_specs=out_specs, check_vma=False)
```

```python
import functools
import math

import jax
import jax.numpy as jnp
import numpy as np
from jax import lax
from jax.experimental import pallas as pl
from jax.experimental.pallas import tpu as pltpu
from jax.sharding import PartitionSpec as P

NT = 2048
FILT = 4
ITERS = 2
RADIX = 16
SPAN = 128
BINS = 64
WINDOWS = 4
WX = 32
LANES = 128
f32, bf16 = jnp.float32, jnp.bfloat16


def low_bin(m, s, b):
    residue = m if s == 0 else (8 if m == 0 else RADIX - m)
    return 16 * b + residue


INNER = [(a, s, b) for a in range(2) for s in range(2) for b in range(2)]
HALF = BINS // 2


def split_table(table):
    high = table.astype(np.float32).astype(bf16)
    low = (table - high.astype(np.float64)).astype(np.float32).astype(bf16)
    return high, low


def transform_tables():
    forward = np.zeros((2, 2 * SPAN, 2 * SPAN))
    inverse = np.zeros((2, 2 * SPAN, 2 * SPAN))
    r = np.arange(SPAN)
    for spot in range(2 * 8):
        kappa, part = divmod(spot, 8)
        zh, zl = divmod(part, 4)
        for place, (a, s, b) in enumerate(INNER):
            base = BINS * (4 * (2 * kappa + a) + zl) + HALF * zh + 16 * b
            col = spot * 8 + place
            f = base + 8 * s
            angle = 2.0 * np.pi * ((f * r) % NT) / NT
            span = slice(s * SPAN, (s + 1) * SPAN)
            forward[0, span, col] = np.cos(angle)
            forward[0, span, SPAN + col] = -np.sin(angle)
            angle = 2.0 * np.pi * (((base // RADIX + s) * r) % SPAN) / SPAN
            sign = 1.0 if s == 0 else -1.0
            forward[1, :SPAN, col] = np.cos(angle)
            forward[1, SPAN:, col] = sign * np.sin(angle)
            forward[1, :SPAN, SPAN + col] = -np.sin(angle)
            forward[1, SPAN:, SPAN + col] = sign * np.cos(angle)
            scale = (1.0 if f == 0 else 2.0) / NT
            for which, factor in ((0, scale), (1, 1.0 / NT)):
                inverse[which, col] = forward[which, :, col] * factor
                inverse[which, SPAN + col] = forward[which, :, SPAN + col] * factor
    return split_table(forward), split_table(inverse)


def turn_table():
    angle = 2.0 * np.pi * np.arange(8)[:, None] * np.arange(SPAN)[None] / NT
    return np.stack([np.cos(angle), np.sin(angle)]).astype(np.float32)


def spread_table():
    table = np.zeros((BINS, LANES), np.float32)
    for m in range(8):
        for place, (a, s, b) in enumerate(INNER):
            row = HALF * a + low_bin(m, s, b)
            table[row, m * 8 + place] = 1.0
            table[row, BINS + m * 8 + place] = 1.0
    return table.astype(bf16)


def cadd(a, b):
    im = a[1] if b[1] is None else (b[1] if a[1] is None else a[1] + b[1])
    return a[0] + b[0], im


def csub(a, b):
    im = a[1] if b[1] is None else (-b[1] if a[1] is None else a[1] - b[1])
    return a[0] - b[0], im


def conj(a):
    return a[0], None if a[1] is None else -a[1]


def turn(a, step, size):
    step = step % size
    if step == 0:
        return a
    if 4 * step == size:
        return (jnp.zeros_like(a[0]) if a[1] is None else -a[1]), a[0]
    if 4 * step == 3 * size:
        return (jnp.zeros_like(a[0]) if a[1] is None else a[1]), -a[0]
    c, s = math.cos(2 * math.pi * step / size), math.sin(2 * math.pi * step / size)
    if a[1] is None:
        return a[0] * c, a[0] * s
    return a[0] * c - a[1] * s, a[0] * s + a[1] * c


def real_transform(values):
    n = len(values)
    if n == 1:
        return [(values[0], None)]
    if n == 2:
        return [(values[0] + values[1], None), (values[0] - values[1], None)]
    even, odd = real_transform(values[::2]), real_transform(values[1::2])
    out = [None] * (n // 2 + 1)
    for p in range(n // 4 + 1):
        turned = turn(odd[p], -p, n)
        out[p] = cadd(even[p], turned)
        out[n // 2 - p] = conj(csub(even[p], turned))
    out[0] = (out[0][0], None)
    out[n // 2] = (out[n // 2][0], None)
    return out


def real_inverse(bins):
    n = 2 * (len(bins) - 1)
    if n == 2:
        return [bins[0][0] + bins[1][0], bins[0][0] - bins[1][0]]
    quarter = n // 4
    first, second = [], []
    for p in range(quarter + 1):
        other = conj(bins[n // 2 - p])
        total, rest = cadd(bins[p], other), turn(csub(bins[p], other), p, n)
        if p in (0, quarter):
            total, rest = (total[0], None), (rest[0], None)
        first.append(total)
        second.append(rest)
    out = [None] * n
    out[::2], out[1::2] = real_inverse(first), real_inverse(second)
    return out


def split_dot(lhs, high, low):
    rows = lhs.shape[0]
    top = lhs.astype(bf16)
    rest = (lhs - top.astype(f32)).astype(bf16)
    both = jnp.dot(jnp.concatenate([top, rest], axis=0), high, preferred_element_type=f32)
    return both[:rows] + both[rows:] + jnp.dot(top, low, preferred_element_type=f32)


def swap_blocks(arrays, lane, width):
    arrays = list(arrays)
    n = len(arrays)
    d = 1
    while d < n:
        upper = (lane & (width * d)) != 0
        for i in range(n):
            if i & d:
                continue
            a, b = arrays[i], arrays[i + d]
            arrays[i] = jnp.where(upper, pltpu.roll(b, width * d, 1), a)
            arrays[i + d] = jnp.where(upper, b, pltpu.roll(a, LANES - width * d, 1))
        d *= 2
    return arrays


def lanes_of(rows):
    return lax.broadcasted_iota(jnp.int32, (rows, LANES), 1)


def send_kernel(traces, out):
    for i in range(FILT):
        turned = traces[pl.ds(i, SPAN, stride=FILT), :].T
        for w in range(WINDOWS):
            out[w * FILT + i] = turned[w * WX : (w + 1) * WX]


def forward_kernel(blocks, live, high, low, turns, out, alive):
    row = live[pl.ds(lax.axis_index("zl"), 1), :].astype(f32)
    alive[...] = jnp.broadcast_to(row, (LANES, LANES)).T
    mask = alive[pl.ds(pl.multiple_of(lax.axis_index("x") * WX, WX), WX), :]
    lane = lanes_of(WX)
    bins = real_transform([blocks[j] * mask for j in range(RADIX)])
    first = split_dot(jnp.concatenate([bins[0][0], bins[8][0]], axis=1), high[0], low[0])
    rows = []
    for m in range(1, 8):
        (re, im), c, s = bins[m], turns[0, m : m + 1, :], turns[1, m : m + 1, :]
        rows.append(jnp.concatenate([re * c + im * s, im * c - re * s], axis=1))
    others = split_dot(jnp.concatenate(rows, axis=0), high[1], low[1])
    real = [first[:, :LANES]] + [others[WX * m : WX * m + WX, :LANES] for m in range(7)]
    imag = [first[:, LANES:]] + [others[WX * m : WX * m + WX, LANES:] for m in range(7)]
    real, imag = swap_blocks(real, lane, 8), swap_blocks(imag, lane, 8)
    left = lane < BINS
    for part in range(8):
        out[part, 0] = jnp.where(left, real[part], pltpu.roll(imag[part], BINS, 1))
        out[part, 1] = jnp.where(left, pltpu.roll(real[part], BINS, 1), imag[part])


def inverse_kernel(blocks, high, low, turns, out):
    lane = lanes_of(WX)
    left = lane < BINS
    real, imag = [], []
    for part in range(8):
        first, second = blocks[part, 0], blocks[part, 1]
        real.append(jnp.where(left, first, pltpu.roll(second, BINS, 1)))
        imag.append(jnp.where(left, pltpu.roll(first, BINS, 1), second))
    real, imag = swap_blocks(real, lane, 8), swap_blocks(imag, lane, 8)
    first = split_dot(jnp.concatenate([real[0], imag[0]], axis=1), high[0], low[0])
    rows = [jnp.concatenate([real[m], imag[m]], axis=1) for m in range(1, 8)]
    others = split_dot(jnp.concatenate(rows, axis=0), high[1], low[1])
    bins = [(first[:, :LANES], None)] + [None] * 7 + [(first[:, LANES:], None)]
    for m in range(1, 8):
        value = others[WX * (m - 1) : WX * m]
        re, im, c, s = value[:, :LANES], value[:, LANES:], turns[0, m : m + 1, :], turns[1, m : m + 1, :]
        bins[m] = (re * c - im * s, re * s + im * c)
    for j, values in enumerate(real_inverse(bins)):
        out[j] = values


def receive_kernel(blocks, out):
    for i in range(FILT):
        rows = jnp.concatenate([blocks[w * FILT + i] for w in range(WINDOWS)], axis=0)
        out[pl.ds(i, SPAN, stride=FILT), :] = rows.T


def solve(matrix, target):
    n = FILT
    trace = matrix[0][0][0]
    for k in range(1, n):
        trace = trace + matrix[k][k][0]
    ridge = (0.05 * 2.0 / (2 * n)) * trace + 1e-05

    def cmul(a, b):
        return a[0] * b[0] - a[1] * b[1], a[0] * b[1] + a[1] * b[0]

    diag = [matrix[k][k][0] + ridge for k in range(n)]
    upper = {(k, l): matrix[k][l] for k in range(n) for l in range(k + 1, n)}
    rhs = list(target)
    inv = [None] * n
    for k in range(n):
        inv[k] = 1.0 / diag[k]
        for i in range(k + 1, n):
            re, im = upper[k, i]
            factor = (re * inv[k], -im * inv[k])
            diag[i] = diag[i] - (re * factor[0] - im * factor[1])
            for l in range(i + 1, n):
                t = cmul(factor, upper[k, l])
                upper[i, l] = (upper[i, l][0] - t[0], upper[i, l][1] - t[1])
            t = cmul(factor, rhs[k])
            rhs[i] = (rhs[i][0] - t[0], rhs[i][1] - t[1])
    found = [None] * n
    for k in reversed(range(n)):
        re, im = rhs[k]
        for l in range(k + 1, n):
            t = cmul(upper[k, l], found[l])
            re, im = re - t[0], im - t[1]
        found[k] = (re * inv[k], im * inv[k])
    return found


PAIRS = [(k, l) for k in range(FILT) for l in range(k, FILT)]
OFF = [(k, l) for k, l in PAIRS if k < l]
SUMS = len(PAIRS) + len(OFF) + 2 * FILT


def windows_kernel(weights, live, *refs):
    *outs, held = refs
    x = lax.axis_index("x")
    alive = live[...].astype(f32)
    for n in range(ITERS):
        rows = []
        for i in range(FILT):
            start = n * BINS * FILT + i
            rows.append(weights[pl.ds(start, BINS, stride=FILT), :] * alive[i : i + 1])
        for w, block in enumerate(swap_blocks(rows, lanes_of(BINS), WX)):
            held[w, n] = block
    for k, out in enumerate(outs):
        out[...] = held[lax.rem(x + k, WINDOWS)]


def halves_kernel(*refs):
    *sources, keep, give = refs
    x, own = lax.axis_index("x"), lax.axis_index("zh") * HALF
    for k, source in enumerate(sources):
        place = lax.rem(x + WINDOWS - k, WINDOWS)
        for n in range(ITERS):
            keep[place, n] = source[n, pl.ds(pl.multiple_of(own, HALF), HALF), :]
            give[place, n] = source[n, pl.ds(pl.multiple_of(HALF - own, HALF), HALF), :]


def prepare_kernel(keep, got, spread, omega):
    own = lax.axis_index("zh")
    table = spread[...]
    over = (((0,), (0,)), ((), ()))
    for n in range(ITERS):
        for source, beta in ((keep, own), (got, 1 - own)):
            for kappa in range(2):
                rows = jnp.concatenate([source[2 * kappa + a, n] for a in range(2)], axis=0)
                top = rows.astype(bf16)
                rest = (rows - top.astype(f32)).astype(bf16)
                omega[n, beta * 2 + kappa] = lax.dot_general(
                    top, table, over, preferred_element_type=f32
                ) + lax.dot_general(rest, table, over, preferred_element_type=f32)


def predictions(jobs, omega, turned, sums, coefs, store):
    slots = TWO * len(jobs)
    blocks = []
    for own, side, _, _ in jobs:
        blocks += [ref for ref in (own, side) if all(ref is not other for other in blocks)]
    for place, ref in enumerate(blocks):
        for k in range(TWO * FILT):
            turned[place, k] = pltpu.roll(ref[k], BINS, 1)
    places = [[next(p for p, other in enumerate(blocks) if other is ref) for ref in job[:2]] for job in jobs]

    def tile_of(row, w, flip):
        row = row % FILT
        return (row + flip * (FILT - 1 - 2 * row)) * TWO + w

    def rows_of(job, w, lines):
        own, side, _, flip = jobs[job]
        plain, quarter = [], []
        for row in range(2 * FILT):
            which, tile = row // FILT, tile_of(row, w, flip)
            plain.append((own, side)[which][tile, lines, :])
            quarter.append(turned[places[job][which], tile, lines, :])
        return plain, quarter

    def weight_of(job, i, w, sub):
        _, _, beta, flip = jobs[job]
        start = tile_of(i, 0, flip) // TWO * ROWS + sub * 8
        return omega[beta * TWO + w, pl.ds(pl.multiple_of(start, 8), 8), :]

    def gather(w, carry):
        for job in range(len(jobs)):
            acc = [None] * SUMS

            def add(place, value):
                acc[place] = value if acc[place] is None else acc[place] + value

            for sub in range(ROWS // 8):
                rows, turns = rows_of(job, w, pl.ds(sub * 8, 8))
                for i in range(FILT):
                    om = weight_of(job, i, w, sub)
                    weighted = [om * rows[i + k + 1] for k in range(FILT)]
                    place = 0
                    for k, l in PAIRS:
                        add(place, weighted[k] * rows[i + l + 1])
                        place += 1
                    for k, l in OFF:
                        add(place, weighted[k] * turns[i + l + 1])
                        place += 1
                    for k in range(FILT):
                        add(place, weighted[k] * rows[i])
                        add(place + 1, weighted[k] * turns[i])
                        place += 2
            start = pl.multiple_of((job * TWO + w) * 8, 8)
            for place in range(SUMS):
                sums[place, pl.ds(start, 8), :] = acc[place]
        return carry

    lax.fori_loop(0, TWO, gather, 0)

    sign = jnp.where(lanes_of(slots) < BINS, 1.0, -1.0).astype(f32)

    def total(place):
        value = sums[place, pl.ds(0, slots, stride=8), :]
        for s in range(1, 8):
            value = value + sums[place, pl.ds(s, slots, stride=8), :]
        return value

    def real_sum(place):
        value = total(place)
        return value + pltpu.roll(value, BINS, 1)

    def imag_sum(place):
        value = total(place)
        return (value - pltpu.roll(value, BINS, 1)) * sign

    matrix = [[None] * FILT for _ in range(FILT)]
    for place, (k, l) in enumerate(PAIRS):
        matrix[k][l] = (real_sum(place), None)
    for place, (k, l) in enumerate(OFF):
        matrix[k][l] = (matrix[k][l][0], imag_sum(len(PAIRS) + place))
    base = len(PAIRS) + len(OFF)
    target = [(real_sum(base + 2 * k), imag_sum(base + 2 * k + 1)) for k in range(FILT)]
    for k, (re, im) in enumerate(solve(matrix, target)):
        coefs[2 * k] = re
        coefs[2 * k + 1] = -im * sign

    def predict(w, carry):
        for sub in range(ROWS // 8):
            lines = pl.ds(sub * 8, 8)
            for job in range(len(jobs)):
                rows, turns = rows_of(job, w, lines)
                acc = [None] * FILT
                for k in range(FILT):
                    one = coefs[2 * k, pl.ds(job * TWO + w, 1), :]
                    two = coefs[2 * k + 1, pl.ds(job * TWO + w, 1), :]
                    for i in range(FILT):
                        value = one * rows[i + k + 1] + two * turns[i + k + 1]
                        acc[i] = value if acc[i] is None else acc[i] + value
                for i in range(FILT):
                    store(job, tile_of(i, w, jobs[job][3]), lines, acc[i], weight_of(job, i, w, sub))
        return carry

    lax.fori_loop(0, TWO, predict, 0)


def pick_kernel(block, out):
    out[...] = block[lax.axis_index("c")]


def beyond_kernel(n, beyond, edge, omegas, out, turned, sums, coefs):
    core = lax.axis_index("c")

    def store(job, tile, lines, value, weight):
        out[tile, lines, :] = value

    predictions([(edge, beyond, core, 1 - core)], omegas.at[n], turned, sums, coefs, store)


def filter_kernel(n, part, own, partner, omegas, *refs):
    *outs, turned, sums, coefs = refs
    core = lax.axis_index("c")
    rest_at, edge_at = (1 - core, core) if n == 0 else (0, 1)
    rest, edge = own.at[rest_at], own.at[edge_at]
    near, far = (partner.at[core], partner.at[1 - core]) if n == 0 else (partner.at[0], partner.at[1])
    new_rest, new_edge = (outs[0].at[0], outs[0].at[1]) if n + 1 < ITERS else (outs[0].at[1 - core], outs[0].at[core])

    def store(job, tile, lines, value, weight):
        half = jnp.where(weight > 0.0, 0.5, 0.0)
        if job == 0:
            value = (value + part[tile, lines, :]) * half
            new_edge[tile, lines, :] = value
            if n + 1 < ITERS:
                outs[1][tile, lines, :] = value
        elif job == 1:
            new_rest[tile, lines, :] = value
        else:
            new_rest[tile, lines, :] = (new_rest[tile, lines, :] + value) * half

    jobs = [(edge, near, core, core), (rest, near, 1 - core, 1 - core), (rest, far, 1 - core, core)]
    predictions(jobs, omegas.at[n], turned, sums, coefs, store)


def kernel_call(body, shapes, scratch=(), name=None, cost=None):
    out = [jax.ShapeDtypeStruct(shape, f32) for shape in shapes]
    return pl.pallas_call(
        body,
        out_shape=out if len(out) > 1 else out[0],
        scratch_shapes=list(scratch),
        compiler_params=pltpu.CompilerParams(vmem_limit_bytes=16 * 1024 * 1024),
        name=name,
        cost_estimate=cost,
    )


TRACES = (RADIX, WX, LANES)
TWO = 2
ROWS = WX
TILES = (2 * FILT, TWO, ROWS, LANES)
EDGE = (TWO * FILT, ROWS, LANES)
PART = (ITERS, BINS, LANES)
HALVES = (WINDOWS, ITERS, HALF, LANES)


def send_call(traces):
    return kernel_call(send_kernel, [TRACES], name="send")(traces.reshape(SPAN * FILT, LANES))


def forward_call(blocks, live, *tables):
    scratch = [pltpu.VMEM((LANES, LANES), f32)]
    return kernel_call(forward_kernel, [TILES], scratch, "forward")(blocks, live, *tables)


def inverse_call(blocks, *tables):
    return kernel_call(inverse_kernel, [TRACES], name="inverse")(blocks, *tables)


LONG = pl.CostEstimate(flops=16_000_000_000, bytes_accessed=64_000_000, transcendentals=0)


def windows_call(weights, live):
    scratch = [pltpu.VMEM((WINDOWS,) + PART, f32)]
    return kernel_call(windows_kernel, [PART] * WINDOWS, scratch, "windows")(weights, live)


def halves_call(*arrays):
    return kernel_call(halves_kernel, [HALVES, HALVES], (), "halves", LONG)(*arrays)


def prepare_call(*arrays):
    shape = (ITERS, 2 * TWO, FILT * ROWS, LANES)
    return kernel_call(prepare_kernel, [shape], (), "prepare")(*arrays)


def filter_scratch(blocks, jobs):
    return [
        pltpu.VMEM((blocks,) + EDGE, f32),
        pltpu.VMEM((SUMS, 8 * TWO * jobs, LANES), f32),
        pltpu.VMEM((2 * FILT, TWO * jobs, LANES), f32),
    ]


def pick_call(block):
    return kernel_call(pick_kernel, [EDGE], (), "pick", LONG)(block)


def beyond_call(n, edge, beyond, omegas):
    body = functools.partial(beyond_kernel, n)
    cost = pl.CostEstimate(flops=4_000_000_000, bytes_accessed=16_000_000, transcendentals=0)
    return kernel_call(body, [EDGE], filter_scratch(2, 1), "beyond", cost)(beyond, edge, omegas)


def filter_call(n, part, own, partner, omegas):
    both = (2,) + EDGE
    shapes = [both, EDGE] if n + 1 < ITERS else [both]
    body = functools.partial(filter_kernel, n)
    return kernel_call(body, shapes, filter_scratch(4, 3), name="filter")(part, own, partner, omegas)


def receive_call(blocks):
    return kernel_call(receive_kernel, [(SPAN * FILT, LANES)], name="receive")(blocks).reshape(
        SPAN, FILT, LANES
    )


def local(tables, traces_in, reweights, live_mask):
    (fh, fl), (ih, il), spread, turns = tables
    fh, fl, ih, il, spread, turns = (jnp.asarray(t) for t in (fh, fl, ih, il, spread, turns))

    def exchange(blocks, axes):
        return lax.all_to_all(blocks, axes, 0, 0, tiled=True)

    swap = [(0, 1), (1, 0)]
    ys = lax.axis_size("y")
    shift = [(2 * y + 1, 2 * y + 2) for y in range(ys - 1)] + [(2 * y + 2, 2 * y + 1) for y in range(ys - 1)]
    weights = reweights.reshape(ITERS * BINS * FILT, LANES)
    sent = send_call(traces_in)
    shares = list(windows_call(weights, live_mask))
    for k in range(1, WINDOWS):
        shares[k] = lax.ppermute(shares[k], "x", [(i, (i + k) % WINDOWS) for i in range(WINDOWS)])
    keep, give = halves_call(*shares)
    got = lax.ppermute(give, "zh", swap)
    spectra = forward_call(exchange(sent, ("x", "zl")), live_mask, fh, fl, turns)
    block = exchange(spectra, ("zh", "zl")).reshape((2,) + EDGE)
    edge = pick_call(block)
    omegas = None
    for n in range(ITERS):
        beyond = lax.ppermute(edge, ("y", "c"), shift)
        partner = lax.ppermute(block, "c", swap)
        if omegas is None:
            edge, got = lax.optimization_barrier((edge, got))
            omegas = prepare_call(keep, got, spread)
        part = beyond_call(n, edge, beyond, omegas)
        found = filter_call(n, part, block, partner, omegas)
        block, edge = found if n + 1 < ITERS else (found, None)
    back = exchange(block.reshape(TILES), ("zh", "zl"))
    return receive_call(exchange(inverse_call(back, ih, il, turns), ("x", "zl")))


def solution(mesh):
    tables = (*transform_tables(), spread_table(), turn_table())

    def run(traces_in, reweights, live_mask):
        return local(tables, traces_in, reweights, live_mask)

    inner = jax.sharding.Mesh(mesh.devices.reshape(-1, 2, 2, 4, 4), ("y", "zh", "c", "x", "zl"))
    inline, freq = ("y", "zh", "c"), ("x", "zl")
    in_specs = (P(freq, inline, None), P(None, freq, inline, None), P(inline, None))
    out_specs = P(freq, inline, None)
    return jax.shard_map(run, mesh=inner, in_specs=in_specs, out_specs=out_specs, check_vma=False)
```

```python
import functools
import math

import jax
import jax.numpy as jnp
import numpy as np
from jax import lax
from jax.experimental import pallas as pl
from jax.experimental.pallas import tpu as pltpu
from jax.sharding import PartitionSpec as P

NT = 2048
FILT = 4
ITERS = 2
RADIX = 16
SPAN = 128
BINS = 64
WINDOWS = 4
WX = 32
LANES = 128
f32, bf16 = jnp.float32, jnp.bfloat16


def low_bin(m, s, b):
    residue = m if s == 0 else (8 if m == 0 else RADIX - m)
    return 16 * b + residue


INNER = [(a, s, b) for a in range(2) for s in range(2) for b in range(2)]
HALF = BINS // 2
SETS = ((0, 3), (1, 2))


def split_table(table):
    high = table.astype(np.float32).astype(bf16)
    low = (table - high.astype(np.float64)).astype(np.float32).astype(bf16)
    return high, low


def transform_tables():
    forward = np.zeros((2, 2 * SPAN, 2 * SPAN))
    inverse = np.zeros((2, 2 * SPAN, 2 * SPAN))
    r = np.arange(SPAN)
    for spot in range(2 * 8):
        kappa, part = divmod(spot, 8)
        zh, zl = divmod(part, 4)
        for place, (a, s, b) in enumerate(INNER):
            base = BINS * (4 * SETS[kappa][a] + zl) + HALF * zh + 16 * b
            col = spot * 8 + place
            f = base + 8 * s
            angle = 2.0 * np.pi * ((f * r) % NT) / NT
            span = slice(s * SPAN, (s + 1) * SPAN)
            forward[0, span, col] = np.cos(angle)
            forward[0, span, SPAN + col] = -np.sin(angle)
            angle = 2.0 * np.pi * (((base // RADIX + s) * r) % SPAN) / SPAN
            sign = 1.0 if s == 0 else -1.0
            forward[1, :SPAN, col] = np.cos(angle)
            forward[1, SPAN:, col] = sign * np.sin(angle)
            forward[1, :SPAN, SPAN + col] = -np.sin(angle)
            forward[1, SPAN:, SPAN + col] = sign * np.cos(angle)
            scale = (1.0 if f == 0 else 2.0) / NT
            for which, factor in ((0, scale), (1, 1.0 / NT)):
                inverse[which, col] = forward[which, :, col] * factor
                inverse[which, SPAN + col] = forward[which, :, SPAN + col] * factor
    return split_table(forward), split_table(inverse)


def turn_table():
    angle = 2.0 * np.pi * np.arange(8)[:, None] * np.arange(SPAN)[None] / NT
    return np.stack([np.cos(angle), np.sin(angle)]).astype(np.float32)


def spread_table():
    table = np.zeros((BINS, LANES), np.float32)
    for m in range(8):
        for place, (a, s, b) in enumerate(INNER):
            row = HALF * a + low_bin(m, s, b)
            table[row, m * 8 + place] = 1.0
            table[row, BINS + m * 8 + place] = 1.0
    return table.astype(bf16)


def cadd(a, b):
    im = a[1] if b[1] is None else (b[1] if a[1] is None else a[1] + b[1])
    return a[0] + b[0], im


def csub(a, b):
    im = a[1] if b[1] is None else (-b[1] if a[1] is None else a[1] - b[1])
    return a[0] - b[0], im


def conj(a):
    return a[0], None if a[1] is None else -a[1]


def turn(a, step, size):
    step = step % size
    if step == 0:
        return a
    if 4 * step == size:
        return (jnp.zeros_like(a[0]) if a[1] is None else -a[1]), a[0]
    if 4 * step == 3 * size:
        return (jnp.zeros_like(a[0]) if a[1] is None else a[1]), -a[0]
    c, s = math.cos(2 * math.pi * step / size), math.sin(2 * math.pi * step / size)
    if a[1] is None:
        return a[0] * c, a[0] * s
    return a[0] * c - a[1] * s, a[0] * s + a[1] * c


def real_transform(values):
    n = len(values)
    if n == 1:
        return [(values[0], None)]
    if n == 2:
        return [(values[0] + values[1], None), (values[0] - values[1], None)]
    even, odd = real_transform(values[::2]), real_transform(values[1::2])
    out = [None] * (n // 2 + 1)
    for p in range(n // 4 + 1):
        turned = turn(odd[p], -p, n)
        out[p] = cadd(even[p], turned)
        out[n // 2 - p] = conj(csub(even[p], turned))
    out[0] = (out[0][0], None)
    out[n // 2] = (out[n // 2][0], None)
    return out


def real_inverse(bins):
    n = 2 * (len(bins) - 1)
    if n == 2:
        return [bins[0][0] + bins[1][0], bins[0][0] - bins[1][0]]
    quarter = n // 4
    first, second = [], []
    for p in range(quarter + 1):
        other = conj(bins[n // 2 - p])
        total, rest = cadd(bins[p], other), turn(csub(bins[p], other), p, n)
        if p in (0, quarter):
            total, rest = (total[0], None), (rest[0], None)
        first.append(total)
        second.append(rest)
    out = [None] * n
    out[::2], out[1::2] = real_inverse(first), real_inverse(second)
    return out


def split_dot(lhs, high, low):
    rows = lhs.shape[0]
    top = lhs.astype(bf16)
    rest = (lhs - top.astype(f32)).astype(bf16)
    both = jnp.dot(jnp.concatenate([top, rest], axis=0), high, preferred_element_type=f32)
    return both[:rows] + both[rows:] + jnp.dot(top, low, preferred_element_type=f32)


def swap_blocks(arrays, lane, width):
    arrays = list(arrays)
    n = len(arrays)
    d = 1
    while d < n:
        upper = (lane & (width * d)) != 0
        for i in range(n):
            if i & d:
                continue
            a, b = arrays[i], arrays[i + d]
            arrays[i] = jnp.where(upper, pltpu.roll(b, width * d, 1), a)
            arrays[i + d] = jnp.where(upper, b, pltpu.roll(a, LANES - width * d, 1))
        d *= 2
    return arrays


def lanes_of(rows):
    return lax.broadcasted_iota(jnp.int32, (rows, LANES), 1)


def place_x():
    return 2 * lax.axis_index("xq") + lax.axis_index("xr")


def send_kernel(traces, out):
    for i in range(FILT):
        turned = traces[pl.ds(i, SPAN, stride=FILT), :].T
        for w in range(WINDOWS):
            out[w * FILT + i] = turned[w * WX : (w + 1) * WX]


def forward_kernel(blocks, live, high, low, turns, out, alive):
    xq = lax.axis_index("xq")
    row = live[pl.ds(lax.axis_index("zl"), 1), :].astype(f32)
    alive[...] = jnp.broadcast_to(row, (LANES, LANES)).T
    mask = alive[pl.ds(pl.multiple_of(place_x() * WX, WX), WX), :]
    lane = lanes_of(WX)
    bins = real_transform([blocks[j] * mask for j in range(RADIX)])
    first = split_dot(jnp.concatenate([bins[0][0], bins[8][0]], axis=1), high[0], low[0])
    rows = []
    for m in range(1, 8):
        (re, im), c, s = bins[m], turns[0, m : m + 1, :], turns[1, m : m + 1, :]
        rows.append(jnp.concatenate([re * c + im * s, im * c - re * s], axis=1))
    others = split_dot(jnp.concatenate(rows, axis=0), high[1], low[1])
    real = [first[:, :LANES]] + [others[WX * m : WX * m + WX, :LANES] for m in range(7)]
    imag = [first[:, LANES:]] + [others[WX * m : WX * m + WX, LANES:] for m in range(7)]
    real, imag = swap_blocks(real, lane, 8), swap_blocks(imag, lane, 8)
    left = lane < BINS
    for part in range(8):
        place = part // 4 * 8 + part % 4
        out[place + 4 * xq] = jnp.where(left, real[part], pltpu.roll(imag[part], BINS, 1))
        out[place + 4 - 4 * xq] = jnp.where(left, pltpu.roll(real[part], BINS, 1), imag[part])


def inverse_kernel(blocks, high, low, turns, out):
    xq = lax.axis_index("xq")
    lane = lanes_of(WX)
    left = lane < BINS
    real, imag = [], []
    for part in range(8):
        place = part // 4 * 8 + part % 4
        first, second = blocks[place + 4 * xq], blocks[place + 4 - 4 * xq]
        real.append(jnp.where(left, first, pltpu.roll(second, BINS, 1)))
        imag.append(jnp.where(left, pltpu.roll(first, BINS, 1), second))
    real, imag = swap_blocks(real, lane, 8), swap_blocks(imag, lane, 8)
    first = split_dot(jnp.concatenate([real[0], imag[0]], axis=1), high[0], low[0])
    rows = [jnp.concatenate([real[m], imag[m]], axis=1) for m in range(1, 8)]
    others = split_dot(jnp.concatenate(rows, axis=0), high[1], low[1])
    bins = [(first[:, :LANES], None)] + [None] * 7 + [(first[:, LANES:], None)]
    for m in range(1, 8):
        value = others[WX * (m - 1) : WX * m]
        re, im, c, s = value[:, :LANES], value[:, LANES:], turns[0, m : m + 1, :], turns[1, m : m + 1, :]
        bins[m] = (re * c - im * s, re * s + im * c)
    for j, values in enumerate(real_inverse(bins)):
        out[j] = values


def receive_kernel(blocks, out):
    for i in range(FILT):
        rows = jnp.concatenate([blocks[w * FILT + i] for w in range(WINDOWS)], axis=0)
        out[pl.ds(i, SPAN, stride=FILT), :] = rows.T


def solve(matrix, target):
    n = FILT
    trace = matrix[0][0][0]
    for k in range(1, n):
        trace = trace + matrix[k][k][0]
    ridge = (0.05 * 2.0 / (2 * n)) * trace + 1e-05

    def cmul(a, b):
        return a[0] * b[0] - a[1] * b[1], a[0] * b[1] + a[1] * b[0]

    diag = [matrix[k][k][0] + ridge for k in range(n)]
    upper = {(k, l): matrix[k][l] for k in range(n) for l in range(k + 1, n)}
    rhs = list(target)
    inv = [None] * n
    for k in range(n):
        inv[k] = 1.0 / diag[k]
        for i in range(k + 1, n):
            re, im = upper[k, i]
            factor = (re * inv[k], -im * inv[k])
            diag[i] = diag[i] - (re * factor[0] - im * factor[1])
            for l in range(i + 1, n):
                t = cmul(factor, upper[k, l])
                upper[i, l] = (upper[i, l][0] - t[0], upper[i, l][1] - t[1])
            t = cmul(factor, rhs[k])
            rhs[i] = (rhs[i][0] - t[0], rhs[i][1] - t[1])
    found = [None] * n
    for k in reversed(range(n)):
        re, im = rhs[k]
        for l in range(k + 1, n):
            t = cmul(upper[k, l], found[l])
            re, im = re - t[0], im - t[1]
        found[k] = (re * inv[k], im * inv[k])
    return found


PAIRS = [(k, l) for k in range(FILT) for l in range(k, FILT)]
OFF = [(k, l) for k, l in PAIRS if k < l]
SUMS = len(PAIRS) + len(OFF) + 2 * FILT


def windows_kernel(weights, live, here, across, held):
    alive = live[...].astype(f32)
    for n in range(ITERS):
        rows = []
        for i in range(FILT):
            start = n * BINS * FILT + i
            rows.append(weights[pl.ds(start, BINS, stride=FILT), :] * alive[i : i + 1])
        for w, block in enumerate(swap_blocks(rows, lanes_of(BINS), WX)):
            held[w, n] = block
    xq = lax.axis_index("xq")
    for w in range(2):
        here[w] = held[2 * xq + w]
        across[w] = held[2 - 2 * xq + w]


def halves_kernel(here, across, keep, give):
    own, xq = lax.axis_index("zh") * HALF, lax.axis_index("xq")
    for source, place in ((here, xq), (across, 1 - xq)):
        for w in range(2):
            for n in range(ITERS):
                keep[place, w, n] = source[w, n, pl.ds(pl.multiple_of(own, HALF), HALF), :]
                give[place, w, n] = source[w, n, pl.ds(pl.multiple_of(HALF - own, HALF), HALF), :]


def prepare_kernel(keep, got, spread, omega):
    own = lax.axis_index("zh")
    table = spread[...]
    over = (((0,), (0,)), ((), ()))
    for n in range(ITERS):
        for source, beta in ((keep, own), (got, 1 - own)):
            for w in range(2):
                rows = jnp.concatenate([source[a, w, n] for a in range(2)], axis=0)
                top = rows.astype(bf16)
                rest = (rows - top.astype(f32)).astype(bf16)
                omega[n, beta * 2 + w] = lax.dot_general(
                    top, table, over, preferred_element_type=f32
                ) + lax.dot_general(rest, table, over, preferred_element_type=f32)


def predictions(jobs, omega, turned, sums, coefs, store):
    slots = TWO * len(jobs)
    blocks = []
    for own, side, _, _ in jobs:
        blocks += [ref for ref in (own, side) if all(ref is not other for other in blocks)]
    for place, ref in enumerate(blocks):
        for k in range(TWO * FILT):
            turned[place, k] = pltpu.roll(ref[k], BINS, 1)
    places = [[next(p for p, other in enumerate(blocks) if other is ref) for ref in job[:2]] for job in jobs]

    def tile_of(row, w, flip):
        row = row % FILT
        return w * FILT + row + flip * (FILT - 1 - 2 * row)

    def rows_of(job, w, lines):
        own, side, _, flip = jobs[job]
        plain, quarter = [], []
        for row in range(2 * FILT):
            which, tile = row // FILT, tile_of(row, w, flip)
            plain.append((own, side)[which][tile, lines, :])
            quarter.append(turned[places[job][which], tile, lines, :])
        return plain, quarter

    def weight_of(job, i, w, sub):
        _, _, beta, flip = jobs[job]
        start = tile_of(i, 0, flip) * ROWS + sub * 8
        return omega[beta * TWO + w, pl.ds(pl.multiple_of(start, 8), 8), :]

    def gather(w, carry):
        for job in range(len(jobs)):
            acc = [None] * SUMS

            def add(place, value):
                acc[place] = value if acc[place] is None else acc[place] + value

            for sub in range(ROWS // 8):
                rows, turns = rows_of(job, w, pl.ds(sub * 8, 8))
                for i in range(FILT):
                    om = weight_of(job, i, w, sub)
                    weighted = [om * rows[i + k + 1] for k in range(FILT)]
                    place = 0
                    for k, l in PAIRS:
                        add(place, weighted[k] * rows[i + l + 1])
                        place += 1
                    for k, l in OFF:
                        add(place, weighted[k] * turns[i + l + 1])
                        place += 1
                    for k in range(FILT):
                        add(place, weighted[k] * rows[i])
                        add(place + 1, weighted[k] * turns[i])
                        place += 2
            start = pl.multiple_of((job * TWO + w) * 8, 8)
            for place in range(SUMS):
                sums[place, pl.ds(start, 8), :] = acc[place]
        return carry

    lax.fori_loop(0, TWO, gather, 0)

    sign = jnp.where(lanes_of(slots) < BINS, 1.0, -1.0).astype(f32)

    def total(place):
        value = sums[place, pl.ds(0, slots, stride=8), :]
        for s in range(1, 8):
            value = value + sums[place, pl.ds(s, slots, stride=8), :]
        return value

    def real_sum(place):
        value = total(place)
        return value + pltpu.roll(value, BINS, 1)

    def imag_sum(place):
        value = total(place)
        return (value - pltpu.roll(value, BINS, 1)) * sign

    matrix = [[None] * FILT for _ in range(FILT)]
    for place, (k, l) in enumerate(PAIRS):
        matrix[k][l] = (real_sum(place), None)
    for place, (k, l) in enumerate(OFF):
        matrix[k][l] = (matrix[k][l][0], imag_sum(len(PAIRS) + place))
    base = len(PAIRS) + len(OFF)
    target = [(real_sum(base + 2 * k), imag_sum(base + 2 * k + 1)) for k in range(FILT)]
    for k, (re, im) in enumerate(solve(matrix, target)):
        coefs[2 * k] = re
        coefs[2 * k + 1] = -im * sign

    def predict(w, carry):
        for sub in range(ROWS // 8):
            lines = pl.ds(sub * 8, 8)
            for job in range(len(jobs)):
                rows, turns = rows_of(job, w, lines)
                acc = [None] * FILT
                for k in range(FILT):
                    one = coefs[2 * k, pl.ds(job * TWO + w, 1), :]
                    two = coefs[2 * k + 1, pl.ds(job * TWO + w, 1), :]
                    for i in range(FILT):
                        value = one * rows[i + k + 1] + two * turns[i + k + 1]
                        acc[i] = value if acc[i] is None else acc[i] + value
                for i in range(FILT):
                    store(job, tile_of(i, w, jobs[job][3]), lines, acc[i], weight_of(job, i, w, sub))
        return carry

    lax.fori_loop(0, TWO, predict, 0)


def pick_kernel(block, out):
    out[...] = block[lax.axis_index("c")]


def beyond_kernel(n, beyond, edge, omegas, out, turned, sums, coefs):
    core = lax.axis_index("c")

    def store(job, tile, lines, value, weight):
        out[tile, lines, :] = value

    predictions([(edge, beyond, core, 1 - core)], omegas.at[n], turned, sums, coefs, store)


def filter_kernel(n, part, own, partner, omegas, *refs):
    *outs, turned, sums, coefs = refs
    core = lax.axis_index("c")
    rest_at, edge_at = (1 - core, core) if n == 0 else (0, 1)
    rest, edge = own.at[rest_at], own.at[edge_at]
    near, far = (partner.at[core], partner.at[1 - core]) if n == 0 else (partner.at[0], partner.at[1])
    new_rest, new_edge = (outs[0].at[0], outs[0].at[1]) if n + 1 < ITERS else (outs[0].at[1 - core], outs[0].at[core])

    def store(job, tile, lines, value, weight):
        half = jnp.where(weight > 0.0, 0.5, 0.0)
        if job == 0:
            value = (value + part[tile, lines, :]) * half
            new_edge[tile, lines, :] = value
            if n + 1 < ITERS:
                outs[1][tile, lines, :] = value
        elif job == 1:
            new_rest[tile, lines, :] = value
        else:
            new_rest[tile, lines, :] = (new_rest[tile, lines, :] + value) * half

    jobs = [(edge, near, core, core), (rest, near, 1 - core, 1 - core), (rest, far, 1 - core, core)]
    predictions(jobs, omegas.at[n], turned, sums, coefs, store)


def kernel_call(body, shapes, scratch=(), name=None, cost=None):
    out = [jax.ShapeDtypeStruct(shape, f32) for shape in shapes]
    return pl.pallas_call(
        body,
        out_shape=out if len(out) > 1 else out[0],
        scratch_shapes=list(scratch),
        compiler_params=pltpu.CompilerParams(vmem_limit_bytes=16 * 1024 * 1024),
        name=name,
        cost_estimate=cost,
    )


TRACES = (RADIX, WX, LANES)
TWO = 2
ROWS = WX
TILES = (2 * TWO * FILT, ROWS, LANES)
EDGE = (TWO * FILT, ROWS, LANES)
PART = (2, ITERS, BINS, LANES)
HALVES = (2, 2, ITERS, HALF, LANES)


def send_call(traces):
    return kernel_call(send_kernel, [TRACES], name="send")(traces.reshape(SPAN * FILT, LANES))


def forward_call(blocks, live, *tables):
    scratch = [pltpu.VMEM((LANES, LANES), f32)]
    return kernel_call(forward_kernel, [TILES], scratch, "forward")(blocks, live, *tables)


def inverse_call(blocks, *tables):
    return kernel_call(inverse_kernel, [TRACES], name="inverse")(blocks, *tables)


LONG = pl.CostEstimate(flops=16_000_000_000, bytes_accessed=64_000_000, transcendentals=0)


def windows_call(weights, live):
    scratch = [pltpu.VMEM((WINDOWS,) + PART[1:], f32)]
    return kernel_call(windows_kernel, [PART, PART], scratch, "windows")(weights, live)


def halves_call(*arrays):
    return kernel_call(halves_kernel, [HALVES, HALVES], (), "halves", LONG)(*arrays)


def prepare_call(*arrays):
    shape = (ITERS, 2 * TWO, FILT * ROWS, LANES)
    return kernel_call(prepare_kernel, [shape], (), "prepare")(*arrays)


def filter_scratch(blocks, jobs):
    return [
        pltpu.VMEM((blocks,) + EDGE, f32),
        pltpu.VMEM((SUMS, 8 * TWO * jobs, LANES), f32),
        pltpu.VMEM((2 * FILT, TWO * jobs, LANES), f32),
    ]


def pick_call(block):
    return kernel_call(pick_kernel, [EDGE], (), "pick", LONG)(block)


def beyond_call(n, edge, beyond, omegas):
    body = functools.partial(beyond_kernel, n)
    cost = pl.CostEstimate(flops=4_000_000_000, bytes_accessed=16_000_000, transcendentals=0)
    return kernel_call(body, [EDGE], filter_scratch(2, 1), "beyond", cost)(beyond, edge, omegas)


def filter_call(n, part, own, partner, omegas):
    both = (2,) + EDGE
    shapes = [both, EDGE] if n + 1 < ITERS else [both]
    body = functools.partial(filter_kernel, n)
    return kernel_call(body, shapes, filter_scratch(4, 3), name="filter")(part, own, partner, omegas)


def receive_call(blocks):
    return kernel_call(receive_kernel, [(SPAN * FILT, LANES)], name="receive")(blocks).reshape(
        SPAN, FILT, LANES
    )


def local(tables, traces_in, reweights, live_mask):
    (fh, fl), (ih, il), spread, turns = tables
    fh, fl, ih, il, spread, turns = (jnp.asarray(t) for t in (fh, fl, ih, il, spread, turns))

    def exchange(blocks, axes):
        return lax.all_to_all(blocks, axes, 0, 0, tiled=True)

    swap = [(0, 1), (1, 0)]
    ys = lax.axis_size("y")
    shift = [(2 * y + 1, 2 * y + 2) for y in range(ys - 1)] + [(2 * y + 2, 2 * y + 1) for y in range(ys - 1)]
    weights = reweights.reshape(ITERS * BINS * FILT, LANES)
    sent = send_call(traces_in)
    here, across = windows_call(weights, live_mask)
    across = lax.ppermute(across, ("xq", "xr"), [(i, WINDOWS - 1 - i) for i in range(WINDOWS)])
    keep, give = halves_call(here, across)
    got = lax.ppermute(give, "zh", swap)
    spectra = forward_call(exchange(sent, ("xq", "xr", "zl")), live_mask, fh, fl, turns)
    block = exchange(spectra, ("zh", "xr", "zl")).reshape((2,) + EDGE)
    edge = pick_call(block)
    omegas = None
    for n in range(ITERS):
        beyond = lax.ppermute(edge, ("y", "c"), shift)
        partner = lax.ppermute(block, "c", swap)
        if omegas is None:
            edge, got = lax.optimization_barrier((edge, got))
            omegas = prepare_call(keep, got, spread)
        part = beyond_call(n, edge, beyond, omegas)
        found = filter_call(n, part, block, partner, omegas)
        block, edge = found if n + 1 < ITERS else (found, None)
    back = exchange(block.reshape(TILES), ("zh", "xr", "zl"))
    return receive_call(exchange(inverse_call(back, ih, il, turns), ("xq", "xr", "zl")))


def solution(mesh):
    tables = (*transform_tables(), spread_table(), turn_table())

    def run(traces_in, reweights, live_mask):
        return local(tables, traces_in, reweights, live_mask)

    inner = jax.sharding.Mesh(mesh.devices.reshape(-1, 2, 2, 2, 2, 4), ("y", "zh", "c", "xq", "xr", "zl"))
    inline, freq = ("y", "zh", "c"), ("xq", "xr", "zl")
    in_specs = (P(freq, inline, None), P(None, freq, inline, None), P(inline, None))
    out_specs = P(freq, inline, None)
    return jax.shard_map(run, mesh=inner, in_specs=in_specs, out_specs=out_specs, check_vma=False)
```

```python
import functools
import math

import jax
import jax.numpy as jnp
import numpy as np
from jax import lax
from jax.experimental import pallas as pl
from jax.experimental.pallas import tpu as pltpu
from jax.sharding import PartitionSpec as P

NT = 2048
FILT = 4
ITERS = 2
RADIX = 16
SPAN = 128
BINS = 64
WINDOWS = 4
WX = 32
LANES = 128
f32, bf16 = jnp.float32, jnp.bfloat16


def low_bin(m, s, b):
    residue = m if s == 0 else (8 if m == 0 else RADIX - m)
    return 16 * b + residue


INNER = [(a, s, b) for a in range(2) for s in range(2) for b in range(2)]
HALF = BINS // 2
SETS = ((0, 3), (1, 2))


def held_bins(zh, zl):
    z = 4 * zh + zl
    return (0, z - 2) if 2 <= z <= 5 else (1, (z + 2) % 8)


def split_table(table):
    high = table.astype(np.float32).astype(bf16)
    low = (table - high.astype(np.float64)).astype(np.float32).astype(bf16)
    return high, low


def transform_tables():
    forward = np.zeros((2, 2 * SPAN, 2 * SPAN))
    inverse = np.zeros((2, 2 * SPAN, 2 * SPAN))
    r = np.arange(SPAN)
    for spot in range(2 * 8):
        kappa, part = divmod(spot, 8)
        half, source = held_bins(*divmod(part, 4))
        for place, (a, s, b) in enumerate(INNER):
            base = BINS * (4 * SETS[kappa][a] + source) + HALF * half + 16 * b
            col = spot * 8 + place
            f = base + 8 * s
            angle = 2.0 * np.pi * ((f * r) % NT) / NT
            span = slice(s * SPAN, (s + 1) * SPAN)
            forward[0, span, col] = np.cos(angle)
            forward[0, span, SPAN + col] = -np.sin(angle)
            angle = 2.0 * np.pi * (((base // RADIX + s) * r) % SPAN) / SPAN
            sign = 1.0 if s == 0 else -1.0
            forward[1, :SPAN, col] = np.cos(angle)
            forward[1, SPAN:, col] = sign * np.sin(angle)
            forward[1, :SPAN, SPAN + col] = -np.sin(angle)
            forward[1, SPAN:, SPAN + col] = sign * np.cos(angle)
            scale = (1.0 if f == 0 else 2.0) / NT
            for which, factor in ((0, scale), (1, 1.0 / NT)):
                inverse[which, col] = forward[which, :, col] * factor
                inverse[which, SPAN + col] = forward[which, :, SPAN + col] * factor
    return split_table(forward), split_table(inverse)


def turn_table():
    angle = 2.0 * np.pi * np.arange(8)[:, None] * np.arange(SPAN)[None] / NT
    return np.stack([np.cos(angle), np.sin(angle)]).astype(np.float32)


def spread_table():
    table = np.zeros((BINS, LANES), np.float32)
    for m in range(8):
        for place, (a, s, b) in enumerate(INNER):
            row = HALF * a + low_bin(m, s, b)
            table[row, m * 8 + place] = 1.0
            table[row, BINS + m * 8 + place] = 1.0
    return table.astype(bf16)


def cadd(a, b):
    im = a[1] if b[1] is None else (b[1] if a[1] is None else a[1] + b[1])
    return a[0] + b[0], im


def csub(a, b):
    im = a[1] if b[1] is None else (-b[1] if a[1] is None else a[1] - b[1])
    return a[0] - b[0], im


def conj(a):
    return a[0], None if a[1] is None else -a[1]


def turn(a, step, size):
    step = step % size
    if step == 0:
        return a
    if 4 * step == size:
        return (jnp.zeros_like(a[0]) if a[1] is None else -a[1]), a[0]
    if 4 * step == 3 * size:
        return (jnp.zeros_like(a[0]) if a[1] is None else a[1]), -a[0]
    c, s = math.cos(2 * math.pi * step / size), math.sin(2 * math.pi * step / size)
    if a[1] is None:
        return a[0] * c, a[0] * s
    return a[0] * c - a[1] * s, a[0] * s + a[1] * c


def real_transform(values):
    n = len(values)
    if n == 1:
        return [(values[0], None)]
    if n == 2:
        return [(values[0] + values[1], None), (values[0] - values[1], None)]
    even, odd = real_transform(values[::2]), real_transform(values[1::2])
    out = [None] * (n // 2 + 1)
    for p in range(n // 4 + 1):
        turned = turn(odd[p], -p, n)
        out[p] = cadd(even[p], turned)
        out[n // 2 - p] = conj(csub(even[p], turned))
    out[0] = (out[0][0], None)
    out[n // 2] = (out[n // 2][0], None)
    return out


def real_inverse(bins):
    n = 2 * (len(bins) - 1)
    if n == 2:
        return [bins[0][0] + bins[1][0], bins[0][0] - bins[1][0]]
    quarter = n // 4
    first, second = [], []
    for p in range(quarter + 1):
        other = conj(bins[n // 2 - p])
        total, rest = cadd(bins[p], other), turn(csub(bins[p], other), p, n)
        if p in (0, quarter):
            total, rest = (total[0], None), (rest[0], None)
        first.append(total)
        second.append(rest)
    out = [None] * n
    out[::2], out[1::2] = real_inverse(first), real_inverse(second)
    return out


def split_dot(lhs, high, low):
    rows = lhs.shape[0]
    top = lhs.astype(bf16)
    rest = (lhs - top.astype(f32)).astype(bf16)
    both = jnp.dot(jnp.concatenate([top, rest], axis=0), high, preferred_element_type=f32)
    return both[:rows] + both[rows:] + jnp.dot(top, low, preferred_element_type=f32)


def swap_blocks(arrays, lane, width):
    arrays = list(arrays)
    n = len(arrays)
    d = 1
    while d < n:
        upper = (lane & (width * d)) != 0
        for i in range(n):
            if i & d:
                continue
            a, b = arrays[i], arrays[i + d]
            arrays[i] = jnp.where(upper, pltpu.roll(b, width * d, 1), a)
            arrays[i + d] = jnp.where(upper, b, pltpu.roll(a, LANES - width * d, 1))
        d *= 2
    return arrays


def lanes_of(rows):
    return lax.broadcasted_iota(jnp.int32, (rows, LANES), 1)


def place_x():
    return 2 * lax.axis_index("xq") + lax.axis_index("xr")


def send_kernel(traces, out):
    for i in range(FILT):
        turned = traces[pl.ds(i, SPAN, stride=FILT), :].T
        for w in range(WINDOWS):
            out[w * FILT + i] = turned[w * WX : (w + 1) * WX]


def forward_kernel(blocks, live, high, low, turns, out, alive):
    xq = lax.axis_index("xq")
    row = live[pl.ds(lax.axis_index("zl"), 1), :].astype(f32)
    alive[...] = jnp.broadcast_to(row, (LANES, LANES)).T
    mask = alive[pl.ds(pl.multiple_of(place_x() * WX, WX), WX), :]
    lane = lanes_of(WX)
    bins = real_transform([blocks[j] * mask for j in range(RADIX)])
    first = split_dot(jnp.concatenate([bins[0][0], bins[8][0]], axis=1), high[0], low[0])
    rows = []
    for m in range(1, 8):
        (re, im), c, s = bins[m], turns[0, m : m + 1, :], turns[1, m : m + 1, :]
        rows.append(jnp.concatenate([re * c + im * s, im * c - re * s], axis=1))
    others = split_dot(jnp.concatenate(rows, axis=0), high[1], low[1])
    real = [first[:, :LANES]] + [others[WX * m : WX * m + WX, :LANES] for m in range(7)]
    imag = [first[:, LANES:]] + [others[WX * m : WX * m + WX, LANES:] for m in range(7)]
    real, imag = swap_blocks(real, lane, 8), swap_blocks(imag, lane, 8)
    left = lane < BINS
    for part in range(8):
        place = part // 4 * 8 + part % 4
        out[place + 4 * xq] = jnp.where(left, real[part], pltpu.roll(imag[part], BINS, 1))
        out[place + 4 - 4 * xq] = jnp.where(left, pltpu.roll(real[part], BINS, 1), imag[part])


def inverse_kernel(blocks, high, low, turns, out):
    xq = lax.axis_index("xq")
    lane = lanes_of(WX)
    left = lane < BINS
    real, imag = [], []
    for part in range(8):
        place = part // 4 * 8 + part % 4
        first, second = blocks[place + 4 * xq], blocks[place + 4 - 4 * xq]
        real.append(jnp.where(left, first, pltpu.roll(second, BINS, 1)))
        imag.append(jnp.where(left, pltpu.roll(first, BINS, 1), second))
    real, imag = swap_blocks(real, lane, 8), swap_blocks(imag, lane, 8)
    first = split_dot(jnp.concatenate([real[0], imag[0]], axis=1), high[0], low[0])
    rows = [jnp.concatenate([real[m], imag[m]], axis=1) for m in range(1, 8)]
    others = split_dot(jnp.concatenate(rows, axis=0), high[1], low[1])
    bins = [(first[:, :LANES], None)] + [None] * 7 + [(first[:, LANES:], None)]
    for m in range(1, 8):
        value = others[WX * (m - 1) : WX * m]
        re, im, c, s = value[:, :LANES], value[:, LANES:], turns[0, m : m + 1, :], turns[1, m : m + 1, :]
        bins[m] = (re * c - im * s, re * s + im * c)
    for j, values in enumerate(real_inverse(bins)):
        out[j] = values


def receive_kernel(blocks, out):
    for i in range(FILT):
        rows = jnp.concatenate([blocks[w * FILT + i] for w in range(WINDOWS)], axis=0)
        out[pl.ds(i, SPAN, stride=FILT), :] = rows.T


def solve(matrix, target):
    n = FILT
    trace = matrix[0][0][0]
    for k in range(1, n):
        trace = trace + matrix[k][k][0]
    ridge = (0.05 * 2.0 / (2 * n)) * trace + 1e-05

    def cmul(a, b):
        return a[0] * b[0] - a[1] * b[1], a[0] * b[1] + a[1] * b[0]

    diag = [matrix[k][k][0] + ridge for k in range(n)]
    upper = {(k, l): matrix[k][l] for k in range(n) for l in range(k + 1, n)}
    rhs = list(target)
    inv = [None] * n
    for k in range(n):
        inv[k] = 1.0 / diag[k]
        for i in range(k + 1, n):
            re, im = upper[k, i]
            factor = (re * inv[k], -im * inv[k])
            diag[i] = diag[i] - (re * factor[0] - im * factor[1])
            for l in range(i + 1, n):
                t = cmul(factor, upper[k, l])
                upper[i, l] = (upper[i, l][0] - t[0], upper[i, l][1] - t[1])
            t = cmul(factor, rhs[k])
            rhs[i] = (rhs[i][0] - t[0], rhs[i][1] - t[1])
    found = [None] * n
    for k in reversed(range(n)):
        re, im = rhs[k]
        for l in range(k + 1, n):
            t = cmul(upper[k, l], found[l])
            re, im = re - t[0], im - t[1]
        found[k] = (re * inv[k], im * inv[k])
    return found


PAIRS = [(k, l) for k in range(FILT) for l in range(k, FILT)]
OFF = [(k, l) for k, l in PAIRS if k < l]
SUMS = len(PAIRS) + len(OFF) + 2 * FILT


def windows_kernel(weights, live, here, across, held):
    alive = live[...].astype(f32)
    for n in range(ITERS):
        rows = []
        for i in range(FILT):
            start = n * BINS * FILT + i
            rows.append(weights[pl.ds(start, BINS, stride=FILT), :] * alive[i : i + 1])
        for w, block in enumerate(swap_blocks(rows, lanes_of(BINS), WX)):
            held[w, n] = block
    xq = lax.axis_index("xq")
    for w in range(2):
        here[w] = held[2 * xq + w]
        across[w] = held[2 - 2 * xq + w]


def halves_kernel(here, across, plus, minus):
    own, xq = lax.axis_index("zh") * HALF, lax.axis_index("xq")
    for source, place in ((here, xq), (across, 1 - xq)):
        for w in range(2):
            for n in range(ITERS):
                plus[place, w, n] = source[w, n, pl.ds(pl.multiple_of(own, HALF), HALF), :]
                minus[place, w, n] = source[w, n, pl.ds(pl.multiple_of(HALF - own, HALF), HALF), :]


def prepare_kernel(plus, minus, spread, omega):
    z = 4 * lax.axis_index("zh") + lax.axis_index("zl")
    beta_plus = jnp.where((z >= 2) & (z <= 5), 0, 1)
    table = spread[...]
    over = (((0,), (0,)), ((), ()))
    for n in range(ITERS):
        for source, beta in ((plus, beta_plus), (minus, 1 - beta_plus)):
            for w in range(2):
                rows = jnp.concatenate([source[a, w, n] for a in range(2)], axis=0)
                top = rows.astype(bf16)
                rest = (rows - top.astype(f32)).astype(bf16)
                omega[n, beta * 2 + w] = lax.dot_general(
                    top, table, over, preferred_element_type=f32
                ) + lax.dot_general(rest, table, over, preferred_element_type=f32)


def predictions(jobs, omega, turned, sums, coefs, store):
    slots = TWO * len(jobs)
    def tile_of(row, w, flip):
        row = row % FILT
        return w * FILT + row + flip * (FILT - 1 - 2 * row)

    def rows_of(job, w, lines):
        own, side, _, flip = jobs[job]
        plain, quarter = [], []
        for row in range(2 * FILT):
            which, tile = row // FILT, tile_of(row, w, flip)
            plain.append((own, side)[which][tile, lines, :])
            quarter.append(pltpu.roll(plain[-1], BINS, 1))
        return plain, quarter

    def weight_of(job, i, w, sub):
        _, _, beta, flip = jobs[job]
        start = tile_of(i, 0, flip) * ROWS + sub * 8
        return omega[beta * TWO + w, pl.ds(pl.multiple_of(start, 8), 8), :]

    def gather(w, carry):
        for job in range(len(jobs)):
            acc = [None] * SUMS

            def add(place, value):
                acc[place] = value if acc[place] is None else acc[place] + value

            for sub in range(ROWS // 8):
                rows, turns = rows_of(job, w, pl.ds(sub * 8, 8))
                for i in range(FILT):
                    om = weight_of(job, i, w, sub)
                    weighted = [om * rows[i + k + 1] for k in range(FILT)]
                    place = 0
                    for k, l in PAIRS:
                        add(place, weighted[k] * rows[i + l + 1])
                        place += 1
                    for k, l in OFF:
                        add(place, weighted[k] * turns[i + l + 1])
                        place += 1
                    for k in range(FILT):
                        add(place, weighted[k] * rows[i])
                        add(place + 1, weighted[k] * turns[i])
                        place += 2
            start = (job * TWO + w) * 8
            for place in range(SUMS):
                sums[place, pl.ds(start, 8), :] = acc[place]
        return carry

    for w in range(TWO):
        gather(w, 0)

    sign = jnp.where(lanes_of(slots) < BINS, 1.0, -1.0).astype(f32)

    def total(place):
        value = sums[place, pl.ds(0, slots, stride=8), :]
        for s in range(1, 8):
            value = value + sums[place, pl.ds(s, slots, stride=8), :]
        return value

    def real_sum(place):
        value = total(place)
        return value + pltpu.roll(value, BINS, 1)

    def imag_sum(place):
        value = total(place)
        return (value - pltpu.roll(value, BINS, 1)) * sign

    matrix = [[None] * FILT for _ in range(FILT)]
    for place, (k, l) in enumerate(PAIRS):
        matrix[k][l] = (real_sum(place), None)
    for place, (k, l) in enumerate(OFF):
        matrix[k][l] = (matrix[k][l][0], imag_sum(len(PAIRS) + place))
    base = len(PAIRS) + len(OFF)
    target = [(real_sum(base + 2 * k), imag_sum(base + 2 * k + 1)) for k in range(FILT)]
    for k, (re, im) in enumerate(solve(matrix, target)):
        coefs[2 * k] = re
        coefs[2 * k + 1] = -im * sign

    def predict(w, carry):
        for sub in range(ROWS // 8):
            lines = pl.ds(sub * 8, 8)
            for job in range(len(jobs)):
                rows, turns = rows_of(job, w, lines)
                acc = [None] * FILT
                for k in range(FILT):
                    one = coefs[2 * k, pl.ds(job * TWO + w, 1), :]
                    two = coefs[2 * k + 1, pl.ds(job * TWO + w, 1), :]
                    for i in range(FILT):
                        value = one * rows[i + k + 1] + two * turns[i + k + 1]
                        acc[i] = value if acc[i] is None else acc[i] + value
                for i in range(FILT):
                    store(job, tile_of(i, w, jobs[job][3]), lines, acc[i], weight_of(job, i, w, sub))
        return carry

    for w in range(TWO):
        predict(w, 0)


def pick_kernel(block, out):
    out[...] = block[lax.axis_index("c")]


def beyond_kernel(n, beyond, edge, omegas, out, turned, sums, coefs):
    core = lax.axis_index("c")

    def store(job, tile, lines, value, weight):
        out[tile, lines, :] = value

    predictions([(edge, beyond, core, 1 - core)], omegas.at[n], turned, sums, coefs, store)


def filter_kernel(n, part, own, partner, omegas, *refs):
    *outs, turned, sums, coefs = refs
    core = lax.axis_index("c")
    rest_at, edge_at = (1 - core, core) if n == 0 else (0, 1)
    rest, edge = own.at[rest_at], own.at[edge_at]
    near, far = (partner.at[core], partner.at[1 - core]) if n == 0 else (partner.at[0], partner.at[1])
    new_rest, new_edge = (outs[0].at[0], outs[0].at[1]) if n + 1 < ITERS else (outs[0].at[1 - core], outs[0].at[core])

    def store(job, tile, lines, value, weight):
        half = jnp.where(weight > 0.0, 0.5, 0.0)
        if job == 0:
            value = (value + part[tile, lines, :]) * half
            new_edge[tile, lines, :] = value
            if n + 1 < ITERS:
                outs[1][tile, lines, :] = value
        elif job == 1:
            new_rest[tile, lines, :] = value
        else:
            new_rest[tile, lines, :] = (new_rest[tile, lines, :] + value) * half

    jobs = [(edge, near, core, core), (rest, near, 1 - core, 1 - core), (rest, far, 1 - core, core)]
    predictions(jobs, omegas.at[n], turned, sums, coefs, store)


def kernel_call(body, shapes, scratch=(), name=None, cost=None):
    out = [jax.ShapeDtypeStruct(shape, f32) for shape in shapes]
    return pl.pallas_call(
        body,
        out_shape=out if len(out) > 1 else out[0],
        scratch_shapes=list(scratch),
        compiler_params=pltpu.CompilerParams(vmem_limit_bytes=16 * 1024 * 1024),
        name=name,
        cost_estimate=cost,
    )


TRACES = (RADIX, WX, LANES)
TWO = 2
ROWS = WX
TILES = (2 * TWO * FILT, ROWS, LANES)
EDGE = (TWO * FILT, ROWS, LANES)
PART = (2, ITERS, BINS, LANES)
HALVES = (2, 2, ITERS, HALF, LANES)


def send_call(traces):
    return kernel_call(send_kernel, [TRACES], name="send")(traces.reshape(SPAN * FILT, LANES))


def forward_call(blocks, live, *tables):
    scratch = [pltpu.VMEM((LANES, LANES), f32)]
    return kernel_call(forward_kernel, [TILES], scratch, "forward")(blocks, live, *tables)


def inverse_call(blocks, *tables):
    return kernel_call(inverse_kernel, [TRACES], name="inverse")(blocks, *tables)


LONG = pl.CostEstimate(flops=16_000_000_000, bytes_accessed=64_000_000, transcendentals=0)


def windows_call(weights, live):
    scratch = [pltpu.VMEM((WINDOWS,) + PART[1:], f32)]
    return kernel_call(windows_kernel, [PART, PART], scratch, "windows")(weights, live)


def halves_call(*arrays):
    return kernel_call(halves_kernel, [HALVES, HALVES], (), "halves", LONG)(*arrays)


def prepare_call(*arrays):
    shape = (ITERS, 2 * TWO, FILT * ROWS, LANES)
    return kernel_call(prepare_kernel, [shape], (), "prepare")(*arrays)


def filter_scratch(blocks, jobs):
    return [
        pltpu.VMEM((blocks,) + EDGE, f32),
        pltpu.VMEM((SUMS, 8 * TWO * jobs, LANES), f32),
        pltpu.VMEM((2 * FILT, TWO * jobs, LANES), f32),
    ]


def pick_call(block):
    return kernel_call(pick_kernel, [EDGE], (), "pick", LONG)(block)


def beyond_call(n, edge, beyond, omegas):
    body = functools.partial(beyond_kernel, n)
    cost = pl.CostEstimate(flops=4_000_000_000, bytes_accessed=16_000_000, transcendentals=0)
    return kernel_call(body, [EDGE], filter_scratch(2, 1), "beyond", cost)(beyond, edge, omegas)


def filter_call(n, part, own, partner, omegas):
    both = (2,) + EDGE
    shapes = [both, EDGE] if n + 1 < ITERS else [both]
    body = functools.partial(filter_kernel, n)
    return kernel_call(body, shapes, filter_scratch(4, 3), name="filter")(part, own, partner, omegas)


def receive_call(blocks):
    return kernel_call(receive_kernel, [(SPAN * FILT, LANES)], name="receive")(blocks).reshape(
        SPAN, FILT, LANES
    )


def local(tables, traces_in, reweights, live_mask):
    (fh, fl), (ih, il), spread, turns = tables
    fh, fl, ih, il, spread, turns = (jnp.asarray(t) for t in (fh, fl, ih, il, spread, turns))

    def exchange(blocks, axes):
        return lax.all_to_all(blocks, axes, 0, 0, tiled=True)

    swap = [(0, 1), (1, 0)]
    ys = lax.axis_size("y")
    shift = [(2 * y + 1, 2 * y + 2) for y in range(ys - 1)] + [(2 * y + 2, 2 * y + 1) for y in range(ys - 1)]
    weights = reweights.reshape(ITERS * BINS * FILT, LANES)
    sent = send_call(traces_in)
    here, across = windows_call(weights, live_mask)
    across = lax.ppermute(across, ("xq", "xr"), [(i, WINDOWS - 1 - i) for i in range(WINDOWS)])
    plus, minus = halves_call(here, across)
    plus = lax.ppermute(plus, ("zh", "zl"), [(z, (z + 2) % 8) for z in range(8)])
    minus = lax.ppermute(minus, ("zh", "zl"), [(z, (z - 2) % 8) for z in range(8)])
    spectra = forward_call(exchange(sent, ("xq", "xr", "zl")), live_mask, fh, fl, turns)
    block = exchange(spectra, ("zh", "xr", "zl")).reshape((2,) + EDGE)
    edge = pick_call(block)
    omegas = None
    for n in range(ITERS):
        beyond = lax.ppermute(edge, ("y", "c"), shift)
        partner = lax.ppermute(block, "c", swap)
        if omegas is None:
            edge, plus, minus = lax.optimization_barrier((edge, plus, minus))
            omegas = prepare_call(plus, minus, spread)
        part = beyond_call(n, edge, beyond, omegas)
        found = filter_call(n, part, block, partner, omegas)
        block, edge = found if n + 1 < ITERS else (found, None)
    back = exchange(block.reshape(TILES), ("zh", "xr", "zl"))
    return receive_call(exchange(inverse_call(back, ih, il, turns), ("xq", "xr", "zl")))


def solution(mesh):
    tables = (*transform_tables(), spread_table(), turn_table())

    def run(traces_in, reweights, live_mask):
        return local(tables, traces_in, reweights, live_mask)

    inner = jax.sharding.Mesh(mesh.devices.reshape(-1, 2, 2, 2, 2, 4), ("y", "zh", "c", "xq", "xr", "zl"))
    inline, freq = ("y", "zh", "c"), ("xq", "xr", "zl")
    in_specs = (P(freq, inline, None), P(None, freq, inline, None), P(inline, None))
    out_specs = P(freq, inline, None)
    return jax.shard_map(run, mesh=inner, in_specs=in_specs, out_specs=out_specs, check_vma=False)
```

```python
import functools
import math

import jax
import jax.numpy as jnp
import numpy as np
from jax import lax
from jax.experimental import pallas as pl
from jax.experimental.pallas import tpu as pltpu
from jax.sharding import PartitionSpec as P

NT = 2048
FILT = 4
ITERS = 2
RADIX = 16
SPAN = 128
BINS = 64
WINDOWS = 4
WX = 32
LANES = 128
f32, bf16 = jnp.float32, jnp.bfloat16


def low_bin(m, s, b):
    residue = m if s == 0 else (8 if m == 0 else RADIX - m)
    return 16 * b + residue


INNER = [(a, s, b) for a in range(2) for s in range(2) for b in range(2)]
HALF = BINS // 2
SETS = ((0, 3), (1, 2))


def held_bins(zh, zl):
    z = 4 * zh + zl
    return (0, z - 2) if 2 <= z <= 5 else (1, (z + 2) % 8)


def split_table(table):
    high = table.astype(np.float32).astype(bf16)
    low = (table - high.astype(np.float64)).astype(np.float32).astype(bf16)
    return high, low


def transform_tables():
    forward = np.zeros((2, 2 * SPAN, 2 * SPAN))
    inverse = np.zeros((2, 2 * SPAN, 2 * SPAN))
    r = np.arange(SPAN)
    for spot in range(2 * 8):
        kappa, part = divmod(spot, 8)
        half, source = held_bins(*divmod(part, 4))
        for place, (a, s, b) in enumerate(INNER):
            base = BINS * (4 * SETS[kappa][a] + source) + HALF * half + 16 * b
            col = spot * 8 + place
            f = base + 8 * s
            angle = 2.0 * np.pi * ((f * r) % NT) / NT
            span = slice(s * SPAN, (s + 1) * SPAN)
            forward[0, span, col] = np.cos(angle)
            forward[0, span, SPAN + col] = -np.sin(angle)
            angle = 2.0 * np.pi * (((base // RADIX + s) * r) % SPAN) / SPAN
            sign = 1.0 if s == 0 else -1.0
            forward[1, :SPAN, col] = np.cos(angle)
            forward[1, SPAN:, col] = sign * np.sin(angle)
            forward[1, :SPAN, SPAN + col] = -np.sin(angle)
            forward[1, SPAN:, SPAN + col] = sign * np.cos(angle)
            scale = (1.0 if f == 0 else 2.0) / NT
            for which, factor in ((0, scale), (1, 1.0 / NT)):
                inverse[which, col] = forward[which, :, col] * factor
                inverse[which, SPAN + col] = forward[which, :, SPAN + col] * factor
    return split_table(forward), split_table(inverse)


def turn_table():
    angle = 2.0 * np.pi * np.arange(8)[:, None] * np.arange(SPAN)[None] / NT
    return np.stack([np.cos(angle), np.sin(angle)]).astype(np.float32)


def spread_table():
    table = np.zeros((BINS, LANES), np.float32)
    for m in range(8):
        for place, (a, s, b) in enumerate(INNER):
            row = HALF * a + low_bin(m, s, b)
            table[row, m * 8 + place] = 1.0
            table[row, BINS + m * 8 + place] = 1.0
    return table.astype(bf16)


def cadd(a, b):
    im = a[1] if b[1] is None else (b[1] if a[1] is None else a[1] + b[1])
    return a[0] + b[0], im


def csub(a, b):
    im = a[1] if b[1] is None else (-b[1] if a[1] is None else a[1] - b[1])
    return a[0] - b[0], im


def conj(a):
    return a[0], None if a[1] is None else -a[1]


def turn(a, step, size):
    step = step % size
    if step == 0:
        return a
    if 4 * step == size:
        return (jnp.zeros_like(a[0]) if a[1] is None else -a[1]), a[0]
    if 4 * step == 3 * size:
        return (jnp.zeros_like(a[0]) if a[1] is None else a[1]), -a[0]
    c, s = math.cos(2 * math.pi * step / size), math.sin(2 * math.pi * step / size)
    if a[1] is None:
        return a[0] * c, a[0] * s
    return a[0] * c - a[1] * s, a[0] * s + a[1] * c


def real_transform(values):
    n = len(values)
    if n == 1:
        return [(values[0], None)]
    if n == 2:
        return [(values[0] + values[1], None), (values[0] - values[1], None)]
    even, odd = real_transform(values[::2]), real_transform(values[1::2])
    out = [None] * (n // 2 + 1)
    for p in range(n // 4 + 1):
        turned = turn(odd[p], -p, n)
        out[p] = cadd(even[p], turned)
        out[n // 2 - p] = conj(csub(even[p], turned))
    out[0] = (out[0][0], None)
    out[n // 2] = (out[n // 2][0], None)
    return out


def real_inverse(bins):
    n = 2 * (len(bins) - 1)
    if n == 2:
        return [bins[0][0] + bins[1][0], bins[0][0] - bins[1][0]]
    quarter = n // 4
    first, second = [], []
    for p in range(quarter + 1):
        other = conj(bins[n // 2 - p])
        total, rest = cadd(bins[p], other), turn(csub(bins[p], other), p, n)
        if p in (0, quarter):
            total, rest = (total[0], None), (rest[0], None)
        first.append(total)
        second.append(rest)
    out = [None] * n
    out[::2], out[1::2] = real_inverse(first), real_inverse(second)
    return out


def split_dot(lhs, high, low):
    rows = lhs.shape[0]
    top = lhs.astype(bf16)
    rest = (lhs - top.astype(f32)).astype(bf16)
    both = jnp.dot(jnp.concatenate([top, rest], axis=0), high, preferred_element_type=f32)
    return both[:rows] + both[rows:] + jnp.dot(top, low, preferred_element_type=f32)


def swap_blocks(arrays, lane, width):
    arrays = list(arrays)
    n = len(arrays)
    d = 1
    while d < n:
        upper = (lane & (width * d)) != 0
        for i in range(n):
            if i & d:
                continue
            a, b = arrays[i], arrays[i + d]
            arrays[i] = jnp.where(upper, pltpu.roll(b, width * d, 1), a)
            arrays[i + d] = jnp.where(upper, b, pltpu.roll(a, LANES - width * d, 1))
        d *= 2
    return arrays


def lanes_of(rows):
    return lax.broadcasted_iota(jnp.int32, (rows, LANES), 1)


def place_x():
    return 2 * lax.axis_index("xq") + lax.axis_index("xr")


def send_kernel(traces, out):
    for i in range(FILT):
        turned = traces[pl.ds(i, SPAN, stride=FILT), :].T
        for w in range(WINDOWS):
            out[w * FILT + i] = turned[w * WX : (w + 1) * WX]


def forward_kernel(blocks, live, high, low, turns, out, alive):
    xq = lax.axis_index("xq")
    row = live[pl.ds(lax.axis_index("zl"), 1), :].astype(f32)
    alive[...] = jnp.broadcast_to(row, (LANES, LANES)).T
    mask = alive[pl.ds(pl.multiple_of(place_x() * WX, WX), WX), :]
    lane = lanes_of(WX)
    bins = real_transform([blocks[j] * mask for j in range(RADIX)])
    first = split_dot(jnp.concatenate([bins[0][0], bins[8][0]], axis=1), high[0], low[0])
    rows = []
    for m in range(1, 8):
        (re, im), c, s = bins[m], turns[0, m : m + 1, :], turns[1, m : m + 1, :]
        rows.append(jnp.concatenate([re * c + im * s, im * c - re * s], axis=1))
    others = split_dot(jnp.concatenate(rows, axis=0), high[1], low[1])
    real = [first[:, :LANES]] + [others[WX * m : WX * m + WX, :LANES] for m in range(7)]
    imag = [first[:, LANES:]] + [others[WX * m : WX * m + WX, LANES:] for m in range(7)]
    real, imag = swap_blocks(real, lane, 8), swap_blocks(imag, lane, 8)
    left = lane < BINS
    for part in range(8):
        place = part // 4 * 8 + part % 4
        out[place + 4 * xq] = jnp.where(left, real[part], pltpu.roll(imag[part], BINS, 1))
        out[place + 4 - 4 * xq] = jnp.where(left, pltpu.roll(real[part], BINS, 1), imag[part])


def inverse_kernel(blocks, high, low, turns, out):
    xq = lax.axis_index("xq")
    lane = lanes_of(WX)
    left = lane < BINS
    real, imag = [], []
    for part in range(8):
        place = part // 4 * 8 + part % 4
        first, second = blocks[place + 4 * xq], blocks[place + 4 - 4 * xq]
        real.append(jnp.where(left, first, pltpu.roll(second, BINS, 1)))
        imag.append(jnp.where(left, pltpu.roll(first, BINS, 1), second))
    real, imag = swap_blocks(real, lane, 8), swap_blocks(imag, lane, 8)
    first = split_dot(jnp.concatenate([real[0], imag[0]], axis=1), high[0], low[0])
    rows = [jnp.concatenate([real[m], imag[m]], axis=1) for m in range(1, 8)]
    others = split_dot(jnp.concatenate(rows, axis=0), high[1], low[1])
    bins = [(first[:, :LANES], None)] + [None] * 7 + [(first[:, LANES:], None)]
    for m in range(1, 8):
        value = others[WX * (m - 1) : WX * m]
        re, im, c, s = value[:, :LANES], value[:, LANES:], turns[0, m : m + 1, :], turns[1, m : m + 1, :]
        bins[m] = (re * c - im * s, re * s + im * c)
    for j, values in enumerate(real_inverse(bins)):
        out[j] = values


def receive_kernel(blocks, out):
    for i in range(FILT):
        rows = jnp.concatenate([blocks[w * FILT + i] for w in range(WINDOWS)], axis=0)
        out[pl.ds(i, SPAN, stride=FILT), :] = rows.T


def solve(matrix, target):
    n = FILT
    trace = matrix[0][0][0]
    for k in range(1, n):
        trace = trace + matrix[k][k][0]
    ridge = (0.05 * 2.0 / (2 * n)) * trace + 1e-05

    def cmul(a, b):
        return a[0] * b[0] - a[1] * b[1], a[0] * b[1] + a[1] * b[0]

    diag = [matrix[k][k][0] + ridge for k in range(n)]
    upper = {(k, l): matrix[k][l] for k in range(n) for l in range(k + 1, n)}
    rhs = list(target)
    inv = [None] * n
    for k in range(n):
        inv[k] = 1.0 / diag[k]
        for i in range(k + 1, n):
            re, im = upper[k, i]
            factor = (re * inv[k], -im * inv[k])
            diag[i] = diag[i] - (re * factor[0] - im * factor[1])
            for l in range(i + 1, n):
                t = cmul(factor, upper[k, l])
                upper[i, l] = (upper[i, l][0] - t[0], upper[i, l][1] - t[1])
            t = cmul(factor, rhs[k])
            rhs[i] = (rhs[i][0] - t[0], rhs[i][1] - t[1])
    found = [None] * n
    for k in reversed(range(n)):
        re, im = rhs[k]
        for l in range(k + 1, n):
            t = cmul(upper[k, l], found[l])
            re, im = re - t[0], im - t[1]
        found[k] = (re * inv[k], im * inv[k])
    return found


PAIRS = [(k, l) for k in range(FILT) for l in range(k, FILT)]
OFF = [(k, l) for k, l in PAIRS if k < l]
SUMS = len(PAIRS) + len(OFF) + 2 * FILT


def windows_kernel(weights, live, here, across, held):
    alive = live[...].astype(f32)
    for n in range(ITERS):
        rows = []
        for i in range(FILT):
            start = n * BINS * FILT + i
            rows.append(weights[pl.ds(start, BINS, stride=FILT), :] * alive[i : i + 1])
        for w, block in enumerate(swap_blocks(rows, lanes_of(BINS), WX)):
            held[w, n] = block
    xq = lax.axis_index("xq")
    for w in range(2):
        here[w] = held[2 * xq + w]
        across[w] = held[2 - 2 * xq + w]


def halves_kernel(here, across, plus, minus):
    own, xq = lax.axis_index("zh") * HALF, lax.axis_index("xq")
    for source, place in ((here, xq), (across, 1 - xq)):
        for w in range(2):
            for n in range(ITERS):
                plus[place, w, n] = source[w, n, pl.ds(pl.multiple_of(own, HALF), HALF), :]
                minus[place, w, n] = source[w, n, pl.ds(pl.multiple_of(HALF - own, HALF), HALF), :]


def prepare_kernel(plus, minus, spread, omega):
    z = 4 * lax.axis_index("zh") + lax.axis_index("zl")
    beta_plus = jnp.where((z >= 2) & (z <= 5), 0, 1)
    table = spread[...]
    over = (((0,), (0,)), ((), ()))
    for n in range(ITERS):
        for source, beta in ((plus, beta_plus), (minus, 1 - beta_plus)):
            for w in range(2):
                rows = jnp.concatenate([source[a, w, n] for a in range(2)], axis=0)
                top = rows.astype(bf16)
                rest = (rows - top.astype(f32)).astype(bf16)
                omega[n, beta * 2 + w] = lax.dot_general(
                    top, table, over, preferred_element_type=f32
                ) + lax.dot_general(rest, table, over, preferred_element_type=f32)


def predictions(jobs, omega, turned, sums, coefs, store):
    slots = TWO * len(jobs)
    def tile_of(row, w, flip):
        row = row % FILT
        return w * FILT + row + flip * (FILT - 1 - 2 * row)

    def rows_of(job, w, lines):
        own, side, _, flip = jobs[job]
        plain, quarter = [], []
        for row in range(2 * FILT):
            which, tile = row // FILT, tile_of(row, w, flip)
            plain.append((own, side)[which][tile, lines, :])
            quarter.append(pltpu.roll(plain[-1], BINS, 1))
        return plain, quarter

    def weight_of(job, i, w, sub):
        _, _, beta, flip = jobs[job]
        start = tile_of(i, 0, flip) * ROWS + sub * 8
        return omega[beta * TWO + w, pl.ds(pl.multiple_of(start, 8), 8), :]

    def gather(w, carry):
        for job in range(len(jobs)):
            acc = [None] * SUMS

            def add(place, value):
                acc[place] = value if acc[place] is None else acc[place] + value

            for sub in range(ROWS // 8):
                rows, turns = rows_of(job, w, pl.ds(sub * 8, 8))
                for i in range(FILT):
                    om = weight_of(job, i, w, sub)
                    weighted = [om * rows[i + k + 1] for k in range(FILT)]
                    place = 0
                    for k, l in PAIRS:
                        add(place, weighted[k] * rows[i + l + 1])
                        place += 1
                    for k, l in OFF:
                        add(place, weighted[k] * turns[i + l + 1])
                        place += 1
                    for k in range(FILT):
                        add(place, weighted[k] * rows[i])
                        add(place + 1, weighted[k] * turns[i])
                        place += 2
            start = (job * TWO + w) * 8
            for place in range(SUMS):
                sums[place, pl.ds(start, 8), :] = acc[place]
        return carry

    for w in range(TWO):
        gather(w, 0)

    sign = jnp.where(lanes_of(slots) < BINS, 1.0, -1.0).astype(f32)

    def total(place):
        value = sums[place, pl.ds(0, slots, stride=8), :]
        for s in range(1, 8):
            value = value + sums[place, pl.ds(s, slots, stride=8), :]
        return value

    def real_sum(place):
        value = total(place)
        return value + pltpu.roll(value, BINS, 1)

    def imag_sum(place):
        value = total(place)
        return (value - pltpu.roll(value, BINS, 1)) * sign

    matrix = [[None] * FILT for _ in range(FILT)]
    for place, (k, l) in enumerate(PAIRS):
        matrix[k][l] = (real_sum(place), None)
    for place, (k, l) in enumerate(OFF):
        matrix[k][l] = (matrix[k][l][0], imag_sum(len(PAIRS) + place))
    base = len(PAIRS) + len(OFF)
    target = [(real_sum(base + 2 * k), imag_sum(base + 2 * k + 1)) for k in range(FILT)]
    for k, (re, im) in enumerate(solve(matrix, target)):
        coefs[2 * k] = re
        coefs[2 * k + 1] = -im * sign

    def predict(w, carry):
        for sub in range(ROWS // 8):
            lines = pl.ds(sub * 8, 8)
            for job in range(len(jobs)):
                rows, turns = rows_of(job, w, lines)
                acc = [None] * FILT
                for k in range(FILT):
                    one = coefs[2 * k, pl.ds(job * TWO + w, 1), :]
                    two = coefs[2 * k + 1, pl.ds(job * TWO + w, 1), :]
                    for i in range(FILT):
                        value = one * rows[i + k + 1] + two * turns[i + k + 1]
                        acc[i] = value if acc[i] is None else acc[i] + value
                for i in range(FILT):
                    store(job, tile_of(i, w, jobs[job][3]), lines, acc[i], weight_of(job, i, w, sub))
        return carry

    for w in range(TWO):
        predict(w, 0)


def pick_kernel(block, out):
    out[...] = block[lax.axis_index("c")]


def beyond_kernel(n, beyond, edge, omegas, out, turned, sums, coefs):
    core = lax.axis_index("c")

    def store(job, tile, lines, value, weight):
        out[tile, lines, :] = value

    predictions([(edge, beyond, core, 1 - core)], omegas.at[n], turned, sums, coefs, store)


def filter_kernel(part, own, partner, omegas, out, turned, sums, coefs):
    core = lax.axis_index("c")
    rest, edge, near, far = own.at[0], own.at[1], partner.at[0], partner.at[1]

    def store(job, tile, lines, value, weight):
        half = jnp.where(weight > 0.0, 0.5, 0.0)
        if job == 0:
            out[core, tile, lines, :] = (value + part[tile, lines, :]) * half
        elif job == 1:
            out[1 - core, tile, lines, :] = value
        else:
            out[1 - core, tile, lines, :] = (out[1 - core, tile, lines, :] + value) * half

    jobs = [(edge, near, core, core), (rest, near, 1 - core, 1 - core), (rest, far, 1 - core, core)]
    predictions(jobs, omegas.at[ITERS - 1], turned, sums, coefs, store)


def near_kernel(part, own, partner, omegas, out, turned, sums, coefs):
    core = lax.axis_index("c")

    def store(job, tile, lines, value, weight):
        out[tile, lines, :] = (value + part[tile, lines, :]) * jnp.where(weight > 0.0, 0.5, 0.0)

    predictions([(own.at[core], partner.at[core], core, core)], omegas.at[0], turned, sums, coefs, store)


def rest_kernel(edge, own, partner, omegas, out, turned, sums, coefs):
    core = lax.axis_index("c")

    def store(job, tile, lines, value, weight):
        if job == 0:
            out[0, tile, lines, :] = value
        else:
            out[0, tile, lines, :] = (out[0, tile, lines, :] + value) * jnp.where(weight > 0.0, 0.5, 0.0)

    rest, near, far = own.at[1 - core], partner.at[core], partner.at[1 - core]
    jobs = [(rest, near, 1 - core, 1 - core), (rest, far, 1 - core, core)]
    predictions(jobs, omegas.at[0], turned, sums, coefs, store)
    for k in range(TWO * FILT):
        out[1, k] = edge[k]


def kernel_call(body, shapes, scratch=(), name=None, cost=None):
    out = [jax.ShapeDtypeStruct(shape, f32) for shape in shapes]
    return pl.pallas_call(
        body,
        out_shape=out if len(out) > 1 else out[0],
        scratch_shapes=list(scratch),
        compiler_params=pltpu.CompilerParams(vmem_limit_bytes=16 * 1024 * 1024),
        name=name,
        cost_estimate=cost,
    )


TRACES = (RADIX, WX, LANES)
TWO = 2
ROWS = WX
TILES = (2 * TWO * FILT, ROWS, LANES)
EDGE = (TWO * FILT, ROWS, LANES)
PART = (2, ITERS, BINS, LANES)
HALVES = (2, 2, ITERS, HALF, LANES)


def send_call(traces):
    return kernel_call(send_kernel, [TRACES], name="send")(traces.reshape(SPAN * FILT, LANES))


def forward_call(blocks, live, *tables):
    scratch = [pltpu.VMEM((LANES, LANES), f32)]
    return kernel_call(forward_kernel, [TILES], scratch, "forward")(blocks, live, *tables)


def inverse_call(blocks, *tables):
    return kernel_call(inverse_kernel, [TRACES], name="inverse")(blocks, *tables)


LONG = pl.CostEstimate(flops=16_000_000_000, bytes_accessed=64_000_000, transcendentals=0)


def windows_call(weights, live):
    scratch = [pltpu.VMEM((WINDOWS,) + PART[1:], f32)]
    return kernel_call(windows_kernel, [PART, PART], scratch, "windows")(weights, live)


def halves_call(*arrays):
    return kernel_call(halves_kernel, [HALVES, HALVES], (), "halves", LONG)(*arrays)


def prepare_call(*arrays):
    shape = (ITERS, 2 * TWO, FILT * ROWS, LANES)
    return kernel_call(prepare_kernel, [shape], (), "prepare")(*arrays)


def filter_scratch(blocks, jobs):
    return [
        pltpu.VMEM((blocks,) + EDGE, f32),
        pltpu.VMEM((SUMS, 8 * TWO * jobs, LANES), f32),
        pltpu.VMEM((2 * FILT, TWO * jobs, LANES), f32),
    ]


def pick_call(block):
    return kernel_call(pick_kernel, [EDGE], (), "pick", LONG)(block)


def beyond_call(n, edge, beyond, omegas):
    body = functools.partial(beyond_kernel, n)
    cost = pl.CostEstimate(flops=4_000_000_000, bytes_accessed=16_000_000, transcendentals=0)
    return kernel_call(body, [EDGE], filter_scratch(2, 1), "beyond", cost)(beyond, edge, omegas)


def near_call(*arrays):
    return kernel_call(near_kernel, [EDGE], filter_scratch(2, 1), "near")(*arrays)


def rest_call(*arrays):
    return kernel_call(rest_kernel, [(2,) + EDGE], filter_scratch(3, 2), "rest")(*arrays)


def filter_call(*arrays):
    return kernel_call(filter_kernel, [(2,) + EDGE], filter_scratch(4, 3), "filter")(*arrays)


def receive_call(blocks):
    return kernel_call(receive_kernel, [(SPAN * FILT, LANES)], name="receive")(blocks).reshape(
        SPAN, FILT, LANES
    )


def local(tables, traces_in, reweights, live_mask):
    (fh, fl), (ih, il), spread, turns = tables
    fh, fl, ih, il, spread, turns = (jnp.asarray(t) for t in (fh, fl, ih, il, spread, turns))

    def exchange(blocks, axes):
        return lax.all_to_all(blocks, axes, 0, 0, tiled=True)

    swap = [(0, 1), (1, 0)]
    ys = lax.axis_size("y")
    shift = [(2 * y + 1, 2 * y + 2) for y in range(ys - 1)] + [(2 * y + 2, 2 * y + 1) for y in range(ys - 1)]
    weights = reweights.reshape(ITERS * BINS * FILT, LANES)
    sent = send_call(traces_in)
    here, across = windows_call(weights, live_mask)
    across = lax.ppermute(across, ("xq", "xr"), [(i, WINDOWS - 1 - i) for i in range(WINDOWS)])
    plus, minus = halves_call(here, across)
    plus = lax.ppermute(plus, ("zh", "zl"), [(z, (z + 2) % 8) for z in range(8)])
    minus = lax.ppermute(minus, ("zh", "zl"), [(z, (z - 2) % 8) for z in range(8)])
    spectra = forward_call(exchange(sent, ("xq", "xr", "zl")), live_mask, fh, fl, turns)
    block = exchange(spectra, ("zh", "xr", "zl")).reshape((2,) + EDGE)
    edge = pick_call(block)
    omegas = None
    for n in range(ITERS):
        beyond = lax.ppermute(edge, ("y", "c"), shift)
        partner = lax.ppermute(block, "c", swap)
        if omegas is None:
            edge, plus, minus = lax.optimization_barrier((edge, plus, minus))
            omegas = prepare_call(plus, minus, spread)
        part = beyond_call(n, edge, beyond, omegas)
        if n + 1 < ITERS:
            edge = near_call(part, block, partner, omegas)
            block = rest_call(edge, block, partner, omegas)
        else:
            block = filter_call(part, block, partner, omegas)
    back = exchange(block.reshape(TILES), ("zh", "xr", "zl"))
    return receive_call(exchange(inverse_call(back, ih, il, turns), ("xq", "xr", "zl")))


def solution(mesh):
    tables = (*transform_tables(), spread_table(), turn_table())

    def run(traces_in, reweights, live_mask):
        return local(tables, traces_in, reweights, live_mask)

    inner = jax.sharding.Mesh(mesh.devices.reshape(-1, 2, 2, 2, 2, 4), ("y", "zh", "c", "xq", "xr", "zl"))
    inline, freq = ("y", "zh", "c"), ("xq", "xr", "zl")
    in_specs = (P(freq, inline, None), P(None, freq, inline, None), P(inline, None))
    out_specs = P(freq, inline, None)
    return jax.shard_map(run, mesh=inner, in_specs=in_specs, out_specs=out_specs, check_vma=False)
```

```python
import functools
import math

import jax
import jax.numpy as jnp
import numpy as np
from jax import lax
from jax.experimental import pallas as pl
from jax.experimental.pallas import tpu as pltpu
from jax.sharding import PartitionSpec as P

NT = 2048
FILT = 4
ITERS = 2
RADIX = 16
SPAN = 128
BINS = 64
WINDOWS = 4
WX = 32
LANES = 128
f32, bf16 = jnp.float32, jnp.bfloat16


def low_bin(m, s, b):
    residue = m if s == 0 else (8 if m == 0 else RADIX - m)
    return 16 * b + residue


INNER = [(a, s, b) for a in range(2) for s in range(2) for b in range(2)]
HALF = BINS // 2
SETS = ((0, 3), (1, 2))


def held_bins(zh, zl):
    z = 4 * zh + zl
    return (0, z - 2) if 2 <= z <= 5 else (1, (z + 2) % 8)


def split_table(table):
    high = table.astype(np.float32).astype(bf16)
    low = (table - high.astype(np.float64)).astype(np.float32).astype(bf16)
    return high, low


def transform_tables():
    forward = np.zeros((2, 2 * SPAN, 2 * SPAN))
    inverse = np.zeros((2, 2 * SPAN, 2 * SPAN))
    r = np.arange(SPAN)
    for spot in range(2 * 8):
        kappa, part = divmod(spot, 8)
        half, source = held_bins(*divmod(part, 4))
        for place, (a, s, b) in enumerate(INNER):
            base = BINS * (4 * SETS[kappa][a] + source) + HALF * half + 16 * b
            col = spot * 8 + place
            f = base + 8 * s
            angle = 2.0 * np.pi * ((f * r) % NT) / NT
            span = slice(s * SPAN, (s + 1) * SPAN)
            forward[0, span, col] = np.cos(angle)
            forward[0, span, SPAN + col] = -np.sin(angle)
            angle = 2.0 * np.pi * (((base // RADIX + s) * r) % SPAN) / SPAN
            sign = 1.0 if s == 0 else -1.0
            forward[1, :SPAN, col] = np.cos(angle)
            forward[1, SPAN:, col] = sign * np.sin(angle)
            forward[1, :SPAN, SPAN + col] = -np.sin(angle)
            forward[1, SPAN:, SPAN + col] = sign * np.cos(angle)
            scale = (1.0 if f == 0 else 2.0) / NT
            for which, factor in ((0, scale), (1, 1.0 / NT)):
                inverse[which, col] = forward[which, :, col] * factor
                inverse[which, SPAN + col] = forward[which, :, SPAN + col] * factor
    return split_table(forward), split_table(inverse)


def turn_table():
    angle = 2.0 * np.pi * np.arange(8)[:, None] * np.arange(SPAN)[None] / NT
    return np.stack([np.cos(angle), np.sin(angle)]).astype(np.float32)


def spread_table():
    table = np.zeros((BINS, LANES), np.float32)
    for m in range(8):
        for place, (a, s, b) in enumerate(INNER):
            row = HALF * a + low_bin(m, s, b)
            table[row, m * 8 + place] = 1.0
            table[row, BINS + m * 8 + place] = 1.0
    return table.astype(bf16)


def cadd(a, b):
    im = a[1] if b[1] is None else (b[1] if a[1] is None else a[1] + b[1])
    return a[0] + b[0], im


def csub(a, b):
    im = a[1] if b[1] is None else (-b[1] if a[1] is None else a[1] - b[1])
    return a[0] - b[0], im


def conj(a):
    return a[0], None if a[1] is None else -a[1]


def turn(a, step, size):
    step = step % size
    if step == 0:
        return a
    if 4 * step == size:
        return (jnp.zeros_like(a[0]) if a[1] is None else -a[1]), a[0]
    if 4 * step == 3 * size:
        return (jnp.zeros_like(a[0]) if a[1] is None else a[1]), -a[0]
    c, s = math.cos(2 * math.pi * step / size), math.sin(2 * math.pi * step / size)
    if a[1] is None:
        return a[0] * c, a[0] * s
    return a[0] * c - a[1] * s, a[0] * s + a[1] * c


def real_transform(values):
    n = len(values)
    if n == 1:
        return [(values[0], None)]
    if n == 2:
        return [(values[0] + values[1], None), (values[0] - values[1], None)]
    even, odd = real_transform(values[::2]), real_transform(values[1::2])
    out = [None] * (n // 2 + 1)
    for p in range(n // 4 + 1):
        turned = turn(odd[p], -p, n)
        out[p] = cadd(even[p], turned)
        out[n // 2 - p] = conj(csub(even[p], turned))
    out[0] = (out[0][0], None)
    out[n // 2] = (out[n // 2][0], None)
    return out


def real_inverse(bins):
    n = 2 * (len(bins) - 1)
    if n == 2:
        return [bins[0][0] + bins[1][0], bins[0][0] - bins[1][0]]
    quarter = n // 4
    first, second = [], []
    for p in range(quarter + 1):
        other = conj(bins[n // 2 - p])
        total, rest = cadd(bins[p], other), turn(csub(bins[p], other), p, n)
        if p in (0, quarter):
            total, rest = (total[0], None), (rest[0], None)
        first.append(total)
        second.append(rest)
    out = [None] * n
    out[::2], out[1::2] = real_inverse(first), real_inverse(second)
    return out


def split_dot(lhs, high, low):
    top = lhs.astype(bf16)
    rest = (lhs - top.astype(f32)).astype(bf16)
    table = jnp.concatenate([high, high, low], axis=0)
    return jnp.dot(jnp.concatenate([top, rest, top], axis=1), table, preferred_element_type=f32)


def swap_blocks(arrays, lane, width):
    arrays = list(arrays)
    n = len(arrays)
    d = 1
    while d < n:
        upper = (lane & (width * d)) != 0
        for i in range(n):
            if i & d:
                continue
            a, b = arrays[i], arrays[i + d]
            arrays[i] = jnp.where(upper, pltpu.roll(b, width * d, 1), a)
            arrays[i + d] = jnp.where(upper, b, pltpu.roll(a, LANES - width * d, 1))
        d *= 2
    return arrays


def lanes_of(rows):
    return lax.broadcasted_iota(jnp.int32, (rows, LANES), 1)


def place_x():
    return 2 * lax.axis_index("xq") + lax.axis_index("xr")


def send_kernel(traces, out):
    for i in range(FILT):
        turned = traces[pl.ds(i, SPAN, stride=FILT), :].T
        for w in range(WINDOWS):
            out[w * FILT + i] = turned[w * WX : (w + 1) * WX]


def forward_kernel(blocks, live, high, low, turns, out, alive):
    xq = lax.axis_index("xq")
    row = live[pl.ds(lax.axis_index("zl"), 1), :].astype(f32)
    alive[...] = jnp.broadcast_to(row, (LANES, LANES)).T
    mask = alive[pl.ds(pl.multiple_of(place_x() * WX, WX), WX), :]
    lane = lanes_of(WX)
    bins = real_transform([blocks[j] * mask for j in range(RADIX)])
    first = split_dot(jnp.concatenate([bins[0][0], bins[8][0]], axis=1), high[0], low[0])
    rows = []
    for m in range(1, 8):
        (re, im), c, s = bins[m], turns[0, m : m + 1, :], turns[1, m : m + 1, :]
        rows.append(jnp.concatenate([re * c + im * s, im * c - re * s], axis=1))
    others = split_dot(jnp.concatenate(rows, axis=0), high[1], low[1])
    real = [first[:, :LANES]] + [others[WX * m : WX * m + WX, :LANES] for m in range(7)]
    imag = [first[:, LANES:]] + [others[WX * m : WX * m + WX, LANES:] for m in range(7)]
    real, imag = swap_blocks(real, lane, 8), swap_blocks(imag, lane, 8)
    left = lane < BINS
    for part in range(8):
        place = part // 4 * 8 + part % 4
        out[place + 4 * xq] = jnp.where(left, real[part], pltpu.roll(imag[part], BINS, 1))
        out[place + 4 - 4 * xq] = jnp.where(left, pltpu.roll(real[part], BINS, 1), imag[part])


def inverse_kernel(blocks, high, low, turns, out):
    xq = lax.axis_index("xq")
    lane = lanes_of(WX)
    left = lane < BINS
    real, imag = [], []
    for part in range(8):
        place = part // 4 * 8 + part % 4
        first, second = blocks[place + 4 * xq], blocks[place + 4 - 4 * xq]
        real.append(jnp.where(left, first, pltpu.roll(second, BINS, 1)))
        imag.append(jnp.where(left, pltpu.roll(first, BINS, 1), second))
    real, imag = swap_blocks(real, lane, 8), swap_blocks(imag, lane, 8)
    first = split_dot(jnp.concatenate([real[0], imag[0]], axis=1), high[0], low[0])
    rows = [jnp.concatenate([real[m], imag[m]], axis=1) for m in range(1, 8)]
    others = split_dot(jnp.concatenate(rows, axis=0), high[1], low[1])
    bins = [(first[:, :LANES], None)] + [None] * 7 + [(first[:, LANES:], None)]
    for m in range(1, 8):
        value = others[WX * (m - 1) : WX * m]
        re, im, c, s = value[:, :LANES], value[:, LANES:], turns[0, m : m + 1, :], turns[1, m : m + 1, :]
        bins[m] = (re * c - im * s, re * s + im * c)
    for j, values in enumerate(real_inverse(bins)):
        out[j] = values


def receive_kernel(blocks, out):
    for i in range(FILT):
        rows = jnp.concatenate([blocks[w * FILT + i] for w in range(WINDOWS)], axis=0)
        out[pl.ds(i, SPAN, stride=FILT), :] = rows.T


def solve(matrix, target):
    n = FILT
    trace = matrix[0][0][0]
    for k in range(1, n):
        trace = trace + matrix[k][k][0]
    ridge = (0.05 * 2.0 / (2 * n)) * trace + 1e-05

    def cmul(a, b):
        return a[0] * b[0] - a[1] * b[1], a[0] * b[1] + a[1] * b[0]

    diag = [matrix[k][k][0] + ridge for k in range(n)]
    upper = {(k, l): matrix[k][l] for k in range(n) for l in range(k + 1, n)}
    rhs = list(target)
    inv = [None] * n
    for k in range(n):
        inv[k] = 1.0 / diag[k]
        for i in range(k + 1, n):
            re, im = upper[k, i]
            factor = (re * inv[k], -im * inv[k])
            diag[i] = diag[i] - (re * factor[0] - im * factor[1])
            for l in range(i + 1, n):
                t = cmul(factor, upper[k, l])
                upper[i, l] = (upper[i, l][0] - t[0], upper[i, l][1] - t[1])
            t = cmul(factor, rhs[k])
            rhs[i] = (rhs[i][0] - t[0], rhs[i][1] - t[1])
    found = [None] * n
    for k in reversed(range(n)):
        re, im = rhs[k]
        for l in range(k + 1, n):
            t = cmul(upper[k, l], found[l])
            re, im = re - t[0], im - t[1]
        found[k] = (re * inv[k], im * inv[k])
    return found


PAIRS = [(k, l) for k in range(FILT) for l in range(k, FILT)]
OFF = [(k, l) for k, l in PAIRS if k < l]
SUMS = len(PAIRS) + len(OFF) + 2 * FILT


def windows_kernel(weights, live, here, across, held):
    alive = live[...].astype(f32)
    for n in range(ITERS):
        rows = []
        for i in range(FILT):
            start = n * BINS * FILT + i
            rows.append(weights[pl.ds(start, BINS, stride=FILT), :] * alive[i : i + 1])
        for w, block in enumerate(swap_blocks(rows, lanes_of(BINS), WX)):
            held[w, n] = block
    xq = lax.axis_index("xq")
    for w in range(2):
        here[w] = held[2 * xq + w]
        across[w] = held[2 - 2 * xq + w]


def halves_kernel(here, across, plus, minus):
    own, xq = lax.axis_index("zh") * HALF, lax.axis_index("xq")
    for source, place in ((here, xq), (across, 1 - xq)):
        for w in range(2):
            for n in range(ITERS):
                plus[place, w, n] = source[w, n, pl.ds(pl.multiple_of(own, HALF), HALF), :]
                minus[place, w, n] = source[w, n, pl.ds(pl.multiple_of(HALF - own, HALF), HALF), :]


def prepare_kernel(plus, minus, spread, omega):
    z = 4 * lax.axis_index("zh") + lax.axis_index("zl")
    beta_plus = jnp.where((z >= 2) & (z <= 5), 0, 1)
    table = spread[...]
    over = (((0,), (0,)), ((), ()))
    for n in range(ITERS):
        for source, beta in ((plus, beta_plus), (minus, 1 - beta_plus)):
            for w in range(2):
                rows = jnp.concatenate([source[a, w, n] for a in range(2)], axis=0)
                top = rows.astype(bf16)
                rest = (rows - top.astype(f32)).astype(bf16)
                omega[n, beta * 2 + w] = lax.dot_general(
                    top, table, over, preferred_element_type=f32
                ) + lax.dot_general(rest, table, over, preferred_element_type=f32)


def predictions(jobs, omega, turned, sums, coefs, store):
    slots = TWO * len(jobs)
    def tile_of(row, w, flip):
        row = row % FILT
        return w * FILT + row + flip * (FILT - 1 - 2 * row)

    def rows_of(job, w, lines):
        own, side, _, flip = jobs[job]
        plain, quarter = [], []
        for row in range(2 * FILT):
            which, tile = row // FILT, tile_of(row, w, flip)
            plain.append((own, side)[which][tile, lines, :])
            quarter.append(pltpu.roll(plain[-1], BINS, 1))
        return plain, quarter

    def weight_of(job, i, w, sub):
        _, _, beta, flip = jobs[job]
        start = tile_of(i, 0, flip) * ROWS + sub * 8
        return omega[beta * TWO + w, pl.ds(pl.multiple_of(start, 8), 8), :]

    def gather(w, carry):
        for job in range(len(jobs)):
            acc = [None] * SUMS

            def add(place, value):
                acc[place] = value if acc[place] is None else acc[place] + value

            for sub in range(ROWS // 8):
                rows, turns = rows_of(job, w, pl.ds(sub * 8, 8))
                for i in range(FILT):
                    om = weight_of(job, i, w, sub)
                    weighted = [om * rows[i + k + 1] for k in range(FILT)]
                    place = 0
                    for k, l in PAIRS:
                        add(place, weighted[k] * rows[i + l + 1])
                        place += 1
                    for k, l in OFF:
                        add(place, weighted[k] * turns[i + l + 1])
                        place += 1
                    for k in range(FILT):
                        add(place, weighted[k] * rows[i])
                        add(place + 1, weighted[k] * turns[i])
                        place += 2
            start = (job * TWO + w) * 8
            for place in range(SUMS):
                sums[place, pl.ds(start, 8), :] = acc[place]
        return carry

    for w in range(TWO):
        gather(w, 0)

    sign = jnp.where(lanes_of(slots) < BINS, 1.0, -1.0).astype(f32)

    def total(place):
        value = sums[place, pl.ds(0, slots, stride=8), :]
        for s in range(1, 8):
            value = value + sums[place, pl.ds(s, slots, stride=8), :]
        return value

    def real_sum(place):
        value = total(place)
        return value + pltpu.roll(value, BINS, 1)

    def imag_sum(place):
        value = total(place)
        return (value - pltpu.roll(value, BINS, 1)) * sign

    matrix = [[None] * FILT for _ in range(FILT)]
    for place, (k, l) in enumerate(PAIRS):
        matrix[k][l] = (real_sum(place), None)
    for place, (k, l) in enumerate(OFF):
        matrix[k][l] = (matrix[k][l][0], imag_sum(len(PAIRS) + place))
    base = len(PAIRS) + len(OFF)
    target = [(real_sum(base + 2 * k), imag_sum(base + 2 * k + 1)) for k in range(FILT)]
    for k, (re, im) in enumerate(solve(matrix, target)):
        coefs[2 * k] = re
        coefs[2 * k + 1] = -im * sign

    def predict(w, carry):
        for sub in range(ROWS // 8):
            lines = pl.ds(sub * 8, 8)
            for job in range(len(jobs)):
                rows, turns = rows_of(job, w, lines)
                acc = [None] * FILT
                for k in range(FILT):
                    one = coefs[2 * k, pl.ds(job * TWO + w, 1), :]
                    two = coefs[2 * k + 1, pl.ds(job * TWO + w, 1), :]
                    for i in range(FILT):
                        value = one * rows[i + k + 1] + two * turns[i + k + 1]
                        acc[i] = value if acc[i] is None else acc[i] + value
                for i in range(FILT):
                    store(job, tile_of(i, w, jobs[job][3]), lines, acc[i], weight_of(job, i, w, sub))
        return carry

    for w in range(TWO):
        predict(w, 0)


def pick_kernel(block, out):
    out[...] = block[lax.axis_index("c")]


def beyond_kernel(n, beyond, edge, omegas, out, turned, sums, coefs):
    core = lax.axis_index("c")

    def store(job, tile, lines, value, weight):
        out[tile, lines, :] = value

    predictions([(edge, beyond, core, 1 - core)], omegas.at[n], turned, sums, coefs, store)


def filter_kernel(n, part, own, partner, omegas, *refs):
    *outs, turned, sums, coefs = refs
    core = lax.axis_index("c")
    rest_at, edge_at = (1 - core, core) if n == 0 else (0, 1)
    rest, edge = own.at[rest_at], own.at[edge_at]
    near, far = (partner.at[core], partner.at[1 - core]) if n == 0 else (partner.at[0], partner.at[1])
    new_rest, new_edge = (outs[0].at[0], outs[0].at[1]) if n + 1 < ITERS else (outs[0].at[1 - core], outs[0].at[core])

    def store(job, tile, lines, value, weight):
        half = jnp.where(weight > 0.0, 0.5, 0.0)
        if job == 0:
            value = (value + part[tile, lines, :]) * half
            new_edge[tile, lines, :] = value
            if n + 1 < ITERS:
                outs[1][tile, lines, :] = value
        elif job == 1:
            new_rest[tile, lines, :] = value
        else:
            new_rest[tile, lines, :] = (new_rest[tile, lines, :] + value) * half

    jobs = [(edge, near, core, core), (rest, near, 1 - core, 1 - core), (rest, far, 1 - core, core)]
    predictions(jobs, omegas.at[n], turned, sums, coefs, store)


def kernel_call(body, shapes, scratch=(), name=None, cost=None):
    out = [jax.ShapeDtypeStruct(shape, f32) for shape in shapes]
    return pl.pallas_call(
        body,
        out_shape=out if len(out) > 1 else out[0],
        scratch_shapes=list(scratch),
        compiler_params=pltpu.CompilerParams(vmem_limit_bytes=16 * 1024 * 1024),
        name=name,
        cost_estimate=cost,
    )


TRACES = (RADIX, WX, LANES)
TWO = 2
ROWS = WX
TILES = (2 * TWO * FILT, ROWS, LANES)
EDGE = (TWO * FILT, ROWS, LANES)
PART = (2, ITERS, BINS, LANES)
HALVES = (2, 2, ITERS, HALF, LANES)


def send_call(traces):
    return kernel_call(send_kernel, [TRACES], name="send")(traces.reshape(SPAN * FILT, LANES))


def forward_call(blocks, live, *tables):
    scratch = [pltpu.VMEM((LANES, LANES), f32)]
    return kernel_call(forward_kernel, [TILES], scratch, "forward")(blocks, live, *tables)


def inverse_call(blocks, *tables):
    return kernel_call(inverse_kernel, [TRACES], name="inverse")(blocks, *tables)


LONG = pl.CostEstimate(flops=16_000_000_000, bytes_accessed=64_000_000, transcendentals=0)


def windows_call(weights, live):
    scratch = [pltpu.VMEM((WINDOWS,) + PART[1:], f32)]
    return kernel_call(windows_kernel, [PART, PART], scratch, "windows")(weights, live)


def halves_call(*arrays):
    return kernel_call(halves_kernel, [HALVES, HALVES], (), "halves", LONG)(*arrays)


def prepare_call(*arrays):
    shape = (ITERS, 2 * TWO, FILT * ROWS, LANES)
    return kernel_call(prepare_kernel, [shape], (), "prepare")(*arrays)


def filter_scratch(blocks, jobs):
    return [
        pltpu.VMEM((blocks,) + EDGE, f32),
        pltpu.VMEM((SUMS, 8 * TWO * jobs, LANES), f32),
        pltpu.VMEM((2 * FILT, TWO * jobs, LANES), f32),
    ]


def pick_call(block):
    return kernel_call(pick_kernel, [EDGE], (), "pick", LONG)(block)


def beyond_call(n, edge, beyond, omegas):
    body = functools.partial(beyond_kernel, n)
    cost = pl.CostEstimate(flops=4_000_000_000, bytes_accessed=16_000_000, transcendentals=0)
    return kernel_call(body, [EDGE], filter_scratch(2, 1), "beyond", cost)(beyond, edge, omegas)


def filter_call(n, part, own, partner, omegas):
    both = (2,) + EDGE
    shapes = [both, EDGE] if n + 1 < ITERS else [both]
    body = functools.partial(filter_kernel, n)
    return kernel_call(body, shapes, filter_scratch(4, 3), name="filter")(part, own, partner, omegas)


def receive_call(blocks):
    return kernel_call(receive_kernel, [(SPAN * FILT, LANES)], name="receive")(blocks).reshape(
        SPAN, FILT, LANES
    )


def local(tables, traces_in, reweights, live_mask):
    (fh, fl), (ih, il), spread, turns = tables
    fh, fl, ih, il, spread, turns = (jnp.asarray(t) for t in (fh, fl, ih, il, spread, turns))

    def exchange(blocks, axes):
        return lax.all_to_all(blocks, axes, 0, 0, tiled=True)

    swap = [(0, 1), (1, 0)]
    ys = lax.axis_size("y")
    shift = [(2 * y + 1, 2 * y + 2) for y in range(ys - 1)] + [(2 * y + 2, 2 * y + 1) for y in range(ys - 1)]
    weights = reweights.reshape(ITERS * BINS * FILT, LANES)
    sent = send_call(traces_in)
    here, across = windows_call(weights, live_mask)
    across = lax.ppermute(across, ("xq", "xr"), [(i, WINDOWS - 1 - i) for i in range(WINDOWS)])
    plus, minus = halves_call(here, across)
    plus = lax.ppermute(plus, ("zh", "zl"), [(z, (z + 2) % 8) for z in range(8)])
    minus = lax.ppermute(minus, ("zh", "zl"), [(z, (z - 2) % 8) for z in range(8)])
    spectra = forward_call(exchange(sent, ("xq", "xr", "zl")), live_mask, fh, fl, turns)
    block = exchange(spectra, ("zh", "xr", "zl")).reshape((2,) + EDGE)
    edge = pick_call(block)
    omegas = None
    for n in range(ITERS):
        beyond = lax.ppermute(edge, ("y", "c"), shift)
        partner = lax.ppermute(block, "c", swap)
        if omegas is None:
            edge, plus, minus = lax.optimization_barrier((edge, plus, minus))
            omegas = prepare_call(plus, minus, spread)
        part = beyond_call(n, edge, beyond, omegas)
        found = filter_call(n, part, block, partner, omegas)
        block, edge = found if n + 1 < ITERS else (found, None)
    back = exchange(block.reshape(TILES), ("zh", "xr", "zl"))
    return receive_call(exchange(inverse_call(back, ih, il, turns), ("xq", "xr", "zl")))


def solution(mesh):
    tables = (*transform_tables(), spread_table(), turn_table())

    def run(traces_in, reweights, live_mask):
        return local(tables, traces_in, reweights, live_mask)

    inner = jax.sharding.Mesh(mesh.devices.reshape(-1, 2, 2, 2, 2, 4), ("y", "zh", "c", "xq", "xr", "zl"))
    inline, freq = ("y", "zh", "c"), ("xq", "xr", "zl")
    in_specs = (P(freq, inline, None), P(None, freq, inline, None), P(inline, None))
    out_specs = P(freq, inline, None)
    return jax.shard_map(run, mesh=inner, in_specs=in_specs, out_specs=out_specs, check_vma=False)
```
